32 devices in a mesh: dp: 8 (over z, x), tensor: 4 (over y, core).
Axes of the slice: x: 2, y: 2, z: 4, core: 2. Of those that a mesh axis runs over, the one named last changes fastest.
Arguments:
- tokens: bfloat16 [24576, 1024], P(('dp', 'tensor')), may hold values from -6 to 6
- segments: int32 [24, 1024], P('dp'), may hold values from 0 to 3, never falling along the last dimension, each value on 1 to 800 neighbouring positions
- cotangent: bfloat16 [24576, 1024], P(('dp', 'tensor')), may hold values from -6 to 6
- mixer_in: float32 [3, 1024, 1024], P(None, 'dp', 'tensor'), may hold values from -0.1875 to 0.1875
- mixer_out: float32 [1024, 1024], P('tensor', 'dp'), may hold values from -0.1875 to 0.1875
- gate_up: float32 [2, 1024, 4608], P(None, 'dp', 'tensor'), may hold values from -0.1875 to 0.1875
- down_proj: float32 [4608, 1024], P('tensor', 'dp'), may hold values from -0.09375 to 0.09375
- norm_gains: float32 [2, 1024], P(None, ('dp', 'tensor')), may hold values from 0.5 to 1.5
- conv_kernel: float32 [3, 1024], P(None, ('dp', 'tensor')), may hold values from -3 to 3
- first_mixer_in: float32 [3, 1024, 1024], P(None, 'dp', 'tensor'), may hold values from -128 to 128
- second_mixer_in: float32 [3, 1024, 1024], P(None, 'dp', 'tensor'), may hold values from 2457.6 to 9830.4
- first_mixer_out: float32 [1024, 1024], P('tensor', 'dp'), may hold values from -128 to 128
- second_mixer_out: float32 [1024, 1024], P('tensor', 'dp'), may hold values from 2457.6 to 9830.4
- first_gate_up: float32 [2, 1024, 4608], P(None, 'dp', 'tensor'), may hold values from -32 to 32
- second_gate_up: float32 [2, 1024, 4608], P(None, 'dp', 'tensor'), may hold values from 117.9648 to 466.944
- first_down_proj: float32 [4608, 1024], P('tensor', 'dp'), may hold values from -64 to 64
- second_down_proj: float32 [4608, 1024], P('tensor', 'dp'), may hold values from 466.944 to 1867.776
- first_norm_gains: float32 [2, 1024], P(None, ('dp', 'tensor')), may hold values from -128 to 128
- second_norm_gains: float32 [2, 1024], P(None, ('dp', 'tensor')), may hold values from 2457.6 to 9830.4
- first_conv_kernel: float32 [3, 1024], P(None, ('dp', 'tensor')), may hold values from -128 to 128
- second_conv_kernel: float32 [3, 1024], P(None, ('dp', 'tensor')), may hold values from 2457.6 to 9830.4
Outputs:
- block_out: bfloat16 [24576, 1024], P(('dp', 'tensor'))
- grad_input: float32 [24576, 1024], P(('dp', 'tensor'))
- new_mixer_in: float32 [3, 1024, 1024], P(None, 'dp', 'tensor')
- new_first_mixer_in: float32 [3, 1024, 1024], P(None, 'dp', 'tensor')
- new_second_mixer_in: float32 [3, 1024, 1024], P(None, 'dp', 'tensor')
- new_mixer_out: float32 [1024, 1024], P('tensor', 'dp')
- new_first_mixer_out: float32 [1024, 1024], P('tensor', 'dp')
- new_second_mixer_out: float32 [1024, 1024], P('tensor', 'dp')
- new_gate_up: float32 [2, 1024, 4608], P(None, 'dp', 'tensor')
- new_first_gate_up: float32 [2, 1024, 4608], P(None, 'dp', 'tensor')
- new_second_gate_up: float32 [2, 1024, 4608], P(None, 'dp', 'tensor')
- new_down_proj: float32 [4608, 1024], P('tensor', 'dp')
- new_first_down_proj: float32 [4608, 1024], P('tensor', 'dp')
- new_second_down_proj: float32 [4608, 1024], P('tensor', 'dp')
- new_norm_gains: float32 [2, 1024], P(None, ('dp', 'tensor'))
- new_first_norm_gains: float32 [2, 1024], P(None, ('dp', 'tensor'))
- new_second_norm_gains: float32 [2, 1024], P(None, ('dp', 'tensor'))
- new_conv_kernel: float32 [3, 1024], P(None, ('dp', 'tensor'))
- new_first_conv_kernel: float32 [3, 1024], P(None, ('dp', 'tensor'))
- new_second_conv_kernel: float32 [3, 1024], P(None, ('dp', 'tensor'))
The draws below stay inside these ranges and needn't reach their ends.
Inputs may be any that keep to these rules, and one draw needn't show every extreme that they name: `segments`: within a row the document numbers never fall; a document holds 1 to 800 tokens.
All inputs are finite; a program needn't handle non-finite values.
Results may differ from the reference program's by a relative error of at most 0.019.
Values may be sent and summed in bfloat16 or wider, within the bound.
No kernel may reach another device: no remote copies, remote signals or barrier semaphores. Data moves between devices by JAX's collectives and lax.ppermute only.
A program may use at most 192 MiB of HBM per device.

```python
import math
import jax
import jax.numpy as jnp
import numpy as np
from jax import lax

D = 1024
FF = 4608
KW = 3
LEN = 1024
STEP = 10
SEQS = 3
SEQ_ALL = 24
TOKENS = 24576
N_DP = 8


def block_scale(own_key, dims, cuts, least, high):
    gain = 1.0
    for position, parts in cuts:
        heights = jax.random.uniform(jax.random.fold_in(jax.random.fold_in(own_key, 6), position), (parts,), jnp.float32, least / len(cuts), high / len(cuts))
        gain = gain * jnp.repeat(jnp.exp(heights), dims[position] // parts).reshape((-1,) + (1,) * (len(dims) - 1 - position))
    return gain


def split_up(amount, total, most, lean):
    loads = [(1 << 20) // math.isqrt(rank ** lean) + 1 for rank in range(2, amount + 1)]
    spare, holding = total - most - (amount - 1), [1] * (amount - 1)
    while spare > 0:
        free = [i for i in range(amount - 1) if holding[i] < most]
        pool, left = sum([loads[i] for i in free]), spare
        for i in free:
            extra = min(most - holding[i], max(1, left * loads[i] // pool), spare)
            holding[i] = holding[i] + extra
            spare = spare - extra
    return np.array([most] + holding)


def uneven(key, number_of, total, bound, skew):
    if number_of == 2:
        one = jax.random.randint(key, (), max(1, total - bound), min(bound, total - 1) + 1)
        return jnp.stack([one, total - one])
    sizes = jnp.asarray(split_up(number_of, total, bound, skew), jnp.int32)
    pairs = (number_of - 1) // 2
    source_of, sink = sizes[1:1 + 2 * pairs:2], sizes[2:2 + 2 * pairs:2]
    margin = jnp.minimum(source_of - 1, bound - sink)
    shifted = jax.random.randint(jax.random.fold_in(key, 1), (pairs,), 0, 1 << 20) % (margin + 1)
    sizes = sizes.at[1:1 + 2 * pairs:2].set(source_of - shifted).at[2:2 + 2 * pairs:2].set(sink + shifted)
    return sizes[jax.random.permutation(jax.random.fold_in(key, 2), number_of)]


def noise(rng, shape, deviation, reach, cuts=(), held_as=jnp.bfloat16):
    gain = block_scale(rng, shape, cuts, -0.22, 0.18) if cuts else 1.0
    values = jax.random.normal(rng, shape, jnp.float32) * deviation * gain
    return jnp.minimum(jnp.maximum(values, -reach), reach).astype(held_as)


def setup_inputs(seed: int = 0) -> dict:
    seeds = jax.random.split(jax.random.key(seed), 22)
    tokens = noise(seeds[0], (TOKENS, D), 1.0, 6.0, ((0, 32),))
    segments = jax.vmap(lambda own: jnp.searchsorted(jnp.cumsum(uneven(own, max(2, LEN // 256), LEN, LEN * 25 // 32, 1)), jnp.arange(LEN), side="right"))(jax.random.split(seeds[1], SEQ_ALL)).reshape((SEQ_ALL, LEN)).astype(jnp.int32)
    cotangent = noise(seeds[2], (TOKENS, D), 1.0, 6.0, ((0, 32),))
    mixer_in = noise(seeds[3], (3, D, D), D ** -0.5, 0.1875, ((1, 8), (2, 4)), jnp.float32)
    mixer_out = noise(seeds[4], (D, D), D ** -0.5, 0.1875, ((0, 4), (1, 8)), jnp.float32)
    gate_up = noise(seeds[5], (2, D, FF), D ** -0.5, 0.1875, ((1, 8), (2, 4)), jnp.float32)
    down_proj = noise(seeds[6], (FF, D), FF ** -0.5, 0.09375, ((0, 4), (1, 8)), jnp.float32)
    norm_gains = jnp.clip(1.0 + 0.1 * jax.random.normal(seeds[7], (2, D), jnp.float32), 0.5, 1.5)
    conv_kernel = noise(seeds[8], (KW, D), 0.6, 3.0, ((1, 32),), jnp.float32)
    first_mixer_in = noise(seeds[9], (3, D, D), (0.15 * TOKENS ** 0.5), 128.0, ((1, 8), (2, 4)), jnp.float32)
    second_mixer_in = jnp.clip(jnp.exp(math.log(9830.4) - 1.3862944 * jax.random.uniform(seeds[10], (3, D, D), jnp.float32) ** block_scale(seeds[10], (3, D, D), ((1, 8), (2, 4)), -0.2, 0.2)), 2457.6, 9830.4)
    first_mixer_out = noise(seeds[11], (D, D), (0.15 * TOKENS ** 0.5), 128.0, ((0, 4), (1, 8)), jnp.float32)
    second_mixer_out = jnp.clip(jnp.exp(math.log(9830.4) - 1.3862944 * jax.random.uniform(seeds[12], (D, D), jnp.float32) ** block_scale(seeds[12], (D, D), ((0, 4), (1, 8)), -0.2, 0.2)), 2457.6, 9830.4)
    first_gate_up = noise(seeds[13], (2, D, FF), (0.033 * TOKENS ** 0.5), 32.0, ((1, 8), (2, 4)), jnp.float32)
    second_gate_up = jnp.clip(jnp.exp(math.log(466.944) - 1.375823 * jax.random.uniform(seeds[14], (2, D, FF), jnp.float32) ** block_scale(seeds[14], (2, D, FF), ((1, 8), (2, 4)), -0.2, 0.2)), 117.9648, 466.944)
    first_down_proj = noise(seeds[15], (FF, D), (0.066 * TOKENS ** 0.5), 64.0, ((0, 4), (1, 8)), jnp.float32)
    second_down_proj = jnp.clip(jnp.exp(math.log(1867.776) - 1.3862944 * jax.random.uniform(seeds[16], (FF, D), jnp.float32) ** block_scale(seeds[16], (FF, D), ((0, 4), (1, 8)), -0.2, 0.2)), 466.944, 1867.776)
    first_norm_gains = noise(seeds[17], (2, D), (0.15 * TOKENS ** 0.5), 128.0, ((1, 32),), jnp.float32)
    second_norm_gains = jnp.clip(jnp.exp(math.log(9830.4) - 1.3862944 * jax.random.uniform(seeds[18], (2, D), jnp.float32) ** block_scale(seeds[18], (2, D), ((1, 32),), -0.2, 0.2)), 2457.6, 9830.4)
    first_conv_kernel = noise(seeds[19], (KW, D), (0.15 * TOKENS ** 0.5), 128.0, ((1, 32),), jnp.float32)
    second_conv_kernel = jnp.clip(jnp.exp(math.log(9830.4) - 1.3862944 * jax.random.uniform(seeds[20], (KW, D), jnp.float32) ** block_scale(seeds[20], (KW, D), ((1, 32),), -0.2, 0.2)), 2457.6, 9830.4)
    return dict(tokens=tokens, segments=segments, cotangent=cotangent, mixer_in=mixer_in, mixer_out=mixer_out, gate_up=gate_up, down_proj=down_proj, norm_gains=norm_gains, conv_kernel=conv_kernel, first_mixer_in=first_mixer_in, second_mixer_in=second_mixer_in, first_mixer_out=first_mixer_out, second_mixer_out=second_mixer_out, first_gate_up=first_gate_up, second_gate_up=second_gate_up, first_down_proj=first_down_proj, second_down_proj=second_down_proj, first_norm_gains=first_norm_gains, second_norm_gains=second_norm_gains, first_conv_kernel=first_conv_kernel, second_conv_kernel=second_conv_kernel)


EPS_NORM = 1e-05
EPS_ADAM = 1e-08
BETA_FIRST = 0.9
BETA_SECOND = 0.95
RATE_MATRIX = 0.05
RATE_SMALL = 0.5
DECAY = 0.1

@jax.custom_vjp
def low(v):
    return lax.optimization_barrier(v.astype(jnp.bfloat16)).astype(jnp.float32)

@jax.custom_vjp
def low_back(v):
    return v

def low_keep(v):
    return (low(v), None)

def low_pass(kept, grad):
    return (grad,)

def back_keep(v):
    return (v, None)

def back_low(kept, grad):
    return (low(grad),)
low.defvjp(low_keep, low_pass)
low_back.defvjp(back_keep, back_low)

def highest(spec, left, right):
    return jnp.einsum(spec, left, right, precision=lax.Precision.HIGHEST)

def lagged(values, shift):
    return jnp.concatenate([jnp.zeros((shift,) + values.shape[1:], values.dtype), values[:-shift]], 0)

def lag_masks(seg_flat, length):
    positions = jnp.arange(seg_flat.shape[0], dtype=jnp.int32) % length
    masks = [jnp.ones((seg_flat.shape[0], 1), jnp.float32)]
    for shift in range(1, KW):
        same = (positions >= shift) & (seg_flat == lagged(seg_flat, shift))
        masks.append(jnp.where(same, 1.0, 0.0).astype(jnp.float32)[:, None])
    return masks

def rms_scale(values):
    return lax.rsqrt(lax.optimization_barrier(jnp.mean(values * values, axis=-1, keepdims=True)) + EPS_NORM)

def forward(values, masks, gains, kernel, mixer_in, mixer_out, gate_up, down_proj):
    normed_one = low(values * rms_scale(values) * gains[0])
    projected = low_back(highest('td,kdc->tkc', normed_one, low(mixer_in)))
    part_b = projected[:, 0]
    part_c = projected[:, 1]
    part_x = projected[:, 2]
    product = part_b * part_x
    convolved = kernel[0] * product
    for shift in range(1, KW):
        convolved = convolved + kernel[shift] * masks[shift] * lagged(product, shift)
    gated = low(part_c * convolved)
    mixed = low_back(highest('tc,cd->td', gated, low(mixer_out)))
    middle = values + mixed
    normed_two = low(middle * rms_scale(middle) * gains[1])
    hidden = low_back(highest('td,kdf->tkf', normed_two, low(gate_up)))
    activated = low(jax.nn.silu(hidden[:, 0]) * hidden[:, 1])
    branch = low_back(highest('tf,fd->td', activated, low(down_proj)))
    return middle + branch

def adamw(param, grad, first, second, rate, decay):
    first_new = BETA_FIRST * first + (1.0 - BETA_FIRST) * grad
    second_new = BETA_SECOND * second + (1.0 - BETA_SECOND) * grad * grad
    first_hat = first_new / (1.0 - BETA_FIRST ** STEP)
    second_hat = second_new / (1.0 - BETA_SECOND ** STEP)
    return (param - rate * (first_hat / (jnp.sqrt(second_hat) + EPS_ADAM) + decay * param), first_new, second_new)

def reference(tokens, segments, cotangent, mixer_in, mixer_out, gate_up, down_proj, norm_gains, conv_kernel, first_mixer_in, second_mixer_in, first_mixer_out, second_mixer_out, first_gate_up, second_gate_up, first_down_proj, second_down_proj, first_norm_gains, second_norm_gains, first_conv_kernel, second_conv_kernel):
    group = SEQS * LEN
    token_blocks = tokens.reshape(N_DP, group, D)
    seg_blocks = segments.reshape(N_DP, group)
    cot_blocks = cotangent.reshape(N_DP, group, D)
    params = (norm_gains, conv_kernel, mixer_in, mixer_out, gate_up, down_proj)

    def step(totals, item):
        block, seg_block, cot_block = item
        masks = lag_masks(seg_block, LEN)

        def apply(values, gains, kernel, weight_in, weight_out, weight_gu, weight_down):
            return forward(values, masks, gains, kernel, weight_in, weight_out, weight_gu, weight_down)
        result, pull = jax.vjp(apply, block.astype(jnp.float32), norm_gains, conv_kernel, mixer_in, mixer_out, gate_up, down_proj)
        grads = pull(cot_block.astype(jnp.float32))
        totals = tuple((total + grad for total, grad in zip(totals, grads[1:])))
        return (totals, (result.astype(jnp.bfloat16), grads[0]))
    zeros = tuple((jnp.zeros_like(param) for param in params))
    totals, stacked = lax.scan(step, zeros, (token_blocks, seg_blocks, cot_blocks))
    grad_gains, grad_kernel, grad_in, grad_out, grad_gu, grad_down = totals
    block_out = stacked[0].reshape(N_DP * group, D)
    grad_input = stacked[1].reshape(N_DP * group, D)
    in_new = adamw(mixer_in, grad_in, first_mixer_in, second_mixer_in, RATE_MATRIX, DECAY)
    out_new = adamw(mixer_out, grad_out, first_mixer_out, second_mixer_out, RATE_MATRIX, DECAY)
    gu_new = adamw(gate_up, grad_gu, first_gate_up, second_gate_up, RATE_MATRIX, DECAY)
    down_new = adamw(down_proj, grad_down, first_down_proj, second_down_proj, RATE_MATRIX, DECAY)
    gains_new = adamw(norm_gains, grad_gains, first_norm_gains, second_norm_gains, RATE_SMALL, 0.0)
    kernel_new = adamw(conv_kernel, grad_kernel, first_conv_kernel, second_conv_kernel, RATE_SMALL, DECAY)
    return (block_out, grad_input, in_new[0], in_new[1], in_new[2], out_new[0], out_new[1], out_new[2], gu_new[0], gu_new[1], gu_new[2], down_new[0], down_new[1], down_new[2], gains_new[0], gains_new[1], gains_new[2], kernel_new[0], kernel_new[1], kernel_new[2])
```

```python
import jax
import jax.numpy as jnp
from jax import lax
from jax.sharding import PartitionSpec as P

KW = 3
STEP = 10
HALO = 16

EPS_NORM = 1e-05
EPS_ADAM = 1e-08
BETA_FIRST = 0.9
BETA_SECOND = 0.95
RATE_MATRIX = 0.05
RATE_SMALL = 0.5
DECAY = 0.1

BF = jnp.bfloat16
F32 = jnp.float32


def swap(values, axis, bit):
    size = lax.axis_size(axis)
    return lax.ppermute(values, axis, [(i, i ^ bit) for i in range(size)])


def halves(values, axis):
    size = values.shape[axis] // 2
    return (
        lax.slice_in_dim(values, 0, size, axis=axis),
        lax.slice_in_dim(values, size, 2 * size, axis=axis),
    )


def low_bits():
    return (
        [2 << i for i in range((lax.axis_size("dp") // 2).bit_length() - 1)],
        [4 << i for i in range((lax.axis_size("tensor") // 4).bit_length() - 1)],
    )


def gather_weight(shard, wide, cut):
    z_bits, t_bits = low_bits()
    own = shard
    for bit in z_bits:
        own = jnp.concatenate([own, swap(own, "dp", bit)], wide)
    for bit in t_bits:
        own = jnp.concatenate([own, swap(own, "tensor", bit)], cut)
    by_x = swap(own, "dp", 1)
    by_y = swap(own, "tensor", 2)
    near = jnp.concatenate([own, by_x], wide)
    near_core = swap(near, "tensor", 1)
    far_first = swap(halves(by_y, wide)[0], "dp", 1)
    far_second = swap(halves(by_x, wide)[1], "tensor", 2)
    far = jnp.concatenate([by_y, far_first, far_second], wide)
    far_core = swap(far, "tensor", 1)
    return near, near_core, far, far_core


def plus(left, right):
    return (left.astype(F32) + right.astype(F32)).astype(BF)


def scatter_grad(blocks, wide, cut):
    z_bits, t_bits = low_bits()
    near, near_core, far, far_core = blocks
    far_in = swap(far_core, "tensor", 1)
    near_in = swap(near_core, "tensor", 1)
    far_low, far_high = halves(far, wide)
    far_in_low, far_in_high = halves(far_in, wide)
    corner = [plus(a, b) for a, b in zip(halves(far_high, wide), halves(far_in_high, wide))]
    to_x = swap(corner[0], "dp", 1)
    to_y = swap(corner[1], "tensor", 2)
    near_low, near_high = halves(near, wide)
    near_in_low, near_in_high = halves(near_in, wide)
    far_parts = [a.astype(F32) + b.astype(F32) for a, b in zip(halves(far_low, wide), halves(far_in_low, wide))]
    by_y = jnp.concatenate(
        [(far_parts[0] + to_x.astype(F32)).astype(BF), far_parts[1].astype(BF)], wide
    )
    near_parts = [
        a.astype(F32) + b.astype(F32) for a, b in zip(halves(near_high, wide), halves(near_in_high, wide))
    ]
    by_x = jnp.concatenate(
        [near_parts[0].astype(BF), (near_parts[1] + to_y.astype(F32)).astype(BF)], wide
    )
    got_y = swap(by_y, "tensor", 2)
    got_x = swap(by_x, "dp", 1)
    total = (
        near_low.astype(F32) + near_in_low.astype(F32) + got_y.astype(F32) + got_x.astype(F32)
    )
    for bit in reversed(t_bits):
        keep, give = halves(total, cut)
        total = keep + swap(give.astype(BF), "tensor", bit).astype(F32)
    for bit in reversed(z_bits):
        keep, give = halves(total, wide)
        total = keep + swap(give.astype(BF), "dp", bit).astype(F32)
    return total


def rotate_left(values, count):
    bits = count.bit_length() - 1
    return ((values << 1) | (values >> (bits - 1))) & (count - 1)


def rotate_right(values, count):
    bits = count.bit_length() - 1
    return ((values & 1) << (bits - 1)) | (values >> 1)


def to_relative(values, index, count):
    width = values.shape[-1] // count
    axis = values.ndim - 1
    return jnp.concatenate(
        [
            lax.dynamic_slice_in_dim(values, (index ^ rotate_left(j, count)) * width, width, axis)
            for j in range(count)
        ],
        axis,
    )


def to_natural(values, index, count):
    width = values.shape[-1] // count
    axis = values.ndim - 1
    return jnp.concatenate(
        [
            lax.dynamic_slice_in_dim(values, rotate_right(index ^ q, count) * width, width, axis)
            for q in range(count)
        ],
        axis,
    )


def block_codes(count):
    return [base ^ (e << 2) for base in (0, 1, 2, 3) for e in range(count // 4)]


def block_place(code, count):
    return (code & 3) * (count // 4) + (code >> 2)


def shift_rows(values, start, rows):
    return lax.slice_in_dim(values, start, start + rows, axis=0)


def lag_masks(seg_flat, length):
    positions = jnp.arange(seg_flat.shape[0], dtype=jnp.int32) % length
    masks = []
    for shift in range(1, KW):
        before = jnp.concatenate([jnp.zeros((shift,), seg_flat.dtype), seg_flat[:-shift]], 0)
        same = (positions >= shift) & (seg_flat == before)
        masks.append(jnp.where(same, 1.0, 0.0).astype(F32)[:, None])
    return masks


def rms_scale(values):
    return lax.rsqrt(jnp.mean(values * values, axis=-1, keepdims=True) + EPS_NORM)


def norm_back(values, scale, gain, upstream):
    scaled = upstream * gain
    gain_grad = jnp.sum(upstream * values * scale, axis=0)
    value_grad = scale * scaled - values * scale * scale * scale * jnp.mean(
        scaled * values, axis=-1, keepdims=True
    )
    return (value_grad, gain_grad)


def adamw(param, grad, first, second, rate, decay):
    first_new = BETA_FIRST * first + (1.0 - BETA_FIRST) * grad
    second_new = BETA_SECOND * second + (1.0 - BETA_SECOND) * grad * grad
    first_hat = first_new / (1.0 - BETA_FIRST**STEP)
    second_hat = second_new / (1.0 - BETA_SECOND**STEP)
    return (
        param - rate * (first_hat / (jnp.sqrt(second_hat) + EPS_ADAM) + decay * param),
        first_new,
        second_new,
    )


def mm(spec, left, right, out=F32):
    return jnp.einsum(spec, left, right, preferred_element_type=F32).astype(out)


def local(
    tokens,
    segments,
    cotangent,
    mixer_in,
    mixer_out,
    gate_up,
    down_proj,
    norm_gains,
    conv_kernel,
    first_mixer_in,
    second_mixer_in,
    first_mixer_out,
    second_mixer_out,
    first_gate_up,
    second_gate_up,
    first_down_proj,
    second_down_proj,
    first_norm_gains,
    second_norm_gains,
    first_conv_kernel,
    second_conv_kernel,
):
    dp_size, t_size = lax.axis_size("dp"), lax.axis_size("tensor")
    dp_index, t_index = lax.axis_index("dp"), lax.axis_index("tensor")
    rows, length = tokens.shape[0], segments.shape[1]

    small = lax.all_gather(
        jnp.concatenate([norm_gains, conv_kernel], 0), ("dp", "tensor"), axis=1, tiled=True
    )
    before = lax.ppermute(
        tokens[rows - HALO :], "tensor", [(i, i + 1) for i in range(t_size - 1)]
    )
    win = gather_weight(mixer_in.astype(BF), 1, 2)
    wout = gather_weight(mixer_out.astype(BF), 1, 0)
    wgu = gather_weight(gate_up.astype(BF), 1, 2)
    wdown = gather_weight(down_proj.astype(BF), 1, 0)

    gains = to_relative(small[:2], dp_index, dp_size)
    kernel_full = small[2:]
    channels = kernel_full.shape[1] // t_size
    codes = block_codes(t_size)
    kernel = jnp.concatenate(
        [
            lax.dynamic_slice_in_dim(kernel_full, (t_index ^ code) * channels, channels, 1)
            for code in codes
        ],
        1,
    )

    masks = []
    for mask in lag_masks(segments.reshape(-1), length):
        padded = jnp.concatenate([mask, jnp.zeros((HALO, 1), F32)], 0)
        masks.append(lax.dynamic_slice_in_dim(padded, t_index * rows, rows + HALO, 0))

    extended = to_relative(jnp.concatenate([before, tokens], 0), dp_index, dp_size).astype(F32)
    scale_ext = rms_scale(extended)
    normed_ext = (extended * scale_ext * gains[0]).astype(BF)
    values, scale_one, normed_one = extended[HALO:], scale_ext[HALO:], normed_ext[HALO:]
    cot = to_relative(cotangent, dp_index, dp_size)

    win_all = jnp.concatenate(win, 2)
    wout_all = jnp.concatenate(wout, 0)
    projected = mm("td,kdc->ktc", normed_ext, win_all)
    part_b, part_c, part_x = projected[0], projected[1][HALO:], projected[2]
    product_ext = part_b * part_x
    part_b, part_x = part_b[HALO:], part_x[HALO:]
    product = product_ext[HALO:]
    convolved = kernel[0] * product
    for shift in range(1, KW):
        convolved = convolved + kernel[shift] * masks[shift - 1][:rows] * shift_rows(
            product_ext, HALO - shift, rows
        )
    gated = (part_c * convolved).astype(BF)
    middle = values + mm("tc,cd->td", gated, wout_all)
    scale_two = rms_scale(middle)
    normed_two = (middle * scale_two * gains[1]).astype(BF)

    branch = jnp.zeros(middle.shape, F32)
    normed_two_grad = jnp.zeros(middle.shape, F32)
    grads_gu, grads_down = [], []
    for w_gu, w_down in zip(wgu, wdown):
        gate_part = mm("td,df->tf", normed_two, w_gu[0])
        up_part = mm("td,df->tf", normed_two, w_gu[1])
        sigma = jax.nn.sigmoid(gate_part)
        silu_gate = gate_part * sigma
        activated = (silu_gate * up_part).astype(BF)
        grads_down.append(mm("tf,td->fd", activated, cot, BF))
        act_grad = mm("td,fd->tf", cot, w_down)
        gate_grad = (act_grad * up_part * sigma * (1.0 + gate_part * (1.0 - sigma))).astype(BF)
        up_grad = (act_grad * silu_gate).astype(BF)
        grads_gu.append(
            jnp.stack(
                [mm("td,tf->df", normed_two, gate_grad, BF), mm("td,tf->df", normed_two, up_grad, BF)], 0
            )
        )
        branch = branch + mm("tf,fd->td", activated, w_down)
        normed_two_grad = (
            normed_two_grad
            + mm("tf,df->td", gate_grad, w_gu[0])
            + mm("tf,df->td", up_grad, w_gu[1])
        )
    block_out = to_natural((middle + branch).astype(BF), dp_index, dp_size)
    grad_down = scatter_grad(grads_down, 1, 0)
    grad_gate_up = scatter_grad(grads_gu, 1, 2)

    middle_norm_grad, gain_two_grad = norm_back(middle, scale_two, gains[1], normed_two_grad)
    middle_grad = cot.astype(F32) + middle_norm_grad
    mixed_grad = middle_grad.astype(BF)
    gated_grad = mm("td,cd->tc", mixed_grad, wout_all)
    conv_grad = gated_grad * part_c
    after_rel = lax.ppermute(
        conv_grad[:8], "tensor", [(i + 1, i) for i in range(t_size - 1)]
    )
    after = jnp.concatenate(
        [
            lax.dynamic_slice_in_dim(
                after_rel,
                block_place(code ^ t_index ^ (t_index + 1), t_size) % t_size * channels,
                channels,
                1,
            )
            for code in codes
        ],
        1,
    )
    grad_out_all = mm("tc,td->cd", gated, mixed_grad, BF)
    size = channels * (t_size // 4)
    grad_out = scatter_grad([grad_out_all[i * size : (i + 1) * size] for i in range(4)], 1, 0)
    c_grad = gated_grad * convolved
    conv_ext = jnp.concatenate([conv_grad, after], 0)
    kernel_rows = [jnp.sum(conv_grad * product, axis=0)]
    product_grad = kernel[0] * conv_grad
    for shift in range(1, KW):
        masked = masks[shift - 1][: rows + 8] * conv_ext
        kernel_rows.append(
            jnp.sum(masked[:rows] * shift_rows(product_ext, HALO - shift, rows), axis=0)
        )
        product_grad = product_grad + kernel[shift] * shift_rows(masked, shift, rows)
    proj_grad = jnp.stack([product_grad * part_x, c_grad, product_grad * part_b], 0).astype(BF)
    grads_in = [
        mm("td,ktc->kdc", normed_one, proj_grad[:, :, i * size : (i + 1) * size], BF) for i in range(4)
    ]
    grad_in = scatter_grad(grads_in, 1, 2)
    normed_one_grad = mm("ktc,kdc->td", proj_grad, win_all)
    input_norm_grad, gain_one_grad = norm_back(values, scale_one, gains[0], normed_one_grad)
    grad_input = to_natural(middle_grad + input_norm_grad, dp_index, dp_size)

    gain_sums = to_natural(jnp.stack([gain_one_grad, gain_two_grad], 0), dp_index, dp_size)
    kernel_rel = jnp.stack(kernel_rows, 0)
    kernel_sums = jnp.concatenate(
        [
            lax.dynamic_slice_in_dim(
                kernel_rel, block_place(t_index ^ q, t_size) * channels, channels, 1
            )
            for q in range(t_size)
        ],
        1,
    )
    sums = jnp.concatenate([gain_sums, kernel_sums], 0)
    for axis, size_axis in (("tensor", t_size), ("dp", dp_size)):
        for i in range(size_axis.bit_length() - 1):
            sums = sums + swap(sums, axis, 1 << i)
    own_width = norm_gains.shape[1]
    own = lax.dynamic_slice_in_dim(sums, (dp_index * t_size + t_index) * own_width, own_width, 1)

    in_new = adamw(mixer_in, grad_in, first_mixer_in, second_mixer_in, RATE_MATRIX, DECAY)
    out_new = adamw(mixer_out, grad_out, first_mixer_out, second_mixer_out, RATE_MATRIX, DECAY)
    gu_new = adamw(gate_up, grad_gate_up, first_gate_up, second_gate_up, RATE_MATRIX, DECAY)
    down_new = adamw(down_proj, grad_down, first_down_proj, second_down_proj, RATE_MATRIX, DECAY)
    gains_new = adamw(norm_gains, own[:2], first_norm_gains, second_norm_gains, RATE_SMALL, 0.0)
    kernel_new = adamw(conv_kernel, own[2:], first_conv_kernel, second_conv_kernel, RATE_SMALL, DECAY)
    return (block_out, grad_input, *in_new, *out_new, *gu_new, *down_new, *gains_new, *kernel_new)


def solution(mesh):
    rows = P(("dp", "tensor"), None)
    in_w, out_w, small = P(None, "dp", "tensor"), P("tensor", "dp"), P(None, ("dp", "tensor"))
    return jax.shard_map(
        local,
        mesh=mesh,
        in_specs=(
            (rows, P("dp", None), rows, in_w, out_w, in_w, out_w, small, small)
            + (in_w,) * 2
            + (out_w,) * 2
            + (in_w,) * 2
            + (out_w,) * 2
            + (small,) * 4
        ),
        out_specs=(rows, rows)
        + (in_w,) * 3
        + (out_w,) * 3
        + (in_w,) * 3
        + (out_w,) * 3
        + (small,) * 6,
        check_vma=False,
    )
```

```python
import functools

import jax
import jax.numpy as jnp
from jax import lax
from jax.experimental import pallas as pl
from jax.experimental.pallas import tpu as pltpu
from jax.sharding import PartitionSpec as P

KW = 3
STEP = 10
HALO = 16
PARTS = 3

EPS_NORM = 1e-05
EPS_ADAM = 1e-08
BETA_FIRST = 0.9
BETA_SECOND = 0.95
RATE_MATRIX = 0.05
RATE_SMALL = 0.5
DECAY = 0.1

BF = jnp.bfloat16
F32 = jnp.float32


def swap(values, axis, bit):
    size = lax.axis_size(axis)
    return lax.ppermute(values, axis, [(i, i ^ bit) for i in range(size)])


def halves(values, axis):
    size = values.shape[axis] // 2
    return (
        lax.slice_in_dim(values, 0, size, axis=axis),
        lax.slice_in_dim(values, size, 2 * size, axis=axis),
    )


def low_bits():
    return (
        [2 << i for i in range((lax.axis_size("dp") // 2).bit_length() - 1)],
        [4 << i for i in range((lax.axis_size("tensor") // 4).bit_length() - 1)],
    )


def gather_weight(shard, wide, cut):
    z_bits, t_bits = low_bits()
    own = shard
    for bit in z_bits:
        own = jnp.concatenate([own, swap(own, "dp", bit)], wide)
    for bit in t_bits:
        own = jnp.concatenate([own, swap(own, "tensor", bit)], cut)
    by_x = swap(own, "dp", 1)
    by_y = swap(own, "tensor", 2)
    near = jnp.concatenate([own, by_x], wide)
    near_core = swap(near, "tensor", 1)
    far_first = swap(halves(by_y, wide)[0], "dp", 1)
    far_second = swap(halves(by_x, wide)[1], "tensor", 2)
    far = jnp.concatenate([by_y, far_first, far_second], wide)
    far_core = swap(far, "tensor", 1)
    return near, near_core, far, far_core


def plus(left, right):
    return (left.astype(F32) + right.astype(F32)).astype(BF)


def scatter_corner(far, far_in, wide):
    far_high, far_in_high = halves(far, wide)[1], halves(far_in, wide)[1]
    corner = [plus(a, b) for a, b in zip(halves(far_high, wide), halves(far_in_high, wide))]
    return swap(corner[0], "dp", 1), swap(corner[1], "tensor", 2)


def scatter_sides(near, near_in, far, far_in, to_x, to_y, wide):
    far_low, far_in_low = halves(far, wide)[0], halves(far_in, wide)[0]
    near_high, near_in_high = halves(near, wide)[1], halves(near_in, wide)[1]
    far_parts = [a.astype(F32) + b.astype(F32) for a, b in zip(halves(far_low, wide), halves(far_in_low, wide))]
    near_parts = [
        a.astype(F32) + b.astype(F32) for a, b in zip(halves(near_high, wide), halves(near_in_high, wide))
    ]
    by_y = jnp.concatenate(
        [(far_parts[0] + to_x.astype(F32)).astype(BF), far_parts[1].astype(BF)], wide
    )
    by_x = jnp.concatenate(
        [near_parts[0].astype(BF), (near_parts[1] + to_y.astype(F32)).astype(BF)], wide
    )
    return swap(by_x, "dp", 1), swap(by_y, "tensor", 2)


def scatter_rest(near, near_in, got_x, got_y, wide, cut):
    z_bits, t_bits = low_bits()
    terms = [halves(near, wide)[0], halves(near_in, wide)[0], got_x, got_y]
    total = None
    for axis, bits, name in ((cut, t_bits, "tensor"), (wide, z_bits, "dp")):
        for bit in reversed(bits):
            parts = [halves(term, axis) for term in terms]
            give = functools.reduce(jnp.add, [part[1].astype(F32) for part in parts]).astype(BF)
            terms = [part[0] for part in parts] + [swap(give, name, bit)]
    return functools.reduce(jnp.add, [term.astype(F32) for term in terms])


def rotate_left(values, count):
    bits = count.bit_length() - 1
    return ((values << 1) | (values >> (bits - 1))) & (count - 1)


def rotate_right(values, count):
    bits = count.bit_length() - 1
    return ((values & 1) << (bits - 1)) | (values >> 1)


def block_codes(count):
    return [base ^ (e << 2) for base in (0, 1, 2, 3) for e in range(count // 4)]


def block_place(code, count):
    return (code & 3) * (count // 4) + (code >> 2)


def shift_rows(values, start, rows):
    return lax.slice_in_dim(values, start, start + rows, axis=0)


def lag_masks(seg_flat, length):
    positions = jnp.arange(seg_flat.shape[0], dtype=jnp.int32) % length
    masks = []
    for shift in range(1, KW):
        before = jnp.concatenate([jnp.zeros((shift,), seg_flat.dtype), seg_flat[:-shift]], 0)
        same = (positions >= shift) & (seg_flat == before)
        masks.append(jnp.where(same, 1.0, 0.0).astype(F32)[:, None])
    return masks


def rms_scale(values):
    return lax.rsqrt(jnp.mean(values * values, axis=-1, keepdims=True) + EPS_NORM)


def adamw(param, grad, first, second, rate, decay):
    first_new = BETA_FIRST * first + (1.0 - BETA_FIRST) * grad
    second_new = BETA_SECOND * second + (1.0 - BETA_SECOND) * grad * grad
    first_hat = first_new / (1.0 - BETA_FIRST**STEP)
    second_hat = second_new / (1.0 - BETA_SECOND**STEP)
    return (
        param - rate * (first_hat / (jnp.sqrt(second_hat) + EPS_ADAM) + decay * param),
        first_new,
        second_new,
    )


def mm(spec, left, right, out=F32):
    return jnp.einsum(spec, left, right, preferred_element_type=F32).astype(out)


ANY = pl.BlockSpec(memory_space=pl.ANY)
LIMIT = 44 * 1024 * 1024


def params(count=1):
    return pltpu.CompilerParams(
        vmem_limit_bytes=LIMIT, dimension_semantics=("arbitrary",) * count
    )


def whole(shape):
    return pl.BlockSpec(shape, lambda *_: (0,) * len(shape), pipeline_mode=pl.Buffered(1))


def arrange_kernel(order, tokens, before, cot, x_out, cot_out):
    count = order.shape[0]
    width = tokens.shape[1] // count
    for j in range(count):
        spot = pl.ds(pl.multiple_of(order[j] * width, width), width)
        own = pl.ds(j * width, width)
        x_out[:HALO, own] = before[:, spot]
        x_out[HALO:, own] = tokens[:, spot]
        cot_out[:, own] = cot[:, spot]


def pick_blocks(values, places):
    count = places.shape[0]
    width = values.shape[1] // count
    return jnp.concatenate(
        [lax.dynamic_slice_in_dim(values, places[j] * width, width, 1) for j in range(count)], 1
    )


def narrow(order, width):
    return (width // order.shape[0]) % 128 != 0


def to_natural(values, order):
    if not narrow(order, values.shape[1]):
        return values
    return pick_blocks(values, jnp.argsort(order))


def arrange(order, tokens, before, cot):
    rows, width = tokens.shape
    if narrow(order, width):
        extended = jnp.concatenate([before, tokens], 0)
        return pick_blocks(extended, order), pick_blocks(cot, order)
    vmem = pl.BlockSpec(memory_space=pltpu.VMEM)
    return pl.pallas_call(
        arrange_kernel,
        out_shape=(
            jax.ShapeDtypeStruct((rows + HALO, width), BF),
            jax.ShapeDtypeStruct((rows, width), BF),
        ),
        in_specs=[pl.BlockSpec(memory_space=pltpu.SMEM), vmem, vmem, vmem],
        out_specs=(vmem, vmem),
        compiler_params=pltpu.CompilerParams(vmem_limit_bytes=LIMIT),
        name="arrange",
    )(order, tokens, before, cot)


def nt(left, right):
    return lax.dot_general(left, right, (((1,), (1,)), ((), ())), preferred_element_type=F32)


def nn(left, right):
    return jnp.dot(left, right, preferred_element_type=F32)


def ffn_kernel(h, ht, c, ct, wa, wb, *rest):
    ga, gb, branch, back, branch_sum, back_sum = rest[-6:]
    step = pl.program_id(0)
    half = wa.shape[2]
    wg, wu, wd = [jnp.concatenate([wa[k], wb[k]], 1) for k in range(3)]
    gate = nn(h[...], wg)
    up = nn(h[...], wu)
    da = nn(c[...], wd)
    sigma = 1.0 / (1.0 + jnp.exp(-gate))
    silu = gate * sigma
    act = (silu * up).astype(BF)
    dgate = (da * up * sigma * (1.0 + gate * (1.0 - sigma))).astype(BF)
    dup = (da * silu).astype(BF)
    for k, (left, right) in enumerate(((ht, dgate), (ht, dup), (ct, act))):
        grad = nn(left[...], right).astype(BF)
        ga[k] = grad[:, :half]
        gb[k] = grad[:, half:]
    out = nt(act, wd)
    into = nt(jnp.concatenate([dgate, dup], 1), jnp.concatenate([wg, wu], 1))

    @pl.when(step == 0)
    def _():
        branch_sum[...] = out
        back_sum[...] = into

    @pl.when(step > 0)
    def _():
        branch_sum[...] += out
        back_sum[...] += into

    @pl.when(step == pl.num_programs(0) - 1)
    def _():
        branch[...] = branch_sum[...].astype(BF)
        back[...] = back_sum[...].astype(BF)


def ffn(h, ht, c, ct, wa, wb, deps):
    rows, width = h.shape
    cols = wa.shape[2]
    tile = 128
    block = pl.BlockSpec((3, width, tile), lambda j: (0, 0, j))
    grad = jax.ShapeDtypeStruct(wa.shape, BF)
    part = jax.ShapeDtypeStruct((rows, width), BF)
    return pl.pallas_call(
        ffn_kernel,
        grid=(cols // tile,),
        out_shape=(grad, grad, part, part),
        in_specs=[whole((rows, width)), whole((width, rows)), whole((rows, width)), whole((width, rows))]
        + [block, block]
        + [ANY] * len(deps),
        out_specs=(block, block, whole((rows, width)), whole((rows, width))),
        scratch_shapes=[pltpu.VMEM((rows, width), F32)] * 2,
        compiler_params=params(),
        cost_estimate=pl.CostEstimate(
            flops=36 * rows * width * cols,
            bytes_accessed=12 * rows * width + 24 * width * cols,
            transcendentals=2 * rows * cols,
        ),
        name="ffn",
    )(h, ht, c, ct, wa, wb, *deps)


def middle_kernel(order, middle, scale, gain, cot, *rest):
    block_out, grad, grad_low, gain_grad = rest[-4:]
    half = (len(rest) - 4) // 2
    branches, backs = rest[:half], rest[half : 2 * half]
    x2, r2, up = middle[...], scale[...], backs[0][...].astype(F32)
    for ref in backs[1:]:
        up = up + ref[...].astype(F32)
    total = x2
    for ref in branches:
        total = total + ref[...].astype(F32)
    store_natural(order, block_out, total.astype(BF))
    norm_back(x2, r2, gain, up, cot[...].astype(F32), grad, gain_grad)
    grad_low[...] = grad[...].astype(BF)


def store_natural(order, out, total):
    count = order.shape[0]
    if narrow(order, total.shape[1]):
        out[...] = total
        return
    width = total.shape[1] // count
    for j in range(count):
        spot = pl.ds(pl.multiple_of(order[j] * width, width), width)
        out[:, spot] = total[:, j * width : (j + 1) * width]


def norm_back(values, scale, gain, upstream, carried, out, gain_grad, order=None):
    scaled = upstream * gain[...]
    mean = jnp.mean(scaled * values, axis=-1, keepdims=True)
    total = carried + scale * scaled - values * (scale * scale * scale * mean)
    if order is None:
        out[...] = total
    else:
        store_natural(order, out, total)
    sums = jnp.sum(upstream * values * scale, axis=0, keepdims=True)

    @pl.when(pl.program_id(0) == 0)
    def _():
        gain_grad[...] = sums

    @pl.when(pl.program_id(0) > 0)
    def _():
        gain_grad[...] += sums


def row_specs(tile, width):
    return (
        pl.BlockSpec(memory_space=pltpu.SMEM),
        pl.BlockSpec((tile, width), lambda i: (i, 0)),
        pl.BlockSpec((tile, 1), lambda i: (i, 0)),
        pl.BlockSpec((1, width), lambda i: (0, 0)),
    )


def middle_back(order, middle, scale, gain, cot, branches, backs, deps):
    rows, width = middle.shape
    tile = 128
    smem, row, column, single = row_specs(tile, width)
    count = len(branches)

    def kernel(*refs):
        middle_kernel(*refs[: 5 + 2 * count], *refs[5 + 2 * count + len(deps) :])

    return pl.pallas_call(
        kernel,
        grid=(rows // tile,),
        out_shape=(
            jax.ShapeDtypeStruct((rows, width), BF),
            jax.ShapeDtypeStruct((rows, width), F32),
            jax.ShapeDtypeStruct((rows, width), BF),
            jax.ShapeDtypeStruct((1, width), F32),
        ),
        in_specs=[smem, row, column, single, row] + [row] * (2 * count) + [ANY] * len(deps),
        out_specs=(row, row, row, single),
        compiler_params=params(),
        cost_estimate=pl.CostEstimate(
            flops=30 * rows * width, bytes_accessed=(14 + 4 * count) * rows * width, transcendentals=0
        ),
        name="middle_back",
    )(order, middle, scale, gain, cot, *branches, *backs, *deps)


def input_kernel(order, values, scale, gain, carried, upstream, out, gain_grad):
    norm_back(
        values[...].astype(F32), scale[...], gain, upstream[...], carried[...], out, gain_grad, order
    )


def input_back(order, values, scale, gain, carried, upstream):
    rows, width = values.shape
    tile = 128
    smem, row, column, single = row_specs(tile, width)
    return pl.pallas_call(
        input_kernel,
        grid=(rows // tile,),
        out_shape=(
            jax.ShapeDtypeStruct((rows, width), F32),
            jax.ShapeDtypeStruct((1, width), F32),
        ),
        in_specs=[smem, row, column, single, row, row],
        out_specs=(row, single),
        compiler_params=params(),
        cost_estimate=pl.CostEstimate(
            flops=20 * rows * width, bytes_accessed=14 * rows * width, transcendentals=0
        ),
        name="input_back",
    )(order, values, scale, gain, carried, upstream)


def mixer_grad_kernel(ht, dt, pa, pb, ya, yb, *rest):
    ga, gb = rest[-2:]
    step = pl.program_id(0)

    @pl.when(step < 3)
    def _():
        ga[0] = nn(ht[...], pa[0]).astype(BF)
        gb[0] = nn(ht[...], pb[0]).astype(BF)

    @pl.when(step == 3)
    def _():
        ga[0] = nn(dt[...], ya[...]).astype(BF)
        gb[0] = nn(dt[...], yb[...]).astype(BF)


def mixer_grad(ht, dt, proj_grad, gated, first, second, deps):
    width, rows = ht.shape
    cols = gated.shape[1] // 4

    def column(block):
        return pl.BlockSpec((1, rows, cols), lambda k: (jnp.minimum(k, 2), 0, block))

    def gated_column(block):
        return pl.BlockSpec((rows, cols), lambda k: (0, block))

    out = pl.BlockSpec((1, width, cols), lambda k: (k, 0, 0))
    grad = jax.ShapeDtypeStruct((4, width, cols), BF)
    return pl.pallas_call(
        mixer_grad_kernel,
        grid=(4,),
        out_shape=(grad, grad),
        in_specs=[
            whole((width, rows)),
            whole((width, rows)),
            column(first),
            column(second),
            gated_column(first),
            gated_column(second),
        ]
        + [ANY] * len(deps),
        out_specs=(out, out),
        compiler_params=params(),
        cost_estimate=pl.CostEstimate(
            flops=16 * rows * width * cols,
            bytes_accessed=4 * rows * width + 16 * width * cols + 16 * rows * cols,
            transcendentals=0,
        ),
        name="mixer_grad",
    )(ht, dt, proj_grad, proj_grad, gated, gated, *deps)


def update_kernel(*refs):
    count = (len(refs) - 12)
    totals, rest = refs[:count], refs[count:]
    wide, tall, wide_new, tall_new = rest[:3], rest[3:6], rest[6:9], rest[9:]
    for i, total in enumerate(totals):

        @pl.when(pl.program_id(0) == i)
        def _():
            last = total.shape[0] - 1
            new = adamw(wide[0][...], total[:last], wide[1][...], wide[2][...], RATE_MATRIX, DECAY)
            for ref, value in zip(wide_new, new):
                ref[...] = value
            grad = jnp.transpose(total[last])
            new = adamw(tall[0][...], grad, tall[1][...], tall[2][...], RATE_MATRIX, DECAY)
            for ref, value in zip(tall_new, new):
                ref[...] = value


def update(totals, wide, tall):
    if (wide[0].shape[2] // len(totals)) % 128:
        totals = [jnp.concatenate(totals, 2)]
    count = len(totals)
    planes, deep, cols = wide[0].shape
    part = cols // count
    wide_spec = pl.BlockSpec((planes, deep, part), lambda i: (0, 0, i))
    tall_spec = pl.BlockSpec((part, deep), lambda i: (i, 0))
    return pl.pallas_call(
        update_kernel,
        grid=(count,),
        out_shape=tuple(jax.ShapeDtypeStruct(a.shape, F32) for a in wide + tall),
        in_specs=[whole(total.shape) for total in totals] + [wide_spec] * 3 + [tall_spec] * 3,
        out_specs=(wide_spec,) * 3 + (tall_spec,) * 3,
        compiler_params=params(),
        cost_estimate=pl.CostEstimate(
            flops=20 * (planes + 1) * deep * cols,
            bytes_accessed=28 * (planes + 1) * deep * cols,
            transcendentals=(planes + 1) * deep * cols,
        ),
        name="update",
    )(*totals, *wide, *tall)


def local(
    tokens,
    segments,
    cotangent,
    mixer_in,
    mixer_out,
    gate_up,
    down_proj,
    norm_gains,
    conv_kernel,
    first_mixer_in,
    second_mixer_in,
    first_mixer_out,
    second_mixer_out,
    first_gate_up,
    second_gate_up,
    first_down_proj,
    second_down_proj,
    first_norm_gains,
    second_norm_gains,
    first_conv_kernel,
    second_conv_kernel,
):
    dp_size, t_size = lax.axis_size("dp"), lax.axis_size("tensor")
    dp_index, t_index = lax.axis_index("dp"), lax.axis_index("tensor")
    rows, length = tokens.shape[0], segments.shape[1]
    order = dp_index ^ jnp.array([rotate_left(j, dp_size) for j in range(dp_size)], jnp.int32)

    before = lax.ppermute(
        tokens[rows - HALO :], "tensor", [(i, i + 1) for i in range(t_size - 1)]
    )
    wm = gather_weight(
        jnp.concatenate([mixer_in.astype(BF), mixer_out.T.astype(BF)[None]], 0), 1, 2
    )
    ffn_cols = gate_up.shape[2] // PARTS
    wf = []
    for i in range(PARTS):
        cols = slice(i * ffn_cols, (i + 1) * ffn_cols)
        packed = jnp.concatenate(
            [gate_up[:, :, cols].astype(BF), down_proj[cols].T.astype(BF)[None]], 0
        )
        wf.append(gather_weight(packed, 1, 2))

    small = jnp.concatenate([norm_gains, conv_kernel], 0)[:, None, :]
    for axis, size_axis in (("tensor", t_size), ("dp", dp_size)):
        for i in range(size_axis.bit_length() - 1):
            small = jnp.concatenate([small, swap(small, axis, 1 << i)], 1)
    small = small.reshape(small.shape[0], dp_size, t_size, small.shape[2])
    for axis, index, size_axis in ((1, dp_index, dp_size), (2, t_index, t_size)):
        for i in range(size_axis.bit_length() - 1):
            shape = small.shape
            split = small.reshape(shape[:axis] + (size_axis >> (i + 1), 2, 1 << i) + shape[axis + 1 :])
            flipped = jnp.flip(split, axis + 1)
            small = jnp.where((index >> i) & 1 == 1, flipped, split).reshape(shape)
    small = small.reshape(small.shape[0], -1)
    wide = small.shape[1] // dp_size
    gains = jnp.concatenate(
        [lax.dynamic_slice_in_dim(small[:2], order[j] * wide, wide, 1) for j in range(dp_size)], 1
    )
    channels = small.shape[1] // t_size
    codes = block_codes(t_size)
    kernel = jnp.concatenate(
        [
            lax.dynamic_slice_in_dim(small[2:], (t_index ^ code) * channels, channels, 1)
            for code in codes
        ],
        1,
    )

    masks = []
    for mask in lag_masks(segments.reshape(-1), length):
        padded = jnp.concatenate([mask, jnp.zeros((HALO, 1), F32)], 0)
        masks.append(lax.dynamic_slice_in_dim(padded, t_index * rows, rows + HALO, 0))

    x_ext, cot = arrange(order, tokens, before, cotangent)
    extended = x_ext.astype(F32)
    scale_ext = rms_scale(extended)
    normed_ext = (extended * scale_ext * gains[0]).astype(BF)
    values, scale_one, normed_one = extended[HALO:], scale_ext[HALO:], normed_ext[HALO:]
    wm_all = jnp.concatenate(wm, 2)
    win_all, wout_all = wm_all[:3], wm_all[3]
    projected = mm("td,kdc->ktc", normed_ext, win_all)
    part_b, part_c, part_x = projected[0], projected[1][HALO:], projected[2]
    product_ext = part_b * part_x
    part_b, part_x = part_b[HALO:], part_x[HALO:]
    product = product_ext[HALO:]
    convolved = kernel[0] * product
    for shift in range(1, KW):
        convolved = convolved + kernel[shift] * masks[shift - 1][:rows] * shift_rows(
            product_ext, HALO - shift, rows
        )
    gated = (part_c * convolved).astype(BF)
    middle = values + mm("tc,dc->td", gated, wout_all)
    scale_two = rms_scale(middle)
    normed_two = (middle * scale_two * gains[1]).astype(BF)

    norm_t, cot_t = normed_two.T, cot.T
    branches, backs, grads = [], [], []
    near_in, far_in, corner, sides = [], [], [], []
    for i in range(PARTS):
        near, near_core, far, far_core = wf[i]
        deps = []
        if i >= 1:
            deps.append(near_in[i - 1])
        if i >= 2:
            deps += corner[i - 2]
        g_near, g_near_core, branch, back = ffn(normed_two, norm_t, cot, cot_t, near, near_core, deps)
        branches.append(branch)
        backs.append(back)
        near_in.append(swap(g_near_core, "tensor", 1))
        if i >= 2:
            sides.append(scatter_sides(*grads[i - 2][:1], near_in[i - 2], grads[i - 2][1], far_in[i - 2], *corner[i - 2], 1))
        deps = [far_in[i - 1]] if i >= 1 else []
        g_far, g_far_core, branch, back = ffn(normed_two, norm_t, cot, cot_t, far, far_core, deps)
        branches.append(branch)
        backs.append(back)
        far_in.append(swap(g_far_core, "tensor", 1))
        grads.append((g_near, g_far))
        if i >= 1:
            corner.append(scatter_corner(grads[i - 1][1], far_in[i - 1], 1))

    def finish_sides(i):
        return scatter_sides(grads[i][0], near_in[i], grads[i][1], far_in[i], *corner[i], 1)

    block_out, middle_grad, mixed_grad, gain_two_grad = middle_back(
        order, middle, scale_two, gains[1:2], cot, branches, backs, [near_in[-1], *corner[-1]]
    )
    corner.append(scatter_corner(grads[-1][1], far_in[-1], 1))
    while len(sides) < PARTS - 1:
        sides.append(finish_sides(len(sides)))

    gated_grad = mm("td,dc->tc", mixed_grad, wout_all)
    conv_grad = gated_grad * part_c
    after_rel = lax.ppermute(
        conv_grad[:8], "tensor", [(i + 1, i) for i in range(t_size - 1)]
    )
    after = jnp.concatenate(
        [
            lax.dynamic_slice_in_dim(
                after_rel,
                block_place(code ^ t_index ^ (t_index + 1), t_size) % t_size * channels,
                channels,
                1,
            )
            for code in codes
        ],
        1,
    )
    c_grad = gated_grad * convolved
    conv_ext = jnp.concatenate([conv_grad, after], 0)
    kernel_rows = [jnp.sum(conv_grad * product, axis=0)]
    product_grad = kernel[0] * conv_grad
    for shift in range(1, KW):
        masked = masks[shift - 1][: rows + 8] * conv_ext
        kernel_rows.append(
            jnp.sum(masked[:rows] * shift_rows(product_ext, HALO - shift, rows), axis=0)
        )
        product_grad = product_grad + kernel[shift] * shift_rows(masked, shift, rows)
    proj_grad = jnp.stack([product_grad * part_x, c_grad, product_grad * part_b], 0).astype(BF)
    one_t, mixed_t = normed_one.T, mixed_grad.T
    m_near_core, m_far_core = mixer_grad(
        one_t, mixed_t, proj_grad, gated, 1, 3, [*sides[0], *corner[-1]]
    )
    m_far_in, m_near_in = swap(m_far_core, "tensor", 1), swap(m_near_core, "tensor", 1)
    sides.append(finish_sides(PARTS - 1))
    m_near, m_far = mixer_grad(one_t, mixed_t, proj_grad, gated, 0, 2, [])
    m_corner = scatter_corner(m_far, m_far_in, 1)
    normed_one_grad = mm("ktc,kdc->td", proj_grad, win_all)
    grad_input, gain_one_grad = input_back(
        order, x_ext[HALO:], scale_one, gains[:1], middle_grad, normed_one_grad
    )
    m_sides = scatter_sides(m_near, m_near_in, m_far, m_far_in, *m_corner, 1)

    gain_rel = jnp.concatenate([gain_one_grad, gain_two_grad], 0)
    kernel_rel = jnp.stack(kernel_rows, 0)
    gain_sums = jnp.concatenate(
        [
            lax.dynamic_slice_in_dim(gain_rel, rotate_right(dp_index ^ q, dp_size) * wide, wide, 1)
            for q in range(dp_size)
        ],
        1,
    )
    kernel_sums = jnp.concatenate(
        [
            lax.dynamic_slice_in_dim(
                kernel_rel, block_place(t_index ^ q, t_size) * channels, channels, 1
            )
            for q in range(t_size)
        ],
        1,
    )
    sums = jnp.concatenate([gain_sums, kernel_sums], 0)
    for axis, size_axis in (("tensor", t_size), ("dp", dp_size)):
        for i in range(size_axis.bit_length() - 1):
            sums = sums + swap(sums, axis, 1 << i)
    own_width = norm_gains.shape[1]
    own = lax.dynamic_slice_in_dim(sums, (dp_index * t_size + t_index) * own_width, own_width, 1)

    totals = [
        scatter_rest(grads[i][0], near_in[i], *sides[i], 1, 2) for i in range(PARTS)
    ]
    ffn_new = update(
        totals, (gate_up, first_gate_up, second_gate_up), (down_proj, first_down_proj, second_down_proj)
    )
    total = scatter_rest(m_near, m_near_in, *m_sides, 1, 2)
    mix_new = update(
        [total], (mixer_in, first_mixer_in, second_mixer_in), (mixer_out, first_mixer_out, second_mixer_out)
    )
    gains_new = adamw(norm_gains, own[:2], first_norm_gains, second_norm_gains, RATE_SMALL, 0.0)
    kernel_new = adamw(conv_kernel, own[2:], first_conv_kernel, second_conv_kernel, RATE_SMALL, DECAY)
    block_out, grad_input = to_natural(block_out, order), to_natural(grad_input, order)
    return (block_out, grad_input, *mix_new, *ffn_new, *gains_new, *kernel_new)


def solution(mesh):
    rows = P(("dp", "tensor"), None)
    in_w, out_w, small = P(None, "dp", "tensor"), P("tensor", "dp"), P(None, ("dp", "tensor"))
    return jax.shard_map(
        local,
        mesh=mesh,
        in_specs=(
            (rows, P("dp", None), rows, in_w, out_w, in_w, out_w, small, small)
            + (in_w,) * 2
            + (out_w,) * 2
            + (in_w,) * 2
            + (out_w,) * 2
            + (small,) * 4
        ),
        out_specs=(rows, rows)
        + (in_w,) * 3
        + (out_w,) * 3
        + (in_w,) * 3
        + (out_w,) * 3
        + (small,) * 6,
        check_vma=False,
    )
```

```python
import functools

import jax
import jax.numpy as jnp
from jax import lax
from jax.experimental import pallas as pl
from jax.experimental.pallas import tpu as pltpu
from jax.sharding import PartitionSpec as P

KW = 3
STEP = 10
HALO = 16
PARTS = 3

EPS_NORM = 1e-05
EPS_ADAM = 1e-08
BETA_FIRST = 0.9
BETA_SECOND = 0.95
RATE_MATRIX = 0.05
RATE_SMALL = 0.5
DECAY = 0.1

BF = jnp.bfloat16
F32 = jnp.float32


def swap(values, axis, bit):
    size = lax.axis_size(axis)
    return lax.ppermute(values, axis, [(i, i ^ bit) for i in range(size)])


def halves(values, axis):
    size = values.shape[axis] // 2
    return (
        lax.slice_in_dim(values, 0, size, axis=axis),
        lax.slice_in_dim(values, size, 2 * size, axis=axis),
    )


def low_bits():
    return (
        [2 << i for i in range((lax.axis_size("dp") // 2).bit_length() - 1)],
        [4 << i for i in range((lax.axis_size("tensor") // 4).bit_length() - 1)],
    )


def ordered(value, *others):
    return lax.optimization_barrier((value, *others))[0]


def gather_weights(shards, wide, cut, between):
    z_bits, t_bits = low_bits()
    done, corners = {}, []

    def step(name, value, axis, bit):
        if name in done:
            value = ordered(value, *done[name])
        got = swap(value, axis, bit)
        done[name] = (got,)
        return got

    results = []
    for place, own in enumerate(shards):
        for bit in z_bits:
            if place >= 2 and bit == z_bits[-1]:
                own = ordered(own, *corners[place - 2])
            own = jnp.concatenate([own, step(("z", bit), own, "dp", bit)], wide)
        for bit in t_bits:
            own = jnp.concatenate([own, step(("t", bit), own, "tensor", bit)], cut)
        if place == 1:
            own = ordered(own, *corners[0])
        if place == 2:
            own = ordered(own, result)
        by_x = step("x", own, "dp", 1)
        by_y = step("y", own, "tensor", 2)
        if place == 1:
            by_x, by_y = ordered(by_x, result), ordered(by_y, result)
        near = jnp.concatenate([own, by_x], wide)
        near_core = swap(near, "tensor", 1)
        far_first, far_second = halves(by_y, wide)[0], halves(by_x, wide)[1]
        if place == 1:
            far_first, far_second = ordered(far_first, result), ordered(far_second, result)
        far_first, far_second = swap(far_first, "dp", 1), swap(far_second, "tensor", 2)
        corners.append((far_first, far_second))
        far = jnp.concatenate([by_y, far_first, far_second], wide)
        far_core = swap(far, "tensor", 1)
        results.append((near, near_core, far, far_core))
        if place == 0:
            result = between(results[0])
    return results


def plus(left, right):
    return (left.astype(F32) + right.astype(F32)).astype(BF)


def scatter_corner(far, far_in, wide):
    far_high, far_in_high = halves(far, wide)[1], halves(far_in, wide)[1]
    corner = [plus(a, b) for a, b in zip(halves(far_high, wide), halves(far_in_high, wide))]
    return swap(corner[0], "dp", 1), swap(corner[1], "tensor", 2)


def scatter_sides(near, near_in, far, far_in, to_x, to_y, wide):
    far_low, far_in_low = halves(far, wide)[0], halves(far_in, wide)[0]
    near_high, near_in_high = halves(near, wide)[1], halves(near_in, wide)[1]
    far_parts = [a.astype(F32) + b.astype(F32) for a, b in zip(halves(far_low, wide), halves(far_in_low, wide))]
    near_parts = [
        a.astype(F32) + b.astype(F32) for a, b in zip(halves(near_high, wide), halves(near_in_high, wide))
    ]
    by_y = jnp.concatenate(
        [(far_parts[0] + to_x.astype(F32)).astype(BF), far_parts[1].astype(BF)], wide
    )
    by_x = jnp.concatenate(
        [near_parts[0].astype(BF), (near_parts[1] + to_y.astype(F32)).astype(BF)], wide
    )
    return swap(by_x, "dp", 1), swap(by_y, "tensor", 2)


def scatter_rest(near, near_in, got_x, got_y, wide, cut):
    z_bits, t_bits = low_bits()
    terms = [halves(near, wide)[0], halves(near_in, wide)[0], got_x, got_y]
    total = None
    for axis, bits, name in ((cut, t_bits, "tensor"), (wide, z_bits, "dp")):
        for bit in reversed(bits):
            parts = [halves(term, axis) for term in terms]
            give = functools.reduce(jnp.add, [part[1].astype(F32) for part in parts]).astype(BF)
            terms = [part[0] for part in parts] + [swap(give, name, bit)]
    return functools.reduce(jnp.add, [term.astype(F32) for term in terms])


def rotate_left(values, count):
    bits = count.bit_length() - 1
    return ((values << 1) | (values >> (bits - 1))) & (count - 1)


def rotate_right(values, count):
    bits = count.bit_length() - 1
    return ((values & 1) << (bits - 1)) | (values >> 1)


def block_codes(count):
    return [base ^ (e << 2) for base in (0, 1, 2, 3) for e in range(count // 4)]


def block_place(code, count):
    return (code & 3) * (count // 4) + (code >> 2)


def shift_rows(values, start, rows):
    return lax.slice_in_dim(values, start, start + rows, axis=0)


def lag_masks(seg_flat, length):
    positions = jnp.arange(seg_flat.shape[0], dtype=jnp.int32) % length
    masks = []
    for shift in range(1, KW):
        before = jnp.concatenate([jnp.zeros((shift,), seg_flat.dtype), seg_flat[:-shift]], 0)
        same = (positions >= shift) & (seg_flat == before)
        masks.append(jnp.where(same, 1.0, 0.0).astype(F32)[:, None])
    return masks


def rms_scale(values):
    return lax.rsqrt(jnp.mean(values * values, axis=-1, keepdims=True) + EPS_NORM)


def adamw(param, grad, first, second, rate, decay):
    first_new = BETA_FIRST * first + (1.0 - BETA_FIRST) * grad
    second_new = BETA_SECOND * second + (1.0 - BETA_SECOND) * grad * grad
    first_hat = first_new / (1.0 - BETA_FIRST**STEP)
    second_hat = second_new / (1.0 - BETA_SECOND**STEP)
    return (
        param - rate * (first_hat / (jnp.sqrt(second_hat) + EPS_ADAM) + decay * param),
        first_new,
        second_new,
    )


def mm(spec, left, right, out=F32):
    return jnp.einsum(spec, left, right, preferred_element_type=F32).astype(out)


ANY = pl.BlockSpec(memory_space=pl.ANY)
LIMIT = 26 * 1024 * 1024


def params(count=1):
    return pltpu.CompilerParams(
        vmem_limit_bytes=LIMIT, dimension_semantics=("arbitrary",) * count
    )


def whole(shape):
    return pl.BlockSpec(shape, lambda *_: (0,) * len(shape), pipeline_mode=pl.Buffered(1))


def arrange_kernel(order, tokens, before, cot, x_out, cot_out):
    count = order.shape[0]
    width = tokens.shape[1] // count
    for j in range(count):
        spot = pl.ds(pl.multiple_of(order[j] * width, width), width)
        own = pl.ds(j * width, width)
        x_out[:HALO, own] = before[:, spot]
        x_out[HALO:, own] = tokens[:, spot]
        cot_out[:, own] = cot[:, spot]


def pick_blocks(values, places):
    count = places.shape[0]
    width = values.shape[1] // count
    return jnp.concatenate(
        [lax.dynamic_slice_in_dim(values, places[j] * width, width, 1) for j in range(count)], 1
    )


def narrow(order, width):
    return (width // order.shape[0]) % 128 != 0


def to_natural(values, order):
    if not narrow(order, values.shape[1]):
        return values
    return pick_blocks(values, jnp.argsort(order))


def arrange(order, tokens, before, cot):
    rows, width = tokens.shape
    if narrow(order, width):
        extended = jnp.concatenate([before, tokens], 0)
        return pick_blocks(extended, order), pick_blocks(cot, order)
    vmem = pl.BlockSpec(memory_space=pltpu.VMEM)
    return pl.pallas_call(
        arrange_kernel,
        out_shape=(
            jax.ShapeDtypeStruct((rows + HALO, width), BF),
            jax.ShapeDtypeStruct((rows, width), BF),
        ),
        in_specs=[pl.BlockSpec(memory_space=pltpu.SMEM), vmem, vmem, vmem],
        out_specs=(vmem, vmem),
        compiler_params=pltpu.CompilerParams(vmem_limit_bytes=LIMIT),
        name="arrange",
    )(order, tokens, before, cot)


def nt(left, right):
    return lax.dot_general(left, right, (((1,), (1,)), ((), ())), preferred_element_type=F32)


def nn(left, right):
    return jnp.dot(left, right, preferred_element_type=F32)


def ffn_kernel(first, h, ht, c, ct, wa, wb, *rest):
    ga, gb, branch, back, act, dgate, dup = rest[-7:]
    half = wa.shape[2]
    wg, wu, wd = [jnp.concatenate([wa[k], wb[k]], 1) for k in range(3)]
    rows = h.shape[0]
    tall = rows // 2
    if first:

        @pl.when(pl.program_id(0) == 0)
        def _():
            branch[...] = jnp.zeros_like(branch)
            back[...] = jnp.zeros_like(back)

    for start in range(0, rows, tall):
        span = pl.ds(start, tall)
        gate = nn(h[span, :], wg)
        up = nn(h[span, :], wu)
        da = nn(c[span, :], wd)
        sigma = 1.0 / (1.0 + jnp.exp(-gate))
        silu = gate * sigma
        act[span, :] = (silu * up).astype(BF)
        dup[span, :] = (da * silu).astype(BF)
        dgate[span, :] = (da * up * (sigma + silu * (1.0 - sigma))).astype(BF)
    for k, (left, right) in enumerate(((ht, dgate), (ht, dup), (ct, act))):
        grad = nn(left[...], right[...]).astype(BF)
        ga[k] = grad[:, :half]
        gb[k] = grad[:, half:]
    branch[...] += nt(act[...], wd)
    back[...] += nt(dgate[...], wg) + nt(dup[...], wu)


def ffn(h, ht, c, ct, wa, wb, sums, deps):
    rows, width = h.shape
    cols = wa.shape[2]
    tile = 128
    block = pl.BlockSpec((3, width, tile), lambda j: (0, 0, j))
    vmem = pl.BlockSpec(memory_space=pltpu.VMEM)
    grad = jax.ShapeDtypeStruct(wa.shape, BF)
    part = jax.ShapeDtypeStruct((rows, width), F32)
    return pl.pallas_call(
        functools.partial(ffn_kernel, not sums),
        grid=(cols // tile,),
        out_shape=(grad, grad, part, part),
        in_specs=[vmem] * 4 + [block, block] + [vmem] * len(sums) + [ANY] * len(deps),
        out_specs=(block, block, vmem, vmem),
        input_output_aliases={6: 2, 7: 3} if sums else {},
        scratch_shapes=[pltpu.VMEM((rows, 2 * tile), BF)] * 3,
        compiler_params=params(),
        cost_estimate=pl.CostEstimate(
            flops=36 * rows * width * cols,
            bytes_accessed=24 * width * cols,
            transcendentals=2 * rows * cols,
        ),
        name="ffn",
    )(h, ht, c, ct, wa, wb, *sums, *deps)


def middle_kernel(order, middle, scale, gain, cot, *rest):
    block_out, grad, grad_low, gain_grad = rest[-4:]
    half = (len(rest) - 4) // 2
    branches, backs = rest[:half], rest[half : 2 * half]
    x2, r2, up = middle[...], scale[...], backs[0][...].astype(F32)
    for ref in backs[1:]:
        up = up + ref[...].astype(F32)
    total = x2
    for ref in branches:
        total = total + ref[...].astype(F32)
    store_natural(order, block_out, total.astype(BF))
    norm_back(x2, r2, gain, up, cot[...].astype(F32), grad, gain_grad)
    grad_low[...] = grad[...].astype(BF)


def store_natural(order, out, total):
    count = order.shape[0]
    if narrow(order, total.shape[1]):
        out[...] = total
        return
    width = total.shape[1] // count
    for j in range(count):
        spot = pl.ds(pl.multiple_of(order[j] * width, width), width)
        out[:, spot] = total[:, j * width : (j + 1) * width]


def norm_back(values, scale, gain, upstream, carried, out, gain_grad, order=None):
    scaled = upstream * gain[...]
    mean = jnp.mean(scaled * values, axis=-1, keepdims=True)
    total = carried + scale * scaled - values * (scale * scale * scale * mean)
    if order is None:
        out[...] = total
    else:
        store_natural(order, out, total)
    sums = jnp.sum(upstream * values * scale, axis=0, keepdims=True)

    @pl.when(pl.program_id(0) == 0)
    def _():
        gain_grad[...] = sums

    @pl.when(pl.program_id(0) > 0)
    def _():
        gain_grad[...] += sums


def row_specs(tile, width):
    return (
        pl.BlockSpec(memory_space=pltpu.SMEM),
        pl.BlockSpec((tile, width), lambda i: (i, 0)),
        pl.BlockSpec((tile, 1), lambda i: (i, 0)),
        pl.BlockSpec((1, width), lambda i: (0, 0)),
    )


def middle_back(order, middle, scale, gain, cot, branches, backs, deps):
    rows, width = middle.shape
    tile = 128
    smem, row, column, single = row_specs(tile, width)
    count = len(branches)

    def kernel(*refs):
        middle_kernel(*refs[: 5 + 2 * count], *refs[5 + 2 * count + len(deps) :])

    return pl.pallas_call(
        kernel,
        grid=(rows // tile,),
        out_shape=(
            jax.ShapeDtypeStruct((rows, width), BF),
            jax.ShapeDtypeStruct((rows, width), F32),
            jax.ShapeDtypeStruct((rows, width), BF),
            jax.ShapeDtypeStruct((1, width), F32),
        ),
        in_specs=[smem, row, column, single, row] + [row] * (2 * count) + [ANY] * len(deps),
        out_specs=(row, row, row, single),
        compiler_params=params(),
        cost_estimate=pl.CostEstimate(
            flops=30 * rows * width, bytes_accessed=(14 + 8 * count) * rows * width, transcendentals=0
        ),
        name="middle_back",
    )(order, middle, scale, gain, cot, *branches, *backs, *deps)


def input_kernel(order, values, scale, gain, carried, upstream, out, gain_grad):
    norm_back(
        values[...].astype(F32), scale[...], gain, upstream[...], carried[...], out, gain_grad, order
    )


def input_back(order, values, scale, gain, carried, upstream):
    rows, width = values.shape
    tile = 128
    smem, row, column, single = row_specs(tile, width)
    return pl.pallas_call(
        input_kernel,
        grid=(rows // tile,),
        out_shape=(
            jax.ShapeDtypeStruct((rows, width), F32),
            jax.ShapeDtypeStruct((1, width), F32),
        ),
        in_specs=[smem, row, column, single, row, row],
        out_specs=(row, single),
        compiler_params=params(),
        cost_estimate=pl.CostEstimate(
            flops=20 * rows * width, bytes_accessed=14 * rows * width, transcendentals=0
        ),
        name="input_back",
    )(order, values, scale, gain, carried, upstream)


def mixer_grad_kernel(ht, dt, pa, pb, ya, yb, *rest):
    ga, gb = rest[-2:]
    step = pl.program_id(0)

    @pl.when(step < 3)
    def _():
        ga[0] = nn(ht[...], pa[0]).astype(BF)
        gb[0] = nn(ht[...], pb[0]).astype(BF)

    @pl.when(step == 3)
    def _():
        ga[0] = nn(dt[...], ya[...]).astype(BF)
        gb[0] = nn(dt[...], yb[...]).astype(BF)


def mixer_grad(ht, dt, proj_grad, gated, first, second, deps):
    width, rows = ht.shape
    cols = gated.shape[1] // 4

    def column(block):
        return pl.BlockSpec((1, rows, cols), lambda k: (jnp.minimum(k, 2), 0, block))

    def gated_column(block):
        return pl.BlockSpec((rows, cols), lambda k: (0, block))

    out = pl.BlockSpec((1, width, cols), lambda k: (k, 0, 0))
    grad = jax.ShapeDtypeStruct((4, width, cols), BF)
    return pl.pallas_call(
        mixer_grad_kernel,
        grid=(4,),
        out_shape=(grad, grad),
        in_specs=[
            whole((width, rows)),
            whole((width, rows)),
            column(first),
            column(second),
            gated_column(first),
            gated_column(second),
        ]
        + [ANY] * len(deps),
        out_specs=(out, out),
        compiler_params=params(),
        cost_estimate=pl.CostEstimate(
            flops=16 * rows * width * cols,
            bytes_accessed=4 * rows * width + 16 * width * cols + 16 * rows * cols,
            transcendentals=0,
        ),
        name="mixer_grad",
    )(ht, dt, proj_grad, proj_grad, gated, gated, *deps)


def update_kernel(*refs):
    count = (len(refs) - 12)
    totals, rest = refs[:count], refs[count:]
    wide, tall, wide_new, tall_new = rest[:3], rest[3:6], rest[6:9], rest[9:]
    for i, total in enumerate(totals):

        @pl.when(pl.program_id(0) == i)
        def _():
            last = total.shape[0] - 1
            new = adamw(wide[0][...], total[:last], wide[1][...], wide[2][...], RATE_MATRIX, DECAY)
            for ref, value in zip(wide_new, new):
                ref[...] = value
            grad = jnp.transpose(total[last])
            new = adamw(tall[0][...], grad, tall[1][...], tall[2][...], RATE_MATRIX, DECAY)
            for ref, value in zip(tall_new, new):
                ref[...] = value


def update(totals, wide, tall):
    if (wide[0].shape[2] // len(totals)) % 128:
        totals = [jnp.concatenate(totals, 2)]
    count = len(totals)
    planes, deep, cols = wide[0].shape
    part = cols // count
    wide_spec = pl.BlockSpec((planes, deep, part), lambda i: (0, 0, i))
    tall_spec = pl.BlockSpec((part, deep), lambda i: (i, 0))
    return pl.pallas_call(
        update_kernel,
        grid=(count,),
        out_shape=tuple(jax.ShapeDtypeStruct(a.shape, F32) for a in wide + tall),
        in_specs=[whole(total.shape) for total in totals] + [wide_spec] * 3 + [tall_spec] * 3,
        out_specs=(wide_spec,) * 3 + (tall_spec,) * 3,
        compiler_params=params(),
        cost_estimate=pl.CostEstimate(
            flops=20 * (planes + 1) * deep * cols,
            bytes_accessed=28 * (planes + 1) * deep * cols,
            transcendentals=(planes + 1) * deep * cols,
        ),
        name="update",
    )(*totals, *wide, *tall)


def local(
    tokens,
    segments,
    cotangent,
    mixer_in,
    mixer_out,
    gate_up,
    down_proj,
    norm_gains,
    conv_kernel,
    first_mixer_in,
    second_mixer_in,
    first_mixer_out,
    second_mixer_out,
    first_gate_up,
    second_gate_up,
    first_down_proj,
    second_down_proj,
    first_norm_gains,
    second_norm_gains,
    first_conv_kernel,
    second_conv_kernel,
):
    dp_size, t_size = lax.axis_size("dp"), lax.axis_size("tensor")
    dp_index, t_index = lax.axis_index("dp"), lax.axis_index("tensor")
    rows, length = tokens.shape[0], segments.shape[1]
    order = dp_index ^ jnp.array([rotate_left(j, dp_size) for j in range(dp_size)], jnp.int32)

    before = lax.ppermute(
        tokens[rows - HALO :], "tensor", [(i, i + 1) for i in range(t_size - 1)]
    )
    ffn_cols = gate_up.shape[2] // PARTS
    shards = [jnp.concatenate([mixer_in.astype(BF), mixer_out.T.astype(BF)[None]], 0)]
    for i in range(PARTS):
        cols = slice(i * ffn_cols, (i + 1) * ffn_cols)
        shards.append(
            jnp.concatenate([gate_up[:, :, cols].astype(BF), down_proj[cols].T.astype(BF)[None]], 0)
        )

    small = jnp.concatenate([norm_gains, conv_kernel], 0)[:, None, :]
    for axis, size_axis in (("tensor", t_size), ("dp", dp_size)):
        for i in range(size_axis.bit_length() - 1):
            small = jnp.concatenate([small, swap(small, axis, 1 << i)], 1)
    small = small.reshape(small.shape[0], dp_size, t_size, small.shape[2])
    for axis, index, size_axis in ((1, dp_index, dp_size), (2, t_index, t_size)):
        for i in range(size_axis.bit_length() - 1):
            shape = small.shape
            split = small.reshape(shape[:axis] + (size_axis >> (i + 1), 2, 1 << i) + shape[axis + 1 :])
            flipped = jnp.flip(split, axis + 1)
            small = jnp.where((index >> i) & 1 == 1, flipped, split).reshape(shape)
    small = small.reshape(small.shape[0], -1)
    wide = small.shape[1] // dp_size
    gains = jnp.concatenate(
        [lax.dynamic_slice_in_dim(small[:2], order[j] * wide, wide, 1) for j in range(dp_size)], 1
    )
    channels = small.shape[1] // t_size
    codes = block_codes(t_size)
    kernel = jnp.concatenate(
        [
            lax.dynamic_slice_in_dim(small[2:], (t_index ^ code) * channels, channels, 1)
            for code in codes
        ],
        1,
    )

    masks = []
    for mask in lag_masks(segments.reshape(-1), length):
        padded = jnp.concatenate([mask, jnp.zeros((HALO, 1), F32)], 0)
        masks.append(lax.dynamic_slice_in_dim(padded, t_index * rows, rows + HALO, 0))

    x_ext, cot = arrange(order, tokens, before, cotangent)
    extended = x_ext.astype(F32)
    scale_ext = rms_scale(extended)
    normed_ext = (extended * scale_ext * gains[0]).astype(BF)
    values, scale_one, normed_one = extended[HALO:], scale_ext[HALO:], normed_ext[HALO:]
    kept = {}

    def mixer_forward(wm):
        wm_all = jnp.concatenate(wm, 2)
        win_all, wout_all = wm_all[:3], wm_all[3]
        projected = mm("td,kdc->ktc", normed_ext, win_all)
        part_b, part_c, part_x = projected[0], projected[1][HALO:], projected[2]
        product_ext = part_b * part_x
        part_b, part_x = part_b[HALO:], part_x[HALO:]
        product = product_ext[HALO:]
        convolved = kernel[0] * product
        for shift in range(1, KW):
            convolved = convolved + kernel[shift] * masks[shift - 1][:rows] * shift_rows(
                product_ext, HALO - shift, rows
            )
        gated = (part_c * convolved).astype(BF)
        middle = values + mm("tc,dc->td", gated, wout_all)
        scale_two = rms_scale(middle)
        normed_two = (middle * scale_two * gains[1]).astype(BF)
        kept.update(locals())
        return normed_two

    _, *wf = gather_weights(shards, 1, 2, mixer_forward)
    win_all, wout_all, part_b, part_c, part_x = [
        kept[name] for name in ("win_all", "wout_all", "part_b", "part_c", "part_x")
    ]
    product_ext, product, convolved, gated, middle, scale_two, normed_two = [
        kept[name]
        for name in ("product_ext", "product", "convolved", "gated", "middle", "scale_two", "normed_two")
    ]

    norm_t, cot_t = normed_two.T, cot.T
    sums, grads = [], []
    near_in, far_in, corner, sides = [], [], [], []
    for i in range(PARTS):
        near, near_core, far, far_core = wf[i]
        deps = []
        if i >= 1:
            deps.append(near_in[i - 1])
        if i >= 2:
            deps += corner[i - 2]
        g_near, g_near_core, *sums = ffn(normed_two, norm_t, cot, cot_t, near, near_core, sums, deps)
        near_in.append(swap(g_near_core, "tensor", 1))
        if i >= 2:
            sides.append(scatter_sides(*grads[i - 2][:1], near_in[i - 2], grads[i - 2][1], far_in[i - 2], *corner[i - 2], 1))
        deps = [far_in[i - 1]] if i >= 1 else []
        g_far, g_far_core, *sums = ffn(normed_two, norm_t, cot, cot_t, far, far_core, sums, deps)
        far_in.append(swap(g_far_core, "tensor", 1))
        grads.append((g_near, g_far))
        if i >= 1:
            corner.append(scatter_corner(grads[i - 1][1], far_in[i - 1], 1))

    def finish_sides(i):
        return scatter_sides(grads[i][0], near_in[i], grads[i][1], far_in[i], *corner[i], 1)

    block_out, middle_grad, mixed_grad, gain_two_grad = middle_back(
        order, middle, scale_two, gains[1:2], cot, sums[:1], sums[1:], [near_in[-1], *corner[-1]]
    )
    corner.append(scatter_corner(grads[-1][1], far_in[-1], 1))
    while len(sides) < PARTS - 1:
        sides.append(finish_sides(len(sides)))

    gated_grad = mm("td,dc->tc", mixed_grad, wout_all)
    conv_grad = gated_grad * part_c
    after_rel = lax.ppermute(
        conv_grad[:8], "tensor", [(i + 1, i) for i in range(t_size - 1)]
    )
    after = jnp.concatenate(
        [
            lax.dynamic_slice_in_dim(
                after_rel,
                block_place(code ^ t_index ^ (t_index + 1), t_size) % t_size * channels,
                channels,
                1,
            )
            for code in codes
        ],
        1,
    )
    c_grad = gated_grad * convolved
    conv_ext = jnp.concatenate([conv_grad, after], 0)
    kernel_rows = [jnp.sum(conv_grad * product, axis=0)]
    product_grad = kernel[0] * conv_grad
    for shift in range(1, KW):
        masked = masks[shift - 1][: rows + 8] * conv_ext
        kernel_rows.append(
            jnp.sum(masked[:rows] * shift_rows(product_ext, HALO - shift, rows), axis=0)
        )
        product_grad = product_grad + kernel[shift] * shift_rows(masked, shift, rows)
    proj_grad = jnp.stack([product_grad * part_x, c_grad, product_grad * part_b], 0).astype(BF)
    one_t, mixed_t = normed_one.T, mixed_grad.T
    m_near_core, m_far_core = mixer_grad(
        one_t, mixed_t, proj_grad, gated, 1, 3, [*sides[0], *corner[-1]]
    )
    m_far_in, m_near_in = swap(m_far_core, "tensor", 1), swap(m_near_core, "tensor", 1)
    sides.append(finish_sides(PARTS - 1))
    m_near, m_far = mixer_grad(one_t, mixed_t, proj_grad, gated, 0, 2, [])
    m_corner = scatter_corner(m_far, m_far_in, 1)
    normed_one_grad = mm("ktc,kdc->td", ordered(proj_grad, m_far), win_all)
    grad_input, gain_one_grad = input_back(
        order, x_ext[HALO:], scale_one, gains[:1], middle_grad, normed_one_grad
    )
    m_sides = scatter_sides(m_near, m_near_in, m_far, m_far_in, *m_corner, 1)

    gain_rel = jnp.concatenate([gain_one_grad, gain_two_grad], 0)
    kernel_rel = jnp.stack(kernel_rows, 0)
    gain_sums = jnp.concatenate(
        [
            lax.dynamic_slice_in_dim(gain_rel, rotate_right(dp_index ^ q, dp_size) * wide, wide, 1)
            for q in range(dp_size)
        ],
        1,
    )
    kernel_sums = jnp.concatenate(
        [
            lax.dynamic_slice_in_dim(
                kernel_rel, block_place(t_index ^ q, t_size) * channels, channels, 1
            )
            for q in range(t_size)
        ],
        1,
    )
    sums = ordered(jnp.concatenate([gain_sums, kernel_sums], 0), *m_corner)
    for axis, size_axis in (("tensor", t_size), ("dp", dp_size)):
        for i in range(size_axis.bit_length() - 1):
            sums = sums + swap(sums, axis, 1 << i)
    own_width = norm_gains.shape[1]
    own = lax.dynamic_slice_in_dim(sums, (dp_index * t_size + t_index) * own_width, own_width, 1)

    totals = [
        scatter_rest(grads[i][0], near_in[i], *sides[i], 1, 2) for i in range(PARTS)
    ]
    ffn_new = update(
        totals, (gate_up, first_gate_up, second_gate_up), (down_proj, first_down_proj, second_down_proj)
    )
    total = scatter_rest(m_near, m_near_in, *m_sides, 1, 2)
    mix_new = update(
        [total], (mixer_in, first_mixer_in, second_mixer_in), (mixer_out, first_mixer_out, second_mixer_out)
    )
    gains_new = adamw(norm_gains, own[:2], first_norm_gains, second_norm_gains, RATE_SMALL, 0.0)
    kernel_new = adamw(conv_kernel, own[2:], first_conv_kernel, second_conv_kernel, RATE_SMALL, DECAY)
    block_out, grad_input = to_natural(block_out, order), to_natural(grad_input, order)
    return (block_out, grad_input, *mix_new, *ffn_new, *gains_new, *kernel_new)


def solution(mesh):
    rows = P(("dp", "tensor"), None)
    in_w, out_w, small = P(None, "dp", "tensor"), P("tensor", "dp"), P(None, ("dp", "tensor"))
    return jax.shard_map(
        local,
        mesh=mesh,
        in_specs=(
            (rows, P("dp", None), rows, in_w, out_w, in_w, out_w, small, small)
            + (in_w,) * 2
            + (out_w,) * 2
            + (in_w,) * 2
            + (out_w,) * 2
            + (small,) * 4
        ),
        out_specs=(rows, rows)
        + (in_w,) * 3
        + (out_w,) * 3
        + (in_w,) * 3
        + (out_w,) * 3
        + (small,) * 6,
        check_vma=False,
    )
```

```python
import functools

import jax
import jax.numpy as jnp
from jax import lax
from jax.experimental import pallas as pl
from jax.experimental.pallas import tpu as pltpu
from jax.sharding import PartitionSpec as P

KW = 3
STEP = 10
HALO = 16
PARTS = 3

EPS_NORM = 1e-05
EPS_ADAM = 1e-08
BETA_FIRST = 0.9
BETA_SECOND = 0.95
RATE_MATRIX = 0.05
RATE_SMALL = 0.5
DECAY = 0.1

BF = jnp.bfloat16
F32 = jnp.float32


def swap(values, axis, bit):
    size = lax.axis_size(axis)
    return lax.ppermute(values, axis, [(i, i ^ bit) for i in range(size)])


def halves(values, axis):
    size = values.shape[axis] // 2
    return (
        lax.slice_in_dim(values, 0, size, axis=axis),
        lax.slice_in_dim(values, size, 2 * size, axis=axis),
    )


def low_bits():
    return (
        [2 << i for i in range((lax.axis_size("dp") // 2).bit_length() - 1)],
        [4 << i for i in range((lax.axis_size("tensor") // 4).bit_length() - 1)],
    )


def ordered(values, others):
    values = list(values)
    return list(lax.optimization_barrier((*values, *others)))[: len(values)]


def phase(others, sends):
    values = ordered([send[0] for send in sends], others)
    return [swap(value, axis, bit) for value, (_, axis, bit) in zip(values, sends)]


def join(parts, axis):
    return jnp.concatenate(parts, axis)


def fold(parts, wide):
    return functools.reduce(jnp.add, [halves(part, wide)[1].astype(F32) for part in parts]).astype(BF)


def plus(left, right):
    return (left.astype(F32) + right.astype(F32)).astype(BF)


def corner_sends(far, far_in, wide):
    far_high, far_in_high = halves(far, wide)[1], halves(far_in, wide)[1]
    first, second = [plus(a, b) for a, b in zip(halves(far_high, wide), halves(far_in_high, wide))]
    return [(first, "dp", 1), (second, "tensor", 2)]


def side_sends(near, near_in, far, far_in, corner, wide):
    to_x, to_y = corner
    far_low, far_in_low = halves(far, wide)[0], halves(far_in, wide)[0]
    near_high, near_in_high = halves(near, wide)[1], halves(near_in, wide)[1]
    far_parts = [a.astype(F32) + b.astype(F32) for a, b in zip(halves(far_low, wide), halves(far_in_low, wide))]
    near_parts = [
        a.astype(F32) + b.astype(F32) for a, b in zip(halves(near_high, wide), halves(near_in_high, wide))
    ]
    by_y = join([(far_parts[0] + to_x.astype(F32)).astype(BF), far_parts[1].astype(BF)], wide)
    by_x = join([near_parts[0].astype(BF), (near_parts[1] + to_y.astype(F32)).astype(BF)], wide)
    return [(by_x, "dp", 1), (by_y, "tensor", 2)]


def rotate_left(values, count):
    bits = count.bit_length() - 1
    return ((values << 1) | (values >> (bits - 1))) & (count - 1)


def rotate_right(values, count):
    bits = count.bit_length() - 1
    return ((values & 1) << (bits - 1)) | (values >> 1)


def block_codes(count):
    return [base ^ (e << 2) for base in (0, 1, 2, 3) for e in range(count // 4)]


def block_place(code, count):
    return (code & 3) * (count // 4) + (code >> 2)


def shift_rows(values, start, rows):
    return lax.slice_in_dim(values, start, start + rows, axis=0)


def lag_masks(seg_flat, length):
    positions = jnp.arange(seg_flat.shape[0], dtype=jnp.int32) % length
    masks = []
    for shift in range(1, KW):
        before = jnp.concatenate([jnp.zeros((shift,), seg_flat.dtype), seg_flat[:-shift]], 0)
        same = (positions >= shift) & (seg_flat == before)
        masks.append(jnp.where(same, 1.0, 0.0).astype(F32)[:, None])
    return masks


def rms_scale(values):
    return lax.rsqrt(jnp.mean(values * values, axis=-1, keepdims=True) + EPS_NORM)


def adamw(param, grad, first, second, rate, decay):
    first_new = BETA_FIRST * first + (1.0 - BETA_FIRST) * grad
    second_new = BETA_SECOND * second + (1.0 - BETA_SECOND) * grad * grad
    first_hat = first_new / (1.0 - BETA_FIRST**STEP)
    second_hat = second_new / (1.0 - BETA_SECOND**STEP)
    return (
        param - rate * (first_hat / (jnp.sqrt(second_hat) + EPS_ADAM) + decay * param),
        first_new,
        second_new,
    )


def mm(spec, left, right, out=F32):
    return jnp.einsum(spec, left, right, preferred_element_type=F32).astype(out)


ANY = pl.BlockSpec(memory_space=pl.ANY)
LIMIT = 26 * 1024 * 1024


def params(count=1):
    return pltpu.CompilerParams(
        vmem_limit_bytes=LIMIT, dimension_semantics=("arbitrary",) * count
    )


def whole(shape):
    return pl.BlockSpec(shape, lambda *_: (0,) * len(shape), pipeline_mode=pl.Buffered(1))


def arrange_kernel(order, tokens, before, cot, x_out, cot_out):
    count = order.shape[0]
    width = tokens.shape[1] // count
    for j in range(count):
        spot = pl.ds(pl.multiple_of(order[j] * width, width), width)
        own = pl.ds(j * width, width)
        x_out[:HALO, own] = before[:, spot]
        x_out[HALO:, own] = tokens[:, spot]
        cot_out[:, own] = cot[:, spot]


def pick_blocks(values, places):
    count = places.shape[0]
    width = values.shape[1] // count
    return jnp.concatenate(
        [lax.dynamic_slice_in_dim(values, places[j] * width, width, 1) for j in range(count)], 1
    )


def narrow(order, width):
    return (width // order.shape[0]) % 128 != 0


def to_natural(values, order):
    if not narrow(order, values.shape[1]):
        return values
    return pick_blocks(values, jnp.argsort(order))


def arrange(order, tokens, before, cot):
    rows, width = tokens.shape
    if narrow(order, width):
        extended = jnp.concatenate([before, tokens], 0)
        return pick_blocks(extended, order), pick_blocks(cot, order)
    vmem = pl.BlockSpec(memory_space=pltpu.VMEM)
    return pl.pallas_call(
        arrange_kernel,
        out_shape=(
            jax.ShapeDtypeStruct((rows + HALO, width), BF),
            jax.ShapeDtypeStruct((rows, width), BF),
        ),
        in_specs=[pl.BlockSpec(memory_space=pltpu.SMEM), vmem, vmem, vmem],
        out_specs=(vmem, vmem),
        compiler_params=pltpu.CompilerParams(vmem_limit_bytes=LIMIT),
        name="arrange",
    )(order, tokens, before, cot)


def nt(left, right):
    return lax.dot_general(left, right, (((1,), (1,)), ((), ())), preferred_element_type=F32)


def nn(left, right):
    return jnp.dot(left, right, preferred_element_type=F32)


def ffn_kernel(first, h, ht, c, ct, wa, wb, *rest):
    ga, gb, branch, back, act, dgate, dup = rest[-7:]
    half = wa.shape[2]
    wg, wu, wd = [jnp.concatenate([wa[k], wb[k]], 1) for k in range(3)]
    rows = h.shape[0]
    tall = rows // 2
    if first:

        @pl.when(pl.program_id(0) == 0)
        def _():
            branch[...] = jnp.zeros_like(branch)
            back[...] = jnp.zeros_like(back)

    for start in range(0, rows, tall):
        span = pl.ds(start, tall)
        gate = nn(h[span, :], wg)
        up = nn(h[span, :], wu)
        da = nn(c[span, :], wd)
        sigma = 1.0 / (1.0 + jnp.exp(-gate))
        silu = gate * sigma
        act[span, :] = (silu * up).astype(BF)
        dup[span, :] = (da * silu).astype(BF)
        dgate[span, :] = (da * up * (sigma + silu * (1.0 - sigma))).astype(BF)
    for k, (left, right) in enumerate(((ht, dgate), (ht, dup), (ct, act))):
        grad = nn(left[...], right[...]).astype(BF)
        ga[k] = grad[:, :half]
        gb[k] = grad[:, half:]
    branch[...] += nt(act[...], wd)
    back[...] += nt(dgate[...], wg) + nt(dup[...], wu)


def ffn(h, ht, c, ct, wa, wb, sums, deps):
    rows, width = h.shape
    cols = wa.shape[2]
    tile = 128
    block = pl.BlockSpec((3, width, tile), lambda j: (0, 0, j))
    vmem = pl.BlockSpec(memory_space=pltpu.VMEM)
    grad = jax.ShapeDtypeStruct(wa.shape, BF)
    part = jax.ShapeDtypeStruct((rows, width), F32)
    return pl.pallas_call(
        functools.partial(ffn_kernel, not sums),
        grid=(cols // tile,),
        out_shape=(grad, grad, part, part),
        in_specs=[vmem] * 4 + [block, block] + [vmem] * len(sums) + [ANY] * len(deps),
        out_specs=(block, block, vmem, vmem),
        input_output_aliases={6: 2, 7: 3} if sums else {},
        scratch_shapes=[pltpu.VMEM((rows, 2 * tile), BF)] * 3,
        compiler_params=params(),
        cost_estimate=pl.CostEstimate(
            flops=36 * rows * width * cols,
            bytes_accessed=24 * width * cols,
            transcendentals=2 * rows * cols,
        ),
        name="ffn",
    )(h, ht, c, ct, wa, wb, *sums, *deps)


def middle_kernel(order, middle, scale, gain, cot, *rest):
    block_out, grad, grad_low, gain_grad = rest[-4:]
    half = (len(rest) - 4) // 2
    branches, backs = rest[:half], rest[half : 2 * half]
    x2, r2, up = middle[...], scale[...], backs[0][...].astype(F32)
    for ref in backs[1:]:
        up = up + ref[...].astype(F32)
    total = x2
    for ref in branches:
        total = total + ref[...].astype(F32)
    store_natural(order, block_out, total.astype(BF))
    norm_back(x2, r2, gain, up, cot[...].astype(F32), grad, gain_grad)
    grad_low[...] = grad[...].astype(BF)


def store_natural(order, out, total):
    count = order.shape[0]
    if narrow(order, total.shape[1]):
        out[...] = total
        return
    width = total.shape[1] // count
    for j in range(count):
        spot = pl.ds(pl.multiple_of(order[j] * width, width), width)
        out[:, spot] = total[:, j * width : (j + 1) * width]


def norm_back(values, scale, gain, upstream, carried, out, gain_grad, order=None):
    scaled = upstream * gain[...]
    mean = jnp.mean(scaled * values, axis=-1, keepdims=True)
    total = carried + scale * scaled - values * (scale * scale * scale * mean)
    if order is None:
        out[...] = total
    else:
        store_natural(order, out, total)
    sums = jnp.sum(upstream * values * scale, axis=0, keepdims=True)

    @pl.when(pl.program_id(0) == 0)
    def _():
        gain_grad[...] = sums

    @pl.when(pl.program_id(0) > 0)
    def _():
        gain_grad[...] += sums


def row_specs(tile, width):
    return (
        pl.BlockSpec(memory_space=pltpu.SMEM),
        pl.BlockSpec((tile, width), lambda i: (i, 0)),
        pl.BlockSpec((tile, 1), lambda i: (i, 0)),
        pl.BlockSpec((1, width), lambda i: (0, 0)),
    )


def middle_back(order, middle, scale, gain, cot, branches, backs, deps):
    rows, width = middle.shape
    tile = 128
    smem, row, column, single = row_specs(tile, width)
    count = len(branches)

    def kernel(*refs):
        middle_kernel(*refs[: 5 + 2 * count], *refs[5 + 2 * count + len(deps) :])

    return pl.pallas_call(
        kernel,
        grid=(rows // tile,),
        out_shape=(
            jax.ShapeDtypeStruct((rows, width), BF),
            jax.ShapeDtypeStruct((rows, width), F32),
            jax.ShapeDtypeStruct((rows, width), BF),
            jax.ShapeDtypeStruct((1, width), F32),
        ),
        in_specs=[smem, row, column, single, row] + [row] * (2 * count) + [ANY] * len(deps),
        out_specs=(row, row, row, single),
        compiler_params=params(),
        cost_estimate=pl.CostEstimate(
            flops=30 * rows * width, bytes_accessed=(14 + 8 * count) * rows * width, transcendentals=0
        ),
        name="middle_back",
    )(order, middle, scale, gain, cot, *branches, *backs, *deps)


def input_kernel(order, values, scale, gain, carried, upstream, out, gain_grad):
    norm_back(
        values[...].astype(F32), scale[...], gain, upstream[...], carried[...], out, gain_grad, order
    )


def input_back(order, values, scale, gain, carried, upstream):
    rows, width = values.shape
    tile = 128
    smem, row, column, single = row_specs(tile, width)
    return pl.pallas_call(
        input_kernel,
        grid=(rows // tile,),
        out_shape=(
            jax.ShapeDtypeStruct((rows, width), F32),
            jax.ShapeDtypeStruct((1, width), F32),
        ),
        in_specs=[smem, row, column, single, row, row],
        out_specs=(row, single),
        compiler_params=params(),
        cost_estimate=pl.CostEstimate(
            flops=20 * rows * width, bytes_accessed=14 * rows * width, transcendentals=0
        ),
        name="input_back",
    )(order, values, scale, gain, carried, upstream)


def mixer_grad_kernel(ht, dt, pa, pb, ya, yb, *rest):
    ga, gb = rest[-2:]
    step = pl.program_id(0)

    @pl.when(step < 3)
    def _():
        ga[0] = nn(ht[...], pa[0]).astype(BF)
        gb[0] = nn(ht[...], pb[0]).astype(BF)

    @pl.when(step == 3)
    def _():
        ga[0] = nn(dt[...], ya[...]).astype(BF)
        gb[0] = nn(dt[...], yb[...]).astype(BF)


def mixer_grad(ht, dt, proj_grad, gated, first, second, deps):
    width, rows = ht.shape
    cols = gated.shape[1] // 4

    def column(block):
        return pl.BlockSpec((1, rows, cols), lambda k: (jnp.minimum(k, 2), 0, block))

    def gated_column(block):
        return pl.BlockSpec((rows, cols), lambda k: (0, block))

    out = pl.BlockSpec((1, width, cols), lambda k: (k, 0, 0))
    grad = jax.ShapeDtypeStruct((4, width, cols), BF)
    return pl.pallas_call(
        mixer_grad_kernel,
        grid=(4,),
        out_shape=(grad, grad),
        in_specs=[
            whole((width, rows)),
            whole((width, rows)),
            column(first),
            column(second),
            gated_column(first),
            gated_column(second),
        ]
        + [ANY] * len(deps),
        out_specs=(out, out),
        compiler_params=params(),
        cost_estimate=pl.CostEstimate(
            flops=16 * rows * width * cols,
            bytes_accessed=4 * rows * width + 16 * width * cols + 16 * rows * cols,
            transcendentals=0,
        ),
        name="mixer_grad",
    )(ht, dt, proj_grad, proj_grad, gated, gated, *deps)


def update_kernel(*refs):
    count = (len(refs) - 12)
    totals, rest = refs[:count], refs[count:]
    wide, tall, wide_new, tall_new = rest[:3], rest[3:6], rest[6:9], rest[9:]
    for i, total in enumerate(totals):

        @pl.when(pl.program_id(0) == i)
        def _():
            last = total.shape[0] - 1
            new = adamw(wide[0][...], total[:last], wide[1][...], wide[2][...], RATE_MATRIX, DECAY)
            for ref, value in zip(wide_new, new):
                ref[...] = value
            grad = jnp.transpose(total[last])
            new = adamw(tall[0][...], grad, tall[1][...], tall[2][...], RATE_MATRIX, DECAY)
            for ref, value in zip(tall_new, new):
                ref[...] = value


def update(totals, wide, tall):
    if (wide[0].shape[2] // len(totals)) % 128:
        totals = [jnp.concatenate(totals, 2)]
    count = len(totals)
    planes, deep, cols = wide[0].shape
    part = cols // count
    wide_spec = pl.BlockSpec((planes, deep, part), lambda i: (0, 0, i))
    tall_spec = pl.BlockSpec((part, deep), lambda i: (i, 0))
    return pl.pallas_call(
        update_kernel,
        grid=(count,),
        out_shape=tuple(jax.ShapeDtypeStruct(a.shape, F32) for a in wide + tall),
        in_specs=[whole(total.shape) for total in totals] + [wide_spec] * 3 + [tall_spec] * 3,
        out_specs=(wide_spec,) * 3 + (tall_spec,) * 3,
        compiler_params=params(),
        cost_estimate=pl.CostEstimate(
            flops=20 * (planes + 1) * deep * cols,
            bytes_accessed=28 * (planes + 1) * deep * cols,
            transcendentals=(planes + 1) * deep * cols,
        ),
        name="update",
    )(*totals, *wide, *tall)


def local(
    tokens,
    segments,
    cotangent,
    mixer_in,
    mixer_out,
    gate_up,
    down_proj,
    norm_gains,
    conv_kernel,
    first_mixer_in,
    second_mixer_in,
    first_mixer_out,
    second_mixer_out,
    first_gate_up,
    second_gate_up,
    first_down_proj,
    second_down_proj,
    first_norm_gains,
    second_norm_gains,
    first_conv_kernel,
    second_conv_kernel,
):
    dp_size, t_size = lax.axis_size("dp"), lax.axis_size("tensor")
    dp_index, t_index = lax.axis_index("dp"), lax.axis_index("tensor")
    rows, length = tokens.shape[0], segments.shape[1]
    order = dp_index ^ jnp.array([rotate_left(j, dp_size) for j in range(dp_size)], jnp.int32)

    z_bits, t_bits = low_bits()
    wide, cut = 1, 2
    ffn_cols = gate_up.shape[2] // PARTS
    own = [join([mixer_in.astype(BF), mixer_out.T.astype(BF)[None]], 0)]
    for i in range(PARTS):
        cols = slice(i * ffn_cols, (i + 1) * ffn_cols)
        own.append(join([gate_up[:, :, cols].astype(BF), down_proj[cols].T.astype(BF)[None]], 0))

    def deepen(places, others, axis="dp", bit=None, along=wide):
        got = phase(others, [(own[i], axis, bit) for i in places])
        for i, part in zip(places, got):
            own[i] = join([own[i], part], along)
        return got

    def near_block(i, side):
        return join([own[i], side[0]], wide)

    def corner_of(side):
        by_x, by_y = side
        return [(halves(by_y, wide)[0], "dp", 1), (halves(by_x, wide)[1], "tensor", 2)]

    def far_block(side, corner):
        return join([side[1], *corner], wide)

    def sides_of(i):
        return [(own[i], "dp", 1), (own[i], "tensor", 2)]

    def other_core(value):
        return swap(value, "tensor", 1)

    small = jnp.concatenate([norm_gains, conv_kernel], 0)[:, None, :]
    before = lax.ppermute(
        tokens[rows - HALO :], "tensor", [(i, i + 1) for i in range(t_size - 1)]
    )
    small_t = phase([], [(small, "tensor", code) for code in range(1, t_size)])
    last = []
    for bit in z_bits[:-1]:
        last = deepen([0, 1], last, bit=bit)
    small = join([small, *small_t], 1)
    small_x = phase([*last, small], [(small, "dp", 1)])
    later = last
    last = deepen([0], last, bit=z_bits[-1])
    for bit in z_bits[:-1]:
        later = deepen(range(2, PARTS + 1), later, bit=bit)
    for bit in t_bits:
        last = deepen([0], last, "tensor", bit, cut)
    small = join([small, *small_x], 1)
    small_z = phase([*last, small], [(small, "dp", code) for code in range(2, dp_size, 2)])
    side = {0: None}
    side[0] = phase([*last, *later], sides_of(0))
    last = deepen([1], [*last, *later], bit=z_bits[-1])
    for bit in t_bits:
        last = deepen(range(1, PARTS + 1), last, "tensor", bit, cut)
    small = join([small, *small_z], 1)

    small = small.reshape(small.shape[0], dp_size, t_size, small.shape[2])
    for axis, index, size_axis in ((1, dp_index, dp_size), (2, t_index, t_size)):
        for i in range(size_axis.bit_length() - 1):
            shape = small.shape
            split = small.reshape(shape[:axis] + (size_axis >> (i + 1), 2, 1 << i) + shape[axis + 1 :])
            flipped = jnp.flip(split, axis + 1)
            small = jnp.where((index >> i) & 1 == 1, flipped, split).reshape(shape)
    small = small.reshape(small.shape[0], -1)
    block = small.shape[1] // dp_size
    gains = jnp.concatenate(
        [lax.dynamic_slice_in_dim(small[:2], order[j] * block, block, 1) for j in range(dp_size)], 1
    )
    channels = small.shape[1] // t_size
    codes = block_codes(t_size)
    kernel = jnp.concatenate(
        [
            lax.dynamic_slice_in_dim(small[2:], (t_index ^ code) * channels, channels, 1)
            for code in codes
        ],
        1,
    )

    masks = []
    for mask in lag_masks(segments.reshape(-1), length):
        padded = jnp.concatenate([mask, jnp.zeros((HALO, 1), F32)], 0)
        masks.append(lax.dynamic_slice_in_dim(padded, t_index * rows, rows + HALO, 0))

    x_ext, cot = arrange(order, tokens, before, cotangent)
    extended = x_ext.astype(F32)
    scale_ext = rms_scale(extended)
    normed_ext = (extended * scale_ext * gains[0]).astype(BF)
    values, scale_one, normed_one = extended[HALO:], scale_ext[HALO:], normed_ext[HALO:]
    corner = {0: phase([*side[0], *last], corner_of(side[0]))}
    near = near_block(0, side[0])
    near_core = other_core(near)
    later = phase([*side[0], *last], [(own[2], "dp", z_bits[-1])])
    side[1] = phase(corner[0], sides_of(1))
    far = far_block(side[0], corner[0])
    wm = [near, near_core, far, other_core(far)]
    wm_all = jnp.concatenate(wm, 2)
    win_all, wout_all = wm_all[:3], wm_all[3]
    projected = mm("td,kdc->ktc", normed_ext, win_all)
    part_b, part_c, part_x = projected[0], projected[1][HALO:], projected[2]
    product_ext = part_b * part_x
    part_b, part_x = part_b[HALO:], part_x[HALO:]
    product = product_ext[HALO:]
    convolved = kernel[0] * product
    for shift in range(1, KW):
        convolved = convolved + kernel[shift] * masks[shift - 1][:rows] * shift_rows(
            product_ext, HALO - shift, rows
        )
    gated = (part_c * convolved).astype(BF)
    middle = values + mm("tc,dc->td", gated, wout_all)
    scale_two = rms_scale(middle)
    normed_two = (middle * scale_two * gains[1]).astype(BF)

    norm_t, cot_t = normed_two.T, cot.T
    sums = []
    grads, core_grads, near_in, far_in = {}, {}, {}, {}

    def run(weights, other):
        nonlocal sums
        grad, grad_core, *sums = ffn(normed_two, norm_t, cot, cot_t, weights, other, sums, [])
        return grad, grad_core

    *side[1], later = ordered([*side[1], *later], [normed_two])
    own[2] = join([own[2], later], wide)
    last = [own[2]]
    w_far = {}
    for i in range(1, PARTS + 1):
        sends = corner_of(side[i])
        if i < PARTS:
            sends += sides_of(i + 1)
        else:
            sends += corner_sends(grads[1][1], far_in[1], wide)
        if i + 2 <= PARTS:
            sends.append((own[i + 2], "dp", z_bits[-1]))
        if i > 2:
            last = [*last, near_in[i - 2]]
        got = phase(last, sends)
        near = near_block(i, side[i])
        near_core = other_core(near)
        corner[i] = got[:2]
        if i > 1:
            g_far, g_far_core = run(*w_far[i - 1])
            far_in[i - 1] = other_core(g_far_core)
            grads[i - 1] = (g_near, g_far)
            corner[i] = ordered(corner[i], [g_far])
        far = far_block(side[i], corner[i])
        w_far[i] = (far, other_core(far))
        (near,) = ordered([near], corner[i])
        g_near, g_near_core = run(near, near_core)
        near_in[i] = other_core(g_near_core)
        rest = ordered(got[2:], [g_near])
        last = [*corner[i], *rest]
        if i < PARTS:
            side[i + 1] = rest[:2]
        else:
            back_corner = {1: rest[:2]}
        if i + 2 <= PARTS:
            own[i + 2] = join([own[i + 2], rest[2]], wide)

    def back_sides(i):
        return side_sends(grads[i][0], near_in[i], grads[i][1], far_in[i], back_corner[i], wide)

    def back_corners(i):
        return corner_sends(grads[i][1], far_in[i], wide)

    got = phase([*last, near_in[PARTS - 1]], back_sides(1) + back_corners(2))
    g_far, g_far_core = run(*w_far[PARTS])
    far_in[PARTS] = other_core(g_far_core)
    grads[PARTS] = (g_near, g_far)
    block_out, middle_grad, mixed_grad, gain_two_grad = middle_back(
        order, middle, scale_two, gains[1:2], cot, sums[:1], sums[1:], []
    )
    back_side = {1: got[:2]}
    back_corner[2] = got[2:]

    terms = {}

    def last_terms(i):
        terms[i] = [halves(grads[i][0], wide)[0], halves(near_in[i], wide)[0], *back_side[i]]

    def fold_send(i, axis, bit, along):
        return (fold(terms[i], along), axis, bit)

    def folded(i, got, along):
        terms[i] = [halves(term, along)[0] for term in terms[i]] + [got]

    steps = [("tensor", bit, cut) for bit in reversed(t_bits)]
    steps += [("dp", bit, wide) for bit in reversed(z_bits)]

    def advance(work, others, extra=()):
        sends = [fold_send(i, *steps[step]) for i, step in work]
        got = phase(others, [*extra, *sends])
        for (i, step), value in zip(work, got[len(extra) :]):
            folded(i, value, steps[step][2])
        return got

    gated_grad = mm("td,dc->tc", mixed_grad, wout_all)
    conv_grad = gated_grad * part_c
    after_rel = lax.ppermute(
        conv_grad[:8], "tensor", [(i + 1, i) for i in range(t_size - 1)]
    )
    after = jnp.concatenate(
        [
            lax.dynamic_slice_in_dim(
                after_rel,
                block_place(code ^ t_index ^ (t_index + 1), t_size) % t_size * channels,
                channels,
                1,
            )
            for code in codes
        ],
        1,
    )
    c_grad = gated_grad * convolved
    conv_ext = jnp.concatenate([conv_grad, after], 0)
    kernel_rows = [jnp.sum(conv_grad * product, axis=0)]
    product_grad = kernel[0] * conv_grad
    for shift in range(1, KW):
        masked = masks[shift - 1][: rows + 8] * conv_ext
        kernel_rows.append(
            jnp.sum(masked[:rows] * shift_rows(product_ext, HALO - shift, rows), axis=0)
        )
        product_grad = product_grad + kernel[shift] * shift_rows(masked, shift, rows)
    proj_grad = jnp.stack([product_grad * part_x, c_grad, product_grad * part_b], 0).astype(BF)
    last_terms(1)
    (proj_grad,) = ordered([proj_grad], got)
    last = [*got, mixed_grad, near_in[PARTS]]
    extra = back_sides(2) + back_corners(3)
    for i in range(4, PARTS + 1):
        extra += back_corners(i)
    got = advance([(1, 0)], last, extra)
    back_side[2], back_corner[3] = got[:2], got[2:4]
    last_terms(2)
    last = got

    one_t, mixed_t = normed_one.T, mixed_grad.T
    m_near_core, m_far_core = mixer_grad(one_t, mixed_t, proj_grad, gated, 1, 3, [])
    far_in[0], near_in[0] = other_core(m_far_core), other_core(m_near_core)
    m_near, m_far = mixer_grad(one_t, mixed_t, proj_grad, gated, 0, 2, [])
    grads[0] = (m_near, m_far)
    got = advance([(1, 1), (2, 0)], [*last, m_far], back_sides(3))
    back_side[3] = got[:2]
    last_terms(3)
    back_corner[0] = phase([*last, m_far], back_corners(0))
    last = [*got, *back_corner[0]]

    (late,) = ordered([proj_grad], [m_far])
    normed_one_grad = mm("ktc,kdc->td", late, win_all)
    grad_input, gain_one_grad = input_back(
        order, x_ext[HALO:], scale_one, gains[:1], middle_grad, normed_one_grad
    )

    gain_rel = jnp.concatenate([gain_one_grad, gain_two_grad], 0)
    kernel_rel = jnp.stack(kernel_rows, 0)
    gain_sums = jnp.concatenate(
        [
            lax.dynamic_slice_in_dim(gain_rel, rotate_right(dp_index ^ q, dp_size) * block, block, 1)
            for q in range(dp_size)
        ],
        1,
    )
    kernel_sums = jnp.concatenate(
        [
            lax.dynamic_slice_in_dim(
                kernel_rel, block_place(t_index ^ q, t_size) * channels, channels, 1
            )
            for q in range(t_size)
        ],
        1,
    )
    total_small = jnp.concatenate([gain_sums, kernel_sums], 0)

    def small_step(value, others, axis, codes):
        return functools.reduce(jnp.add, [value, *phase(others, [(value, axis, code) for code in codes])])

    stages = len(steps)
    total_small = small_step(total_small, last, "tensor", range(1, t_size))
    work = [(1, 2), (2, 1), (3, 0)]
    got = advance([(i, step) for i, step in work if step < stages], last, back_sides(0))
    back_side[0] = got[:2]
    last_terms(0)
    total_small = small_step(total_small, got, "dp", [1])
    for late_step in range(stages):
        work = [(1, 3 + late_step), (2, 2 + late_step), (3, 1 + late_step), (0, late_step)]
        got = advance([(i, step) for i, step in work if step < stages], got)
    total_small = small_step(total_small, got[:1], "dp", range(2, dp_size, 2))
    own_width = norm_gains.shape[1]
    own_small = lax.dynamic_slice_in_dim(
        total_small, (dp_index * t_size + t_index) * own_width, own_width, 1
    )

    def total(i):
        return functools.reduce(jnp.add, [term.astype(F32) for term in terms[i]])

    ffn_new = update(
        [total(i) for i in range(1, PARTS + 1)],
        (gate_up, first_gate_up, second_gate_up),
        (down_proj, first_down_proj, second_down_proj),
    )
    mix_new = update(
        [total(0)], (mixer_in, first_mixer_in, second_mixer_in), (mixer_out, first_mixer_out, second_mixer_out)
    )
    gains_new = adamw(norm_gains, own_small[:2], first_norm_gains, second_norm_gains, RATE_SMALL, 0.0)
    kernel_new = adamw(conv_kernel, own_small[2:], first_conv_kernel, second_conv_kernel, RATE_SMALL, DECAY)
    block_out, grad_input = to_natural(block_out, order), to_natural(grad_input, order)
    return (block_out, grad_input, *mix_new, *ffn_new, *gains_new, *kernel_new)


def solution(mesh):
    rows = P(("dp", "tensor"), None)
    in_w, out_w, small = P(None, "dp", "tensor"), P("tensor", "dp"), P(None, ("dp", "tensor"))
    return jax.shard_map(
        local,
        mesh=mesh,
        in_specs=(
            (rows, P("dp", None), rows, in_w, out_w, in_w, out_w, small, small)
            + (in_w,) * 2
            + (out_w,) * 2
            + (in_w,) * 2
            + (out_w,) * 2
            + (small,) * 4
        ),
        out_specs=(rows, rows)
        + (in_w,) * 3
        + (out_w,) * 3
        + (in_w,) * 3
        + (out_w,) * 3
        + (small,) * 6,
        check_vma=False,
    )
```

```python
import functools

import jax
import jax.numpy as jnp
from jax import lax
from jax.experimental import pallas as pl
from jax.experimental.pallas import tpu as pltpu
from jax.sharding import PartitionSpec as P

KW = 3
STEP = 10
HALO = 16
PARTS = 3

EPS_NORM = 1e-05
EPS_ADAM = 1e-08
BETA_FIRST = 0.9
BETA_SECOND = 0.95
RATE_MATRIX = 0.05
RATE_SMALL = 0.5
DECAY = 0.1

BF = jnp.bfloat16
F32 = jnp.float32


def swap(values, axis, bit):
    size = lax.axis_size(axis)
    return lax.ppermute(values, axis, [(i, i ^ bit) for i in range(size)])


def halves(values, axis):
    size = values.shape[axis] // 2
    return (
        lax.slice_in_dim(values, 0, size, axis=axis),
        lax.slice_in_dim(values, size, 2 * size, axis=axis),
    )


def low_bits():
    return (
        [2 << i for i in range((lax.axis_size("dp") // 2).bit_length() - 1)],
        [4 << i for i in range((lax.axis_size("tensor") // 4).bit_length() - 1)],
    )


def ordered(values, others):
    values = list(values)
    return list(lax.optimization_barrier((*values, *others)))[: len(values)]


def phase(others, sends):
    values = ordered([send[0] for send in sends], others)
    return [swap(value, axis, bit) for value, (_, axis, bit) in zip(values, sends)]


def join(parts, axis):
    return jnp.concatenate(parts, axis)


def fold(parts, wide):
    return functools.reduce(jnp.add, [halves(part, wide)[1].astype(F32) for part in parts]).astype(BF)


def plus(left, right):
    return (left.astype(F32) + right.astype(F32)).astype(BF)


def rotate_left(values, count):
    bits = count.bit_length() - 1
    return ((values << 1) | (values >> (bits - 1))) & (count - 1)


def rotate_right(values, count):
    bits = count.bit_length() - 1
    return ((values & 1) << (bits - 1)) | (values >> 1)


def block_codes(count):
    return [base ^ (e << 2) for base in (0, 1, 2, 3) for e in range(count // 4)]


def block_place(code, count):
    return (code & 3) * (count // 4) + (code >> 2)


def shift_rows(values, start, rows):
    return lax.slice_in_dim(values, start, start + rows, axis=0)


def lag_masks(seg_flat, length):
    positions = jnp.arange(seg_flat.shape[0], dtype=jnp.int32) % length
    masks = []
    for shift in range(1, KW):
        before = jnp.concatenate([jnp.zeros((shift,), seg_flat.dtype), seg_flat[:-shift]], 0)
        same = (positions >= shift) & (seg_flat == before)
        masks.append(jnp.where(same, 1.0, 0.0).astype(F32)[:, None])
    return masks


def rms_scale(values):
    return lax.rsqrt(jnp.mean(values * values, axis=-1, keepdims=True) + EPS_NORM)


def adamw(param, grad, first, second, rate, decay):
    first_new = BETA_FIRST * first + (1.0 - BETA_FIRST) * grad
    second_new = BETA_SECOND * second + (1.0 - BETA_SECOND) * grad * grad
    first_hat = first_new / (1.0 - BETA_FIRST**STEP)
    second_hat = second_new / (1.0 - BETA_SECOND**STEP)
    return (
        param - rate * (first_hat / (jnp.sqrt(second_hat) + EPS_ADAM) + decay * param),
        first_new,
        second_new,
    )


def mm(spec, left, right, out=F32):
    return jnp.einsum(spec, left, right, preferred_element_type=F32).astype(out)


ANY = pl.BlockSpec(memory_space=pl.ANY)
LIMIT = 26 * 1024 * 1024


def params(count=1):
    return pltpu.CompilerParams(
        vmem_limit_bytes=LIMIT, dimension_semantics=("arbitrary",) * count
    )


def whole(shape):
    return pl.BlockSpec(shape, lambda *_: (0,) * len(shape), pipeline_mode=pl.Buffered(1))


def arrange_kernel(order, tokens, before, cot, x_out, cot_out):
    count = order.shape[0]
    width = tokens.shape[1] // count
    for j in range(count):
        spot = pl.ds(pl.multiple_of(order[j] * width, width), width)
        own = pl.ds(j * width, width)
        x_out[:HALO, own] = before[:, spot]
        x_out[HALO:, own] = tokens[:, spot]
        cot_out[:, own] = cot[:, spot]


def pick_blocks(values, places):
    count = places.shape[0]
    width = values.shape[1] // count
    return jnp.concatenate(
        [lax.dynamic_slice_in_dim(values, places[j] * width, width, 1) for j in range(count)], 1
    )


def narrow(order, width):
    return (width // order.shape[0]) % 128 != 0


def to_natural(values, order):
    if not narrow(order, values.shape[1]):
        return values
    return pick_blocks(values, jnp.argsort(order))


def arrange(order, tokens, before, cot):
    rows, width = tokens.shape
    if narrow(order, width):
        extended = jnp.concatenate([before, tokens], 0)
        return pick_blocks(extended, order), pick_blocks(cot, order)
    vmem = pl.BlockSpec(memory_space=pltpu.VMEM)
    return pl.pallas_call(
        arrange_kernel,
        out_shape=(
            jax.ShapeDtypeStruct((rows + HALO, width), BF),
            jax.ShapeDtypeStruct((rows, width), BF),
        ),
        in_specs=[pl.BlockSpec(memory_space=pltpu.SMEM), vmem, vmem, vmem],
        out_specs=(vmem, vmem),
        compiler_params=pltpu.CompilerParams(vmem_limit_bytes=LIMIT),
        name="arrange",
    )(order, tokens, before, cot)


def nt(left, right):
    return lax.dot_general(left, right, (((1,), (1,)), ((), ())), preferred_element_type=F32)


def nn(left, right):
    return jnp.dot(left, right, preferred_element_type=F32)


def ffn_kernel(first, h, ht, c, ct, *rest):
    pieces, rest = rest[:8], rest[8:]
    grads, (branch, back, w, act, dgate, dup) = rest[-14:-6], rest[-6:]
    deep, half = pieces[0].shape[1:]
    spots = [
        (pl.ds(i % 4 * deep, deep), pl.ds(i // 4 * half, half)) for i in range(8)
    ]
    rows = h.shape[0]
    tall = 384

    @pl.when(pl.program_id(0) == 0)
    def _():
        for i, total in enumerate((branch, back)):
            total[...] = jnp.zeros_like(total) if first else rest[i][...]

    for piece, (deep_span, span) in zip(pieces, spots):
        w[:, deep_span, span] = piece[...]
    for start in range(0, rows, tall):
        span = pl.ds(start, tall)
        gate = nn(h[span, :], w[0])
        up = nn(h[span, :], w[1])
        da = nn(c[span, :], w[2])
        sigma = 1.0 / (1.0 + jnp.exp(-gate))
        silu = gate * sigma
        act[span, :] = (silu * up).astype(BF)
        dup[span, :] = (da * silu).astype(BF)
        dgate[span, :] = (da * up * (sigma + silu * (1.0 - sigma))).astype(BF)
    for k, (left, right) in enumerate(((ht, dgate), (ht, dup), (ct, act))):
        grad = nn(left[...], right[...]).astype(BF)
        for i, out in enumerate(grads):
            out[k] = grad[i % 4 * deep : (i % 4 + 1) * deep, i // 4 * half : (i // 4 + 1) * half]
    for start in range(0, rows, tall):
        span = pl.ds(start, tall)
        branch[span, :] += nt(act[span, :], w[2])
        back[span, :] += nt(dgate[span, :], w[0]) + nt(dup[span, :], w[1])


def ffn(h, ht, c, ct, pieces, sums):
    rows, width = h.shape
    planes, deep, cols = pieces[0].shape
    tile = 128
    block = pl.BlockSpec((planes, deep, tile), lambda j: (0, 0, j))
    vmem = pl.BlockSpec(memory_space=pltpu.VMEM)
    grad = jax.ShapeDtypeStruct(pieces[0].shape, BF)
    part = jax.ShapeDtypeStruct((rows, width), F32)
    out = pl.pallas_call(
        functools.partial(ffn_kernel, not sums),
        grid=(cols // tile,),
        out_shape=(grad,) * 8 + (part, part),
        in_specs=[vmem] * 4 + [block] * 8 + [vmem] * len(sums),
        out_specs=(block,) * 8 + (vmem, vmem),
        input_output_aliases={12: 8, 13: 9} if sums else {},
        scratch_shapes=[pltpu.VMEM((planes, width, 2 * tile), BF)]
        + [pltpu.VMEM((rows, 2 * tile), BF)] * 3,
        compiler_params=params(),
        cost_estimate=pl.CostEstimate(
            flops=36 * rows * width * cols,
            bytes_accessed=24 * width * cols,
            transcendentals=2 * rows * cols,
        ),
        name="ffn",
    )(h, ht, c, ct, *pieces, *sums)
    return out[:8], out[8:]


def middle_kernel(order, middle, scale, gain, cot, *rest):
    block_out, grad, grad_low, gain_grad = rest[-4:]
    half = (len(rest) - 4) // 2
    branches, backs = rest[:half], rest[half : 2 * half]
    x2, r2, up = middle[...], scale[...], backs[0][...].astype(F32)
    for ref in backs[1:]:
        up = up + ref[...].astype(F32)
    total = x2
    for ref in branches:
        total = total + ref[...].astype(F32)
    store_natural(order, block_out, total.astype(BF))
    norm_back(x2, r2, gain, up, cot[...].astype(F32), grad, gain_grad)
    grad_low[...] = grad[...].astype(BF)


def store_natural(order, out, total):
    count = order.shape[0]
    if narrow(order, total.shape[1]):
        out[...] = total
        return
    width = total.shape[1] // count
    for j in range(count):
        spot = pl.ds(pl.multiple_of(order[j] * width, width), width)
        out[:, spot] = total[:, j * width : (j + 1) * width]


def norm_back(values, scale, gain, upstream, carried, out, gain_grad, order=None):
    scaled = upstream * gain[...]
    mean = jnp.mean(scaled * values, axis=-1, keepdims=True)
    total = carried + scale * scaled - values * (scale * scale * scale * mean)
    if order is None:
        out[...] = total
    else:
        store_natural(order, out, total)
    sums = jnp.sum(upstream * values * scale, axis=0, keepdims=True)

    @pl.when(pl.program_id(0) == 0)
    def _():
        gain_grad[...] = sums

    @pl.when(pl.program_id(0) > 0)
    def _():
        gain_grad[...] += sums


def row_specs(tile, width):
    return (
        pl.BlockSpec(memory_space=pltpu.SMEM),
        pl.BlockSpec((tile, width), lambda i: (i, 0)),
        pl.BlockSpec((tile, 1), lambda i: (i, 0)),
        pl.BlockSpec((1, width), lambda i: (0, 0)),
    )


def middle_back(order, middle, scale, gain, cot, branches, backs, deps):
    rows, width = middle.shape
    tile = 128
    smem, row, column, single = row_specs(tile, width)
    count = len(branches)

    def kernel(*refs):
        middle_kernel(*refs[: 5 + 2 * count], *refs[5 + 2 * count + len(deps) :])

    return pl.pallas_call(
        kernel,
        grid=(rows // tile,),
        out_shape=(
            jax.ShapeDtypeStruct((rows, width), BF),
            jax.ShapeDtypeStruct((rows, width), F32),
            jax.ShapeDtypeStruct((rows, width), BF),
            jax.ShapeDtypeStruct((1, width), F32),
        ),
        in_specs=[smem, row, column, single, row] + [row] * (2 * count) + [ANY] * len(deps),
        out_specs=(row, row, row, single),
        compiler_params=params(),
        cost_estimate=pl.CostEstimate(
            flops=30 * rows * width, bytes_accessed=(14 + 8 * count) * rows * width, transcendentals=0
        ),
        name="middle_back",
    )(order, middle, scale, gain, cot, *branches, *backs, *deps)


def input_kernel(order, values, scale, gain, carried, upstream, out, gain_grad):
    norm_back(
        values[...].astype(F32), scale[...], gain, upstream[...], carried[...], out, gain_grad, order
    )


def input_back(order, values, scale, gain, carried, upstream):
    rows, width = values.shape
    tile = 128
    smem, row, column, single = row_specs(tile, width)
    return pl.pallas_call(
        input_kernel,
        grid=(rows // tile,),
        out_shape=(
            jax.ShapeDtypeStruct((rows, width), F32),
            jax.ShapeDtypeStruct((1, width), F32),
        ),
        in_specs=[smem, row, column, single, row, row],
        out_specs=(row, single),
        compiler_params=params(),
        cost_estimate=pl.CostEstimate(
            flops=20 * rows * width, bytes_accessed=14 * rows * width, transcendentals=0
        ),
        name="input_back",
    )(order, values, scale, gain, carried, upstream)


def mixer_grad_kernel(ht, dt, pa, pb, ya, yb, *rest):
    ga, gb = rest[-2:]
    step = pl.program_id(0)

    @pl.when(step < 3)
    def _():
        ga[0] = nn(ht[...], pa[0]).astype(BF)
        gb[0] = nn(ht[...], pb[0]).astype(BF)

    @pl.when(step == 3)
    def _():
        ga[0] = nn(dt[...], ya[...]).astype(BF)
        gb[0] = nn(dt[...], yb[...]).astype(BF)


def mixer_grad(ht, dt, proj_grad, gated, first, second, deps):
    width, rows = ht.shape
    cols = gated.shape[1] // 4

    def column(block):
        return pl.BlockSpec((1, rows, cols), lambda k: (jnp.minimum(k, 2), 0, block))

    def gated_column(block):
        return pl.BlockSpec((rows, cols), lambda k: (0, block))

    out = pl.BlockSpec((1, width, cols), lambda k: (k, 0, 0))
    grad = jax.ShapeDtypeStruct((4, width, cols), BF)
    return pl.pallas_call(
        mixer_grad_kernel,
        grid=(4,),
        out_shape=(grad, grad),
        in_specs=[
            whole((width, rows)),
            whole((width, rows)),
            column(first),
            column(second),
            gated_column(first),
            gated_column(second),
        ]
        + [ANY] * len(deps),
        out_specs=(out, out),
        compiler_params=params(),
        cost_estimate=pl.CostEstimate(
            flops=16 * rows * width * cols,
            bytes_accessed=4 * rows * width + 16 * width * cols + 16 * rows * cols,
            transcendentals=0,
        ),
        name="mixer_grad",
    )(ht, dt, proj_grad, proj_grad, gated, gated, *deps)


def update_kernel(*refs):
    count = (len(refs) - 12)
    totals, rest = refs[:count], refs[count:]
    wide, tall, wide_new, tall_new = rest[:3], rest[3:6], rest[6:9], rest[9:]
    for i, total in enumerate(totals):

        @pl.when(pl.program_id(0) == i)
        def _():
            last = total.shape[0] - 1
            new = adamw(wide[0][...], total[:last], wide[1][...], wide[2][...], RATE_MATRIX, DECAY)
            for ref, value in zip(wide_new, new):
                ref[...] = value
            grad = jnp.transpose(total[last])
            new = adamw(tall[0][...], grad, tall[1][...], tall[2][...], RATE_MATRIX, DECAY)
            for ref, value in zip(tall_new, new):
                ref[...] = value


def update(totals, wide, tall):
    if (wide[0].shape[2] // len(totals)) % 128:
        totals = [jnp.concatenate(totals, 2)]
    count = len(totals)
    planes, deep, cols = wide[0].shape
    part = cols // count
    wide_spec = pl.BlockSpec((planes, deep, part), lambda i: (0, 0, i))
    tall_spec = pl.BlockSpec((part, deep), lambda i: (i, 0))
    return pl.pallas_call(
        update_kernel,
        grid=(count,),
        out_shape=tuple(jax.ShapeDtypeStruct(a.shape, F32) for a in wide + tall),
        in_specs=[whole(total.shape) for total in totals] + [wide_spec] * 3 + [tall_spec] * 3,
        out_specs=(wide_spec,) * 3 + (tall_spec,) * 3,
        compiler_params=params(),
        cost_estimate=pl.CostEstimate(
            flops=20 * (planes + 1) * deep * cols,
            bytes_accessed=28 * (planes + 1) * deep * cols,
            transcendentals=(planes + 1) * deep * cols,
        ),
        name="update",
    )(*totals, *wide, *tall)


def local(
    tokens,
    segments,
    cotangent,
    mixer_in,
    mixer_out,
    gate_up,
    down_proj,
    norm_gains,
    conv_kernel,
    first_mixer_in,
    second_mixer_in,
    first_mixer_out,
    second_mixer_out,
    first_gate_up,
    second_gate_up,
    first_down_proj,
    second_down_proj,
    first_norm_gains,
    second_norm_gains,
    first_conv_kernel,
    second_conv_kernel,
):
    dp_size, t_size = lax.axis_size("dp"), lax.axis_size("tensor")
    dp_index, t_index = lax.axis_index("dp"), lax.axis_index("tensor")
    rows, length = tokens.shape[0], segments.shape[1]
    order = dp_index ^ jnp.array([rotate_left(j, dp_size) for j in range(dp_size)], jnp.int32)

    z_bits, t_bits = low_bits()
    wide, cut = 1, 2
    ffn_cols = gate_up.shape[2] // PARTS
    own = [join([mixer_in.astype(BF), mixer_out.T.astype(BF)[None]], 0)]
    for i in range(PARTS):
        cols = slice(i * ffn_cols, (i + 1) * ffn_cols)
        own.append(join([gate_up[:, :, cols].astype(BF), down_proj[cols].T.astype(BF)[None]], 0))

    def deepen(places, others, axis, bit, along):
        got = phase(others, [(own[i], axis, bit) for i in places])
        for i, part in zip(places, got):
            own[i] = join([own[i], part], along)
        return got

    def first_rows(places, others):
        for bit in z_bits[:-1]:
            others = deepen(places, others, "dp", bit, wide)
        for bit in t_bits:
            others = deepen(places, others, "tensor", bit, cut)
        return others

    def by_x(value):
        return (value, "dp", 1)

    def by_y(value):
        return (value, "tensor", 2)

    def by_z(value):
        return (value, "dp", z_bits[-1])

    def other_core(value):
        return swap(value, "tensor", 1)

    xa, xb, ya, yb, zb, da, db = ({} for _ in range(7))

    def pieces_of(i):
        return [own[i], zb[i], xa[i], xb[i], ya[i], yb[i], da[i], db[i]]

    small = jnp.concatenate([norm_gains, conv_kernel], 0)[:, None, :]
    before = lax.ppermute(
        tokens[rows - HALO :], "tensor", [(i, i + 1) for i in range(t_size - 1)]
    )
    small_t = phase([], [(small, "tensor", code) for code in range(1, t_size)])
    last = first_rows([0, 1], [])
    small = join([small, *small_t], 1)
    small_x = phase([*last, small], [(small, "dp", 1)])
    xa[0], ya[0], zb[0] = got = phase(last, [by_x(own[0]), by_y(own[0]), by_z(own[0])])
    later = first_rows(range(2, PARTS + 1), last)
    small = join([small, *small_x], 1)
    small_z = phase([*got, small], [(small, "dp", code) for code in range(2, dp_size, 2)])
    xb[0], yb[0], da[0], ya[1], zb[1] = got = phase(
        got, [by_x(zb[0]), by_y(zb[0]), by_x(ya[0]), by_y(own[1]), by_z(own[1])]
    )
    x_ext, cot = arrange(order, tokens, before, cotangent)
    db[0], xa[1], zb[2], cot_other = phase(
        [*got[:3], *later], [by_y(xb[0]), by_x(own[1]), by_z(own[2]), (cot, "tensor", 1)]
    )
    small = join([small, *small_z], 1)

    small = small.reshape(small.shape[0], dp_size, t_size, small.shape[2])
    for axis, index, size_axis in ((1, dp_index, dp_size), (2, t_index, t_size)):
        for i in range(size_axis.bit_length() - 1):
            shape = small.shape
            split = small.reshape(shape[:axis] + (size_axis >> (i + 1), 2, 1 << i) + shape[axis + 1 :])
            flipped = jnp.flip(split, axis + 1)
            small = jnp.where((index >> i) & 1 == 1, flipped, split).reshape(shape)
    small = small.reshape(small.shape[0], -1)
    block = small.shape[1] // dp_size
    gains = jnp.concatenate(
        [lax.dynamic_slice_in_dim(small[:2], order[j] * block, block, 1) for j in range(dp_size)], 1
    )
    channels = small.shape[1] // t_size
    codes = block_codes(t_size)
    kernel = jnp.concatenate(
        [
            lax.dynamic_slice_in_dim(small[2:], (t_index ^ code) * channels, channels, 1)
            for code in codes
        ],
        1,
    )

    masks = []
    for mask in lag_masks(segments.reshape(-1), length):
        padded = jnp.concatenate([mask, jnp.zeros((HALO, 1), F32)], 0)
        masks.append(lax.dynamic_slice_in_dim(padded, t_index * rows, rows + HALO, 0))

    extended = x_ext.astype(F32)
    scale_ext = rms_scale(extended)
    normed_ext = (extended * scale_ext * gains[0]).astype(BF)
    values, scale_one, normed_one = extended[HALO:], scale_ext[HALO:], normed_ext[HALO:]
    near, far = join(pieces_of(0)[:4], wide), join(pieces_of(0)[4:], wide)
    wm = [near, other_core(near), far, other_core(far)]
    got = phase(
        [db[0], xa[1], zb[1], ya[1]], [by_x(zb[1]), by_y(zb[1]), by_x(ya[1]), by_y(own[2])]
    )
    wm_all = jnp.concatenate(wm, 2)
    win_all, wout_all = wm_all[:3], wm_all[3]
    projected = mm("td,kdc->ktc", normed_ext, win_all)
    part_b, part_c, part_x = projected[0], projected[1][HALO:], projected[2]
    product_ext = part_b * part_x
    part_b, part_x = part_b[HALO:], part_x[HALO:]
    product = product_ext[HALO:]
    convolved = kernel[0] * product
    for shift in range(1, KW):
        convolved = convolved + kernel[shift] * masks[shift - 1][:rows] * shift_rows(
            product_ext, HALO - shift, rows
        )
    gated = (part_c * convolved).astype(BF)
    (gated,) = ordered([gated], got)
    middle = values + mm("tc,dc->td", gated, wout_all)
    scale_two = rms_scale(middle)
    normed_two = (middle * scale_two * gains[1]).astype(BF)

    normed_other = other_core(normed_two)
    h, c = join([normed_two, normed_other], 0), join([cot, cot_other], 0)
    ht, ct = h.T, c.T
    sums, grads = [], {}
    xb[1], yb[1], da[1], ya[2] = got = ordered(got, [normed_two])
    (zb[2],) = ordered([zb[2]], [normed_two])
    db[1], xa[2], zb[3] = phase(got, [by_y(xb[1]), by_x(own[2]), by_z(own[3])])

    def run(i):
        nonlocal sums
        grads[i], sums = ffn(h, ht, c, ct, pieces_of(i), list(sums))
        return grads[i]

    got = phase([db[1], xa[2], zb[2]], [by_x(zb[2]), by_y(zb[2]), by_x(ya[2]), by_y(own[3])])
    xb[2], yb[2], da[2], ya[3] = got = ordered(got, run(1)[:1])
    db[2], xa[3] = got = phase(got, [by_y(xb[2]), by_x(own[3])])

    axa, axb, aya, ayb, ada, adb = ({} for _ in range(6))

    def sum_xb(i):
        return by_x(plus(grads[i][3], adb[i]))

    def sum_ya(i):
        return by_y(plus(grads[i][4], ada[i]))

    got = phase([*got, zb[3]], [by_x(zb[3]), by_y(zb[3]), by_x(ya[3]), by_y(grads[1][5])])
    xb[3], yb[3], da[3], ayb[1] = got = ordered(got, run(2)[:1])
    db[3], ada[1] = got = phase(got, [by_y(xb[3]), by_x(grads[1][6])])
    (db[3],) = ordered([db[3]], [ada[1]])
    got = phase(
        got, [by_x(grads[1][2]), by_y(grads[1][7]), by_x(grads[2][6]), by_y(grads[2][7])]
    )
    axa[1], adb[1], ada[2], adb[2] = got = ordered(got, run(3)[:1])
    branch, back = ordered(sums, got)
    branch_in, back_in = [other_core(value[rows:].astype(BF)) for value in (branch, back)]
    deps = got
    got = phase(got, [sum_xb(1), sum_ya(1), by_x(grads[2][2]), by_y(grads[2][5])])
    block_out, middle_grad, mixed_grad, gain_two_grad = middle_back(
        order, middle, scale_two, gains[1:2], cot, [branch, branch_in], [back, back_in], deps
    )

    gated_grad = mm("td,dc->tc", mixed_grad, wout_all)
    axb[1], aya[1], axa[2], ayb[2] = got = ordered(got, [gated_grad])
    (gated_grad,) = ordered([gated_grad], got)

    def sum_b(i):
        return by_z(functools.reduce(jnp.add, [v.astype(F32) for v in (grads[i][1], axb[i], ayb[i])]).astype(BF))

    got = phase(
        got, [sum_xb(2), sum_ya(2), by_x(grads[3][6]), by_y(grads[3][7]), sum_b(1)]
    )
    conv_grad = gated_grad * part_c
    after_rel = lax.ppermute(
        conv_grad[:8], "tensor", [(i + 1, i) for i in range(t_size - 1)]
    )
    after = jnp.concatenate(
        [
            lax.dynamic_slice_in_dim(
                after_rel,
                block_place(code ^ t_index ^ (t_index + 1), t_size) % t_size * channels,
                channels,
                1,
            )
            for code in codes
        ],
        1,
    )
    c_grad = gated_grad * convolved
    conv_ext = jnp.concatenate([conv_grad, after], 0)
    kernel_rows = [jnp.sum(conv_grad * product, axis=0)]
    product_grad = kernel[0] * conv_grad
    for shift in range(1, KW):
        masked = masks[shift - 1][: rows + 8] * conv_ext
        kernel_rows.append(
            jnp.sum(masked[:rows] * shift_rows(product_ext, HALO - shift, rows), axis=0)
        )
        product_grad = product_grad + kernel[shift] * shift_rows(masked, shift, rows)
    proj_grad = jnp.stack([product_grad * part_x, c_grad, product_grad * part_b], 0).astype(BF)
    zs = {}
    axb[2], aya[2], ada[3], adb[3], zs[1] = got = ordered(got, [proj_grad])
    one_t, mixed_t = normed_one.T, mixed_grad.T
    got = phase(
        got, [by_x(grads[3][2]), sum_xb(3), by_y(grads[3][5]), sum_ya(3), sum_b(2)]
    )
    m_near_core, m_far_core = mixer_grad(one_t, mixed_t, proj_grad, gated, 1, 3, [])
    m_in = [other_core(m_far_core), other_core(m_near_core)]
    m_near, m_far = mixer_grad(one_t, mixed_t, proj_grad, gated, 0, 2, [axb[2], aya[2], ada[3], adb[3]])
    axa[3], axb[3], ayb[3], aya[3], zs[2] = got = ordered(got, [m_far])
    deep = m_near.shape[wide] // 4
    grads[0] = [
        plus(
            lax.slice_in_dim(value, i * deep, (i + 1) * deep, axis=wide),
            lax.slice_in_dim(other, i * deep, (i + 1) * deep, axis=wide),
        )
        for value, other in ((m_near, m_in[1]), (m_far, m_in[0]))
        for i in range(4)
    ]

    terms, steps = {}, [("tensor", bit, cut) for bit in reversed(t_bits)]
    steps += [("dp", bit, wide) for bit in reversed(z_bits[:-1])]

    def sum_a(i):
        terms[i] = [grads[i][0], axa[i], aya[i], zs[i]]

    def fold_send(i, step):
        axis, bit, along = steps[step]
        return (fold(terms[i], along), axis, bit)

    def folded(i, step, got):
        along = steps[step][2]
        terms[i] = [halves(term, along)[0] for term in terms[i]] + [got]

    sum_a(1)
    got = phase(
        got, [by_x(grads[0][6]), by_x(grads[0][2]), by_y(grads[0][7]), by_y(grads[0][5]), sum_b(3)]
    )
    ada[0], axa[0], adb[0], ayb[0], zs[3] = last = got

    (late,) = ordered([proj_grad], grads[0][:1])
    normed_one_grad = mm("ktc,kdc->td", late, win_all)
    grad_input, gain_one_grad = input_back(
        order, x_ext[HALO:], scale_one, gains[:1], middle_grad, normed_one_grad
    )

    gain_rel = jnp.concatenate([gain_one_grad, gain_two_grad], 0)
    kernel_rel = jnp.stack(kernel_rows, 0)
    gain_sums = jnp.concatenate(
        [
            lax.dynamic_slice_in_dim(gain_rel, rotate_right(dp_index ^ q, dp_size) * block, block, 1)
            for q in range(dp_size)
        ],
        1,
    )
    kernel_sums = jnp.concatenate(
        [
            lax.dynamic_slice_in_dim(
                kernel_rel, block_place(t_index ^ q, t_size) * channels, channels, 1
            )
            for q in range(t_size)
        ],
        1,
    )
    total_small = jnp.concatenate([gain_sums, kernel_sums], 0)

    def small_step(value, others, axis, codes):
        return functools.reduce(jnp.add, [value, *phase(others, [(value, axis, code) for code in codes])])

    sum_a(2)
    sum_a(3)
    total_small = small_step(total_small, last, "tensor", range(1, t_size))
    got = phase(last, [sum_xb(0), sum_ya(0), *[fold_send(i, 0) for i in range(1, PARTS + 1)]])
    axb[0], aya[0] = got[:2]
    for i in range(1, PARTS + 1):
        folded(i, 0, got[i + 1])
    total_small = small_step(total_small, got[:2], "dp", [1])
    (zs[0],) = phase(got[:2], [sum_b(0)])
    for step in range(1, len(steps)):
        got = phase(got, [fold_send(i, step) for i in range(1, PARTS + 1)])
        for i in range(1, PARTS + 1):
            folded(i, step, got[i - 1])
    sum_a(0)
    total_small = small_step(total_small, [zs[0]], "dp", range(2, dp_size, 2))
    for step in range(len(steps)):
        (got,) = phase([], [fold_send(0, step)])
        folded(0, step, got)
    own_width = norm_gains.shape[1]
    own_small = lax.dynamic_slice_in_dim(
        total_small, (dp_index * t_size + t_index) * own_width, own_width, 1
    )

    def total(i):
        return functools.reduce(jnp.add, [term.astype(F32) for term in terms[i]])

    ffn_new = update(
        [total(i) for i in range(1, PARTS + 1)],
        (gate_up, first_gate_up, second_gate_up),
        (down_proj, first_down_proj, second_down_proj),
    )
    mix_new = update(
        [total(0)], (mixer_in, first_mixer_in, second_mixer_in), (mixer_out, first_mixer_out, second_mixer_out)
    )
    gains_new = adamw(norm_gains, own_small[:2], first_norm_gains, second_norm_gains, RATE_SMALL, 0.0)
    kernel_new = adamw(conv_kernel, own_small[2:], first_conv_kernel, second_conv_kernel, RATE_SMALL, DECAY)
    block_out, grad_input = to_natural(block_out, order), to_natural(grad_input, order)
    return (block_out, grad_input, *mix_new, *ffn_new, *gains_new, *kernel_new)


def solution(mesh):
    rows = P(("dp", "tensor"), None)
    in_w, out_w, small = P(None, "dp", "tensor"), P("tensor", "dp"), P(None, ("dp", "tensor"))
    return jax.shard_map(
        local,
        mesh=mesh,
        in_specs=(
            (rows, P("dp", None), rows, in_w, out_w, in_w, out_w, small, small)
            + (in_w,) * 2
            + (out_w,) * 2
            + (in_w,) * 2
            + (out_w,) * 2
            + (small,) * 4
        ),
        out_specs=(rows, rows)
        + (in_w,) * 3
        + (out_w,) * 3
        + (in_w,) * 3
        + (out_w,) * 3
        + (small,) * 6,
        check_vma=False,
    )
```

```python
import functools

import jax
import jax.numpy as jnp
from jax import lax
from jax.experimental import pallas as pl
from jax.experimental.pallas import tpu as pltpu
from jax.sharding import PartitionSpec as P

KW = 3
STEP = 10
HALO = 16
PARTS = 3

EPS_NORM = 1e-05
EPS_ADAM = 1e-08
BETA_FIRST = 0.9
BETA_SECOND = 0.95
RATE_MATRIX = 0.05
RATE_SMALL = 0.5
DECAY = 0.1

BF = jnp.bfloat16
F32 = jnp.float32


def swap(values, axis, bit):
    size = lax.axis_size(axis)
    return lax.ppermute(values, axis, [(i, i ^ bit) for i in range(size)])


def halves(values, axis):
    size = values.shape[axis] // 2
    return (
        lax.slice_in_dim(values, 0, size, axis=axis),
        lax.slice_in_dim(values, size, 2 * size, axis=axis),
    )


def low_bits():
    return (
        [2 << i for i in range((lax.axis_size("dp") // 2).bit_length() - 1)],
        [4 << i for i in range((lax.axis_size("tensor") // 4).bit_length() - 1)],
    )


def ordered(values, others):
    values = list(values)
    return list(lax.optimization_barrier((*values, *others)))[: len(values)]


def phase(others, sends):
    values = ordered([send[0] for send in sends], others)
    return [swap(value, axis, bit) for value, (_, axis, bit) in zip(values, sends)]


def join(parts, axis):
    return jnp.concatenate(parts, axis)


def fold(parts, wide):
    return functools.reduce(jnp.add, [halves(part, wide)[1].astype(F32) for part in parts]).astype(BF)


def plus(left, right):
    return (left.astype(F32) + right.astype(F32)).astype(BF)


def rotate_left(values, count):
    bits = count.bit_length() - 1
    return ((values << 1) | (values >> (bits - 1))) & (count - 1)


def rotate_right(values, count):
    bits = count.bit_length() - 1
    return ((values & 1) << (bits - 1)) | (values >> 1)


def block_codes(count):
    return [base ^ (e << 2) for base in (0, 1, 2, 3) for e in range(count // 4)]


def block_place(code, count):
    return (code & 3) * (count // 4) + (code >> 2)


def shift_rows(values, start, rows):
    return lax.slice_in_dim(values, start, start + rows, axis=0)


def lag_masks(seg_flat, length):
    positions = jnp.arange(seg_flat.shape[0], dtype=jnp.int32) % length
    masks = []
    for shift in range(1, KW):
        before = jnp.concatenate([jnp.zeros((shift,), seg_flat.dtype), seg_flat[:-shift]], 0)
        same = (positions >= shift) & (seg_flat == before)
        masks.append(jnp.where(same, 1.0, 0.0).astype(F32)[:, None])
    return masks


def rms_scale(values):
    return lax.rsqrt(jnp.mean(values * values, axis=-1, keepdims=True) + EPS_NORM)


def adamw(param, grad, first, second, rate, decay):
    first_new = BETA_FIRST * first + (1.0 - BETA_FIRST) * grad
    second_new = BETA_SECOND * second + (1.0 - BETA_SECOND) * grad * grad
    first_hat = first_new / (1.0 - BETA_FIRST**STEP)
    second_hat = second_new / (1.0 - BETA_SECOND**STEP)
    return (
        param - rate * (first_hat / (jnp.sqrt(second_hat) + EPS_ADAM) + decay * param),
        first_new,
        second_new,
    )


def mm(spec, left, right, out=F32):
    return jnp.einsum(spec, left, right, preferred_element_type=F32).astype(out)


ANY = pl.BlockSpec(memory_space=pl.ANY)
LIMIT = 26 * 1024 * 1024


def params(count=1):
    return pltpu.CompilerParams(
        vmem_limit_bytes=LIMIT, dimension_semantics=("arbitrary",) * count
    )


def whole(shape):
    return pl.BlockSpec(shape, lambda *_: (0,) * len(shape), pipeline_mode=pl.Buffered(1))


def arrange_kernel(order, tokens, before, cot, x_out, cot_out):
    count = order.shape[0]
    width = tokens.shape[1] // count
    for j in range(count):
        spot = pl.ds(pl.multiple_of(order[j] * width, width), width)
        own = pl.ds(j * width, width)
        x_out[:HALO, own] = before[:, spot]
        x_out[HALO:, own] = tokens[:, spot]
        cot_out[:, own] = cot[:, spot]


def pick_blocks(values, places):
    count = places.shape[0]
    width = values.shape[1] // count
    return jnp.concatenate(
        [lax.dynamic_slice_in_dim(values, places[j] * width, width, 1) for j in range(count)], 1
    )


def narrow(order, width):
    return (width // order.shape[0]) % 128 != 0


def to_natural(values, order):
    if not narrow(order, values.shape[1]):
        return values
    return pick_blocks(values, jnp.argsort(order))


def arrange(order, tokens, before, cot):
    rows, width = tokens.shape
    if narrow(order, width):
        extended = jnp.concatenate([before, tokens], 0)
        return pick_blocks(extended, order), pick_blocks(cot, order)
    vmem = pl.BlockSpec(memory_space=pltpu.VMEM)
    return pl.pallas_call(
        arrange_kernel,
        out_shape=(
            jax.ShapeDtypeStruct((rows + HALO, width), BF),
            jax.ShapeDtypeStruct((rows, width), BF),
        ),
        in_specs=[pl.BlockSpec(memory_space=pltpu.SMEM), vmem, vmem, vmem],
        out_specs=(vmem, vmem),
        compiler_params=pltpu.CompilerParams(vmem_limit_bytes=LIMIT),
        name="arrange",
    )(order, tokens, before, cot)


def nt(left, right):
    return lax.dot_general(left, right, (((1,), (1,)), ((), ())), preferred_element_type=F32)


def nn(left, right):
    return jnp.dot(left, right, preferred_element_type=F32)


def ffn_kernel(first, h_own, h_other, ht_own, ht_other, c, ct, *rest):
    pieces, rest = rest[:8], rest[8:]
    grads, (branch, back, w, act, dgate, dup) = rest[-14:-6], rest[-6:]
    deep, half = pieces[0].shape[1:]
    spots = [
        (pl.ds(i % 4 * deep, deep), pl.ds(i // 4 * half, half)) for i in range(8)
    ]
    rows = c.shape[0]
    own = rows // 2
    tall = 384

    @pl.when(pl.program_id(0) == 0)
    def _():
        for i, total in enumerate((branch, back)):
            total[...] = jnp.zeros_like(total) if first else rest[i][...]

    for piece, (deep_span, span) in zip(pieces, spots):
        w[:, deep_span, span] = piece[...]
    for start in range(0, rows, tall):
        span = pl.ds(start, tall)
        h = h_own[span, :] if start < own else h_other[pl.ds(start - own, tall), :]
        gate = nn(h, w[0])
        up = nn(h, w[1])
        da = nn(c[span, :], w[2])
        sigma = 1.0 / (1.0 + jnp.exp(-gate))
        silu = gate * sigma
        act[span, :] = (silu * up).astype(BF)
        dup[span, :] = (da * silu).astype(BF)
        dgate[span, :] = (da * up * (sigma + silu * (1.0 - sigma))).astype(BF)
    for k, right in enumerate((dgate, dup, act)):
        if k < 2:
            grad = nn(ht_own[...], right[:own, :]) + nn(ht_other[...], right[own:, :])
        else:
            grad = nn(ct[...], right[...])
        grad = grad.astype(BF)
        for i, out in enumerate(grads):
            out[k] = grad[i % 4 * deep : (i % 4 + 1) * deep, i // 4 * half : (i // 4 + 1) * half]
    for start in range(0, rows, tall):
        span = pl.ds(start, tall)
        branch[span, :] += nt(act[span, :], w[2])
        back[span, :] += nt(dgate[span, :], w[0]) + nt(dup[span, :], w[1])


def ffn(tokens, pieces, sums):
    rows, width = tokens[4].shape
    planes, deep, cols = pieces[0].shape
    tile = 128
    block = pl.BlockSpec((planes, deep, tile), lambda j: (0, 0, j))
    vmem = pl.BlockSpec(memory_space=pltpu.VMEM)
    grad = jax.ShapeDtypeStruct(pieces[0].shape, BF)
    part = jax.ShapeDtypeStruct((rows, width), F32)
    out = pl.pallas_call(
        functools.partial(ffn_kernel, not sums),
        grid=(cols // tile,),
        out_shape=(grad,) * 8 + (part, part),
        in_specs=[vmem] * 6 + [block] * 8 + [vmem] * len(sums),
        out_specs=(block,) * 8 + (vmem, vmem),
        input_output_aliases={14: 8, 15: 9} if sums else {},
        scratch_shapes=[pltpu.VMEM((planes, width, 2 * tile), BF)]
        + [pltpu.VMEM((rows, 2 * tile), BF)] * 3,
        compiler_params=params(),
        cost_estimate=pl.CostEstimate(
            flops=36 * rows * width * cols,
            bytes_accessed=24 * width * cols,
            transcendentals=2 * rows * cols,
        ),
        name="ffn",
    )(*tokens, *pieces, *sums)
    return out[:8], out[8:]


def middle_kernel(order, middle, scale, gain, cot, *rest):
    block_out, grad, grad_low, gain_grad = rest[-4:]
    half = (len(rest) - 4) // 2
    branches, backs = rest[:half], rest[half : 2 * half]
    x2, r2, up = middle[...], scale[...], backs[0][...].astype(F32)
    for ref in backs[1:]:
        up = up + ref[...].astype(F32)
    total = x2
    for ref in branches:
        total = total + ref[...].astype(F32)
    store_natural(order, block_out, total.astype(BF))
    norm_back(x2, r2, gain, up, cot[...].astype(F32), grad, gain_grad)
    grad_low[...] = grad[...].astype(BF)


def store_natural(order, out, total):
    count = order.shape[0]
    if narrow(order, total.shape[1]):
        out[...] = total
        return
    width = total.shape[1] // count
    for j in range(count):
        spot = pl.ds(pl.multiple_of(order[j] * width, width), width)
        out[:, spot] = total[:, j * width : (j + 1) * width]


def norm_back(values, scale, gain, upstream, carried, out, gain_grad, order=None):
    scaled = upstream * gain[...]
    mean = jnp.mean(scaled * values, axis=-1, keepdims=True)
    total = carried + scale * scaled - values * (scale * scale * scale * mean)
    if order is None:
        out[...] = total
    else:
        store_natural(order, out, total)
    sums = jnp.sum(upstream * values * scale, axis=0, keepdims=True)

    @pl.when(pl.program_id(0) == 0)
    def _():
        gain_grad[...] = sums

    @pl.when(pl.program_id(0) > 0)
    def _():
        gain_grad[...] += sums


def row_specs(tile, width):
    return (
        pl.BlockSpec(memory_space=pltpu.SMEM),
        pl.BlockSpec((tile, width), lambda i: (i, 0)),
        pl.BlockSpec((tile, 1), lambda i: (i, 0)),
        pl.BlockSpec((1, width), lambda i: (0, 0)),
    )


def middle_back(order, middle, scale, gain, cot, branches, backs, deps):
    rows, width = middle.shape
    tile = 128
    smem, row, column, single = row_specs(tile, width)
    count = len(branches)

    def kernel(*refs):
        middle_kernel(*refs[: 5 + 2 * count], *refs[5 + 2 * count + len(deps) :])

    return pl.pallas_call(
        kernel,
        grid=(rows // tile,),
        out_shape=(
            jax.ShapeDtypeStruct((rows, width), BF),
            jax.ShapeDtypeStruct((rows, width), F32),
            jax.ShapeDtypeStruct((rows, width), BF),
            jax.ShapeDtypeStruct((1, width), F32),
        ),
        in_specs=[smem, row, column, single, row] + [row] * (2 * count) + [ANY] * len(deps),
        out_specs=(row, row, row, single),
        compiler_params=params(),
        cost_estimate=pl.CostEstimate(
            flops=30 * rows * width, bytes_accessed=(14 + 8 * count) * rows * width, transcendentals=0
        ),
        name="middle_back",
    )(order, middle, scale, gain, cot, *branches, *backs, *deps)


def input_kernel(order, values, scale, gain, carried, upstream, out, gain_grad):
    norm_back(
        values[...].astype(F32), scale[...], gain, upstream[...], carried[...], out, gain_grad, order
    )


def input_back(order, values, scale, gain, carried, upstream):
    rows, width = values.shape
    tile = 128
    smem, row, column, single = row_specs(tile, width)
    return pl.pallas_call(
        input_kernel,
        grid=(rows // tile,),
        out_shape=(
            jax.ShapeDtypeStruct((rows, width), F32),
            jax.ShapeDtypeStruct((1, width), F32),
        ),
        in_specs=[smem, row, column, single, row, row],
        out_specs=(row, single),
        compiler_params=params(),
        cost_estimate=pl.CostEstimate(
            flops=20 * rows * width, bytes_accessed=14 * rows * width, transcendentals=0
        ),
        name="input_back",
    )(order, values, scale, gain, carried, upstream)


def mixer_grad_kernel(ht, dt, pa, pb, ya, yb, *rest):
    ga, gb = rest[-2:]
    step = pl.program_id(0)

    @pl.when(step < 3)
    def _():
        ga[0] = nn(ht[...], pa[0]).astype(BF)
        gb[0] = nn(ht[...], pb[0]).astype(BF)

    @pl.when(step == 3)
    def _():
        ga[0] = nn(dt[...], ya[...]).astype(BF)
        gb[0] = nn(dt[...], yb[...]).astype(BF)


def mixer_grad(ht, dt, proj_grad, gated, first, second, deps):
    width, rows = ht.shape
    cols = gated.shape[1] // 4

    def column(block):
        return pl.BlockSpec((1, rows, cols), lambda k: (jnp.minimum(k, 2), 0, block))

    def gated_column(block):
        return pl.BlockSpec((rows, cols), lambda k: (0, block))

    out = pl.BlockSpec((1, width, cols), lambda k: (k, 0, 0))
    grad = jax.ShapeDtypeStruct((4, width, cols), BF)
    return pl.pallas_call(
        mixer_grad_kernel,
        grid=(4,),
        out_shape=(grad, grad),
        in_specs=[
            whole((width, rows)),
            whole((width, rows)),
            column(first),
            column(second),
            gated_column(first),
            gated_column(second),
        ]
        + [ANY] * len(deps),
        out_specs=(out, out),
        compiler_params=params(),
        cost_estimate=pl.CostEstimate(
            flops=16 * rows * width * cols,
            bytes_accessed=4 * rows * width + 16 * width * cols + 16 * rows * cols,
            transcendentals=0,
        ),
        name="mixer_grad",
    )(ht, dt, proj_grad, proj_grad, gated, gated, *deps)


def update_kernel(*refs):
    count = (len(refs) - 12)
    totals, rest = refs[:count], refs[count:]
    wide, tall, wide_new, tall_new = rest[:3], rest[3:6], rest[6:9], rest[9:]
    for i, total in enumerate(totals):

        @pl.when(pl.program_id(0) == i)
        def _():
            last = total.shape[0] - 1
            new = adamw(wide[0][...], total[:last], wide[1][...], wide[2][...], RATE_MATRIX, DECAY)
            for ref, value in zip(wide_new, new):
                ref[...] = value
            grad = jnp.transpose(total[last])
            new = adamw(tall[0][...], grad, tall[1][...], tall[2][...], RATE_MATRIX, DECAY)
            for ref, value in zip(tall_new, new):
                ref[...] = value


def update(totals, wide, tall):
    if (wide[0].shape[2] // len(totals)) % 128:
        totals = [jnp.concatenate(totals, 2)]
    count = len(totals)
    planes, deep, cols = wide[0].shape
    part = cols // count
    wide_spec = pl.BlockSpec((planes, deep, part), lambda i: (0, 0, i))
    tall_spec = pl.BlockSpec((part, deep), lambda i: (i, 0))
    return pl.pallas_call(
        update_kernel,
        grid=(count,),
        out_shape=tuple(jax.ShapeDtypeStruct(a.shape, F32) for a in wide + tall),
        in_specs=[whole(total.shape) for total in totals] + [wide_spec] * 3 + [tall_spec] * 3,
        out_specs=(wide_spec,) * 3 + (tall_spec,) * 3,
        compiler_params=params(),
        cost_estimate=pl.CostEstimate(
            flops=20 * (planes + 1) * deep * cols,
            bytes_accessed=28 * (planes + 1) * deep * cols,
            transcendentals=(planes + 1) * deep * cols,
        ),
        name="update",
    )(*totals, *wide, *tall)


def local(
    tokens,
    segments,
    cotangent,
    mixer_in,
    mixer_out,
    gate_up,
    down_proj,
    norm_gains,
    conv_kernel,
    first_mixer_in,
    second_mixer_in,
    first_mixer_out,
    second_mixer_out,
    first_gate_up,
    second_gate_up,
    first_down_proj,
    second_down_proj,
    first_norm_gains,
    second_norm_gains,
    first_conv_kernel,
    second_conv_kernel,
):
    dp_size, t_size = lax.axis_size("dp"), lax.axis_size("tensor")
    dp_index, t_index = lax.axis_index("dp"), lax.axis_index("tensor")
    rows, length = tokens.shape[0], segments.shape[1]
    order = dp_index ^ jnp.array([rotate_left(j, dp_size) for j in range(dp_size)], jnp.int32)

    z_bits, t_bits = low_bits()
    wide, cut = 1, 2
    ffn_cols = gate_up.shape[2] // PARTS
    own = [join([mixer_in.astype(BF), mixer_out.T.astype(BF)[None]], 0)]
    for i in range(PARTS):
        cols = slice(i * ffn_cols, (i + 1) * ffn_cols)
        own.append(join([gate_up[:, :, cols].astype(BF), down_proj[cols].T.astype(BF)[None]], 0))

    def deepen(places, others, axis, bit, along):
        got = phase(others, [(own[i], axis, bit) for i in places])
        for i, part in zip(places, got):
            own[i] = join([own[i], part], along)
        return got

    def first_rows(places, others):
        for bit in z_bits[:-1]:
            others = deepen(places, others, "dp", bit, wide)
        for bit in t_bits:
            others = deepen(places, others, "tensor", bit, cut)
        return others

    def by_x(value):
        return (value, "dp", 1)

    def by_y(value):
        return (value, "tensor", 2)

    def by_z(value):
        return (value, "dp", z_bits[-1])

    def other_core(value):
        return swap(value, "tensor", 1)

    xa, xb, ya, yb, zb, da, db = ({} for _ in range(7))

    def pieces_of(i):
        return [own[i], zb[i], xa[i], xb[i], ya[i], yb[i], da[i], db[i]]

    small = jnp.concatenate([norm_gains, conv_kernel], 0)[:, None, :]
    before = lax.ppermute(
        tokens[rows - HALO :], "tensor", [(i, i + 1) for i in range(t_size - 1)]
    )
    small_t = phase([], [(small, "tensor", code) for code in range(1, t_size)])
    last = first_rows([0, 1], [])
    small = join([small, *small_t], 1)
    small_x = phase([*last, small], [(small, "dp", 1)])
    xa[0], ya[0], zb[0] = got = phase(last, [by_x(own[0]), by_y(own[0]), by_z(own[0])])
    later = first_rows(range(2, PARTS + 1), last)
    small = join([small, *small_x], 1)
    small_z = phase([*got, small], [(small, "dp", code) for code in range(2, dp_size, 2)])
    xb[0], yb[0], da[0], ya[1], zb[1] = got = phase(
        [*got, *later], [by_x(zb[0]), by_y(zb[0]), by_x(ya[0]), by_y(own[1]), by_z(own[1])]
    )
    x_ext, cot = arrange(order, *ordered([tokens, before, cotangent], last))
    db[0], xa[1], zb[2], cot_other = phase(
        got[:3], [by_y(xb[0]), by_x(own[1]), by_z(own[2]), (cot, "tensor", 1)]
    )
    small = join([small, *small_z], 1)

    small = small.reshape(small.shape[0], dp_size, t_size, small.shape[2])
    for axis, index, size_axis in ((1, dp_index, dp_size), (2, t_index, t_size)):
        for i in range(size_axis.bit_length() - 1):
            shape = small.shape
            split = small.reshape(shape[:axis] + (size_axis >> (i + 1), 2, 1 << i) + shape[axis + 1 :])
            flipped = jnp.flip(split, axis + 1)
            small = jnp.where((index >> i) & 1 == 1, flipped, split).reshape(shape)
    small = small.reshape(small.shape[0], -1)
    block = small.shape[1] // dp_size
    gains = jnp.concatenate(
        [lax.dynamic_slice_in_dim(small[:2], order[j] * block, block, 1) for j in range(dp_size)], 1
    )
    channels = small.shape[1] // t_size
    codes = block_codes(t_size)
    kernel = jnp.concatenate(
        [
            lax.dynamic_slice_in_dim(small[2:], (t_index ^ code) * channels, channels, 1)
            for code in codes
        ],
        1,
    )

    masks = []
    for mask in lag_masks(segments.reshape(-1), length):
        padded = jnp.concatenate([mask, jnp.zeros((HALO, 1), F32)], 0)
        masks.append(lax.dynamic_slice_in_dim(padded, t_index * rows, rows + HALO, 0))

    extended = x_ext.astype(F32)
    scale_ext = rms_scale(extended)
    normed_ext = (extended * scale_ext * gains[0]).astype(BF)
    c = join([cot, cot_other], 0)
    ct = c.T
    (normed_ext,) = ordered([normed_ext], [c, ct])
    values, scale_one, normed_one = extended[HALO:], scale_ext[HALO:], normed_ext[HALO:]
    near, far = join(pieces_of(0)[:4], wide), join(pieces_of(0)[4:], wide)
    wm = [near, other_core(near), far, other_core(far)]
    got = phase(
        [db[0], xa[1], zb[1], ya[1], zb[2]],
        [by_x(zb[1]), by_y(zb[1]), by_x(ya[1]), by_y(own[2]), by_z(own[3])],
    )
    wm_all = jnp.concatenate(wm, 2)
    win_all, wout_all = wm_all[:3], wm_all[3]
    projected = mm("td,kdc->ktc", normed_ext, win_all)
    part_b, part_c, part_x = projected[0], projected[1][HALO:], projected[2]
    product_ext = part_b * part_x
    part_b, part_x = part_b[HALO:], part_x[HALO:]
    product = product_ext[HALO:]
    convolved = kernel[0] * product
    for shift in range(1, KW):
        convolved = convolved + kernel[shift] * masks[shift - 1][:rows] * shift_rows(
            product_ext, HALO - shift, rows
        )
    gated = (part_c * convolved).astype(BF)
    (gated,) = ordered([gated], got)
    middle = values + mm("tc,dc->td", gated, wout_all)
    scale_two = rms_scale(middle)
    normed_two = (middle * scale_two * gains[1]).astype(BF)

    normed_other = other_core(normed_two)
    tokens_both = (normed_two, normed_other, normed_two.T, normed_other.T, c, ct)
    sums, grads = [], {}
    xb[1], yb[1], da[1], ya[2], zb[3] = got = ordered(got, [normed_two])
    db[1], xa[2] = got = phase(got, [by_y(xb[1]), by_x(own[2])])

    def run(i):
        nonlocal sums
        grads[i], sums = ffn(tokens_both, pieces_of(i), list(sums))
        return grads[i]

    got = phase(got, [by_x(zb[2]), by_y(zb[2]), by_x(ya[2]), by_y(own[3])])
    xb[2], yb[2], da[2], ya[3] = got = ordered(got, run(1)[:1])
    db[2], xa[3] = got = phase(got, [by_y(xb[2]), by_x(own[3])])

    axa, axb, aya, ayb, ada, adb = ({} for _ in range(6))

    def sum_xb(i):
        return by_x(plus(grads[i][3], adb[i]))

    def sum_ya(i):
        return by_y(plus(grads[i][4], ada[i]))

    got = phase(got, [by_x(zb[3]), by_y(zb[3]), by_x(ya[3]), by_y(grads[1][5])])
    xb[3], yb[3], da[3], ayb[1] = got = ordered(got, run(2)[:1])
    db[3], ada[1] = got = phase(got, [by_y(xb[3]), by_x(grads[1][6])])
    one_t = normed_one.T
    (db[3],) = ordered([db[3]], [ada[1], one_t])
    got = phase(
        got, [by_x(grads[1][2]), by_y(grads[1][7]), by_x(grads[2][6]), by_y(grads[2][7])]
    )
    axa[1], adb[1], ada[2], adb[2] = got = ordered(got, run(3)[:1])
    branch, back = ordered(sums, got)
    branch_in, back_in = [other_core(value[rows:].astype(BF)) for value in (branch, back)]
    deps = got
    got = phase(got, [sum_xb(1), sum_ya(1), by_x(grads[2][2]), by_y(grads[2][5])])
    block_out, middle_grad, mixed_grad, gain_two_grad = middle_back(
        order, middle, scale_two, gains[1:2], cot, [branch, branch_in], [back, back_in], deps
    )

    gated_grad = mm("td,dc->tc", mixed_grad, wout_all)
    axb[1], aya[1], axa[2], ayb[2] = got = ordered(got, [gated_grad])
    (gated_grad,) = ordered([gated_grad], got)

    def sum_b(i):
        return by_z(functools.reduce(jnp.add, [v.astype(F32) for v in (grads[i][1], axb[i], ayb[i])]).astype(BF))

    got = phase(
        got, [sum_xb(2), sum_ya(2), by_x(grads[3][6]), by_y(grads[3][7]), sum_b(1)]
    )
    conv_grad = gated_grad * part_c
    after_rel = lax.ppermute(
        conv_grad[:8], "tensor", [(i + 1, i) for i in range(t_size - 1)]
    )
    after = jnp.concatenate(
        [
            lax.dynamic_slice_in_dim(
                after_rel,
                block_place(code ^ t_index ^ (t_index + 1), t_size) % t_size * channels,
                channels,
                1,
            )
            for code in codes
        ],
        1,
    )
    c_grad = gated_grad * convolved
    conv_ext = jnp.concatenate([conv_grad, after], 0)
    kernel_rows = [jnp.sum(conv_grad * product, axis=0)]
    product_grad = kernel[0] * conv_grad
    for shift in range(1, KW):
        masked = masks[shift - 1][: rows + 8] * conv_ext
        kernel_rows.append(
            jnp.sum(masked[:rows] * shift_rows(product_ext, HALO - shift, rows), axis=0)
        )
        product_grad = product_grad + kernel[shift] * shift_rows(masked, shift, rows)
    proj_grad = jnp.stack([product_grad * part_x, c_grad, product_grad * part_b], 0).astype(BF)
    zs = {}
    axb[2], aya[2], ada[3], adb[3], zs[1] = got = ordered(got, [proj_grad])
    mixed_t = mixed_grad.T
    m_near_core, m_far_core = mixer_grad(one_t, mixed_t, proj_grad, gated, 1, 3, [axb[2], aya[2], ada[3], adb[3]])
    m_in = [other_core(m_far_core), other_core(m_near_core)]
    got = phase(
        [*got, *m_in],
        [by_x(grads[3][2]), sum_xb(3), by_y(grads[3][5]), sum_ya(3), sum_b(2)],
    )
    m_near, m_far = mixer_grad(one_t, mixed_t, proj_grad, gated, 0, 2, m_in)
    axa[3], axb[3], ayb[3], aya[3], zs[2] = got = ordered(got, [m_far])
    deep = m_near.shape[wide] // 4
    grads[0] = [
        plus(
            lax.slice_in_dim(value, i * deep, (i + 1) * deep, axis=wide),
            lax.slice_in_dim(other, i * deep, (i + 1) * deep, axis=wide),
        )
        for value, other in ((m_near, m_in[1]), (m_far, m_in[0]))
        for i in range(4)
    ]

    terms, steps = {}, [("tensor", bit, cut) for bit in reversed(t_bits)]
    steps += [("dp", bit, wide) for bit in reversed(z_bits[:-1])]

    def sum_a(i):
        terms[i] = [grads[i][0], axa[i], aya[i], zs[i]]

    def fold_send(i, step):
        axis, bit, along = steps[step]
        return (fold(terms[i], along), axis, bit)

    def folded(i, step, got):
        along = steps[step][2]
        terms[i] = [halves(term, along)[0] for term in terms[i]] + [got]

    sum_a(1)
    got = phase(
        got, [by_x(grads[0][6]), by_x(grads[0][2]), by_y(grads[0][7]), by_y(grads[0][5]), sum_b(3)]
    )
    ada[0], axa[0], adb[0], ayb[0], zs[3] = last = got

    (late,) = ordered([proj_grad], grads[0][:1])
    normed_one_grad = mm("ktc,kdc->td", late, win_all)
    grad_input, gain_one_grad = input_back(
        order, x_ext[HALO:], scale_one, gains[:1], middle_grad, normed_one_grad
    )

    gain_rel = jnp.concatenate([gain_one_grad, gain_two_grad], 0)
    kernel_rel = jnp.stack(kernel_rows, 0)
    gain_sums = jnp.concatenate(
        [
            lax.dynamic_slice_in_dim(gain_rel, rotate_right(dp_index ^ q, dp_size) * block, block, 1)
            for q in range(dp_size)
        ],
        1,
    )
    kernel_sums = jnp.concatenate(
        [
            lax.dynamic_slice_in_dim(
                kernel_rel, block_place(t_index ^ q, t_size) * channels, channels, 1
            )
            for q in range(t_size)
        ],
        1,
    )
    total_small = jnp.concatenate([gain_sums, kernel_sums], 0)

    def small_step(value, others, axis, codes):
        return functools.reduce(jnp.add, [value, *phase(others, [(value, axis, code) for code in codes])])

    sum_a(2)
    sum_a(3)
    total_small = small_step(total_small, last, "tensor", range(1, t_size))
    got = phase([*last, gain_one_grad], [sum_xb(0), sum_ya(0), *[fold_send(i, 0) for i in range(1, PARTS + 1)]])
    axb[0], aya[0] = got[:2]
    for i in range(1, PARTS + 1):
        folded(i, 0, got[i + 1])
    total_small = small_step(total_small, got[:2], "dp", [1])
    (zs[0],) = phase(got[:2], [sum_b(0)])
    for step in range(1, len(steps)):
        got = phase(got, [fold_send(i, step) for i in range(1, PARTS + 1)])
        for i in range(1, PARTS + 1):
            folded(i, step, got[i - 1])
    sum_a(0)
    total_small = small_step(total_small, [zs[0]], "dp", range(2, dp_size, 2))
    for step in range(len(steps)):
        (got,) = phase([], [fold_send(0, step)])
        folded(0, step, got)
    own_width = norm_gains.shape[1]
    own_small = lax.dynamic_slice_in_dim(
        total_small, (dp_index * t_size + t_index) * own_width, own_width, 1
    )

    def total(i):
        return functools.reduce(jnp.add, [term.astype(F32) for term in terms[i]])

    ffn_new = update(
        [total(i) for i in range(1, PARTS + 1)],
        (gate_up, first_gate_up, second_gate_up),
        (down_proj, first_down_proj, second_down_proj),
    )
    mix_new = update(
        [total(0)], (mixer_in, first_mixer_in, second_mixer_in), (mixer_out, first_mixer_out, second_mixer_out)
    )
    gains_new = adamw(norm_gains, own_small[:2], first_norm_gains, second_norm_gains, RATE_SMALL, 0.0)
    kernel_new = adamw(conv_kernel, own_small[2:], first_conv_kernel, second_conv_kernel, RATE_SMALL, DECAY)
    block_out, grad_input = to_natural(block_out, order), to_natural(grad_input, order)
    return (block_out, grad_input, *mix_new, *ffn_new, *gains_new, *kernel_new)


def solution(mesh):
    rows = P(("dp", "tensor"), None)
    in_w, out_w, small = P(None, "dp", "tensor"), P("tensor", "dp"), P(None, ("dp", "tensor"))
    return jax.shard_map(
        local,
        mesh=mesh,
        in_specs=(
            (rows, P("dp", None), rows, in_w, out_w, in_w, out_w, small, small)
            + (in_w,) * 2
            + (out_w,) * 2
            + (in_w,) * 2
            + (out_w,) * 2
            + (small,) * 4
        ),
        out_specs=(rows, rows)
        + (in_w,) * 3
        + (out_w,) * 3
        + (in_w,) * 3
        + (out_w,) * 3
        + (small,) * 6,
        check_vma=False,
    )
```

```python
import functools

import jax
import jax.numpy as jnp
from jax import lax
from jax.experimental import pallas as pl
from jax.experimental.pallas import tpu as pltpu
from jax.sharding import PartitionSpec as P

KW = 3
STEP = 10
HALO = 16
PARTS = 3

EPS_NORM = 1e-05
EPS_ADAM = 1e-08
BETA_FIRST = 0.9
BETA_SECOND = 0.95
RATE_MATRIX = 0.05
RATE_SMALL = 0.5
DECAY = 0.1

BF = jnp.bfloat16
F32 = jnp.float32


def swap(values, axis, bit):
    size = lax.axis_size(axis)
    return lax.ppermute(values, axis, [(i, i ^ bit) for i in range(size)])


def halves(values, axis):
    size = values.shape[axis] // 2
    return (
        lax.slice_in_dim(values, 0, size, axis=axis),
        lax.slice_in_dim(values, size, 2 * size, axis=axis),
    )


def low_bits():
    return (
        [2 << i for i in range((lax.axis_size("dp") // 2).bit_length() - 1)],
        [4 << i for i in range((lax.axis_size("tensor") // 4).bit_length() - 1)],
    )


def ordered(values, others):
    values = list(values)
    return list(lax.optimization_barrier((*values, *others)))[: len(values)]


def phase(others, sends):
    values = ordered([send[0] for send in sends], others)
    return [swap(value, axis, bit) for value, (_, axis, bit) in zip(values, sends)]


def join(parts, axis):
    return jnp.concatenate(parts, axis)


def fold(parts, wide):
    return functools.reduce(jnp.add, [halves(part, wide)[1].astype(F32) for part in parts]).astype(BF)


def plus(left, right):
    return (left.astype(F32) + right.astype(F32)).astype(BF)


def rotate_left(values, count):
    bits = count.bit_length() - 1
    return ((values << 1) | (values >> (bits - 1))) & (count - 1)


def rotate_right(values, count):
    bits = count.bit_length() - 1
    return ((values & 1) << (bits - 1)) | (values >> 1)


def block_codes(count):
    return [base ^ (e << 2) for base in (0, 1, 2, 3) for e in range(count // 4)]


def block_place(code, count):
    return (code & 3) * (count // 4) + (code >> 2)


def shift_rows(values, start, rows):
    return lax.slice_in_dim(values, start, start + rows, axis=0)


def lag_masks(seg_flat, length):
    positions = jnp.arange(seg_flat.shape[0], dtype=jnp.int32) % length
    masks = []
    for shift in range(1, KW):
        before = jnp.concatenate([jnp.zeros((shift,), seg_flat.dtype), seg_flat[:-shift]], 0)
        same = (positions >= shift) & (seg_flat == before)
        masks.append(jnp.where(same, 1.0, 0.0).astype(F32)[:, None])
    return masks


def rms_scale(values):
    return lax.rsqrt(jnp.mean(values * values, axis=-1, keepdims=True) + EPS_NORM)


def adamw(param, grad, first, second, rate, decay):
    first_new = BETA_FIRST * first + (1.0 - BETA_FIRST) * grad
    second_new = BETA_SECOND * second + (1.0 - BETA_SECOND) * grad * grad
    first_hat = first_new / (1.0 - BETA_FIRST**STEP)
    second_hat = second_new / (1.0 - BETA_SECOND**STEP)
    return (
        param - rate * (first_hat / (jnp.sqrt(second_hat) + EPS_ADAM) + decay * param),
        first_new,
        second_new,
    )


def mm(spec, left, right, out=F32):
    return jnp.einsum(spec, left, right, preferred_element_type=F32).astype(out)


ANY = pl.BlockSpec(memory_space=pl.ANY)
LIMIT = 26 * 1024 * 1024


def params(count=1):
    return pltpu.CompilerParams(
        vmem_limit_bytes=LIMIT, dimension_semantics=("arbitrary",) * count
    )


def whole(shape):
    return pl.BlockSpec(shape, lambda *_: (0,) * len(shape), pipeline_mode=pl.Buffered(1))


def arrange_kernel(order, tokens, before, cot, x_out, cot_out):
    count = order.shape[0]
    width = tokens.shape[1] // count
    for j in range(count):
        spot = pl.ds(pl.multiple_of(order[j] * width, width), width)
        own = pl.ds(j * width, width)
        x_out[:HALO, own] = before[:, spot]
        x_out[HALO:, own] = tokens[:, spot]
        cot_out[:, own] = cot[:, spot]


def pick_blocks(values, places):
    count = places.shape[0]
    width = values.shape[1] // count
    return jnp.concatenate(
        [lax.dynamic_slice_in_dim(values, places[j] * width, width, 1) for j in range(count)], 1
    )


def narrow(order, width):
    return (width // order.shape[0]) % 128 != 0


def to_natural(values, order):
    if not narrow(order, values.shape[1]):
        return values
    return pick_blocks(values, jnp.argsort(order))


def arrange(order, tokens, before, cot):
    rows, width = tokens.shape
    if narrow(order, width):
        extended = jnp.concatenate([before, tokens], 0)
        return pick_blocks(extended, order), pick_blocks(cot, order)
    vmem = pl.BlockSpec(memory_space=pltpu.VMEM)
    return pl.pallas_call(
        arrange_kernel,
        out_shape=(
            jax.ShapeDtypeStruct((rows + HALO, width), BF),
            jax.ShapeDtypeStruct((rows, width), BF),
        ),
        in_specs=[pl.BlockSpec(memory_space=pltpu.SMEM), vmem, vmem, vmem],
        out_specs=(vmem, vmem),
        compiler_params=pltpu.CompilerParams(vmem_limit_bytes=LIMIT),
        name="arrange",
    )(order, tokens, before, cot)


def nt(left, right):
    return lax.dot_general(left, right, (((1,), (1,)), ((), ())), preferred_element_type=F32)


def nn(left, right):
    return jnp.dot(left, right, preferred_element_type=F32)


def ffn_kernel(first, final, *refs):
    tokens, pieces, rest = refs[:8], refs[8:16], refs[16:]
    h, ht, c, ct = tokens[:2], tokens[2:4], tokens[4:6], tokens[6:]
    branch, w, act, dgate, dup = rest[-5:]
    back, outs = rest[-6], rest[: -6] if first else rest[1:-6]
    grads, branch_own, branch_other = outs[:8], outs[8], outs[9]
    deep, half = pieces[0].shape[1:]
    spots = [
        (pl.ds(i % 4 * deep, deep), pl.ds(i // 4 * half, half)) for i in range(8)
    ]
    own = h[0].shape[0]
    tall = 384

    @pl.when(pl.program_id(0) == 0)
    def _():
        branch[...] = jnp.zeros_like(branch)
        back[...] = jnp.zeros_like(back) if first else rest[0][...]

    for piece, (deep_span, span) in zip(pieces, spots):
        w[:, deep_span, span] = piece[...]
    for start in range(0, 2 * own, tall):
        span, part = pl.ds(start, tall), pl.ds(start % own, tall)
        gate = nn(h[start // own][part, :], w[0])
        up = nn(h[start // own][part, :], w[1])
        da = nn(c[start // own][part, :], w[2])
        sigma = 1.0 / (1.0 + jnp.exp(-gate))
        silu = gate * sigma
        act[span, :] = (silu * up).astype(BF)
        dup[span, :] = (da * silu).astype(BF)
        dgate[span, :] = (da * up * (sigma + silu * (1.0 - sigma))).astype(BF)
    for k, (left, right) in enumerate(((ht, dgate), (ht, dup), (ct, act))):
        grad = (nn(left[0][...], right[:own, :]) + nn(left[1][...], right[own:, :])).astype(BF)
        for i, out in enumerate(grads):
            out[k] = grad[i % 4 * deep : (i % 4 + 1) * deep, i // 4 * half : (i // 4 + 1) * half]
    for start in range(0, 2 * own, tall):
        span = pl.ds(start, tall)
        branch[span, :] += nt(act[span, :], w[2])
        back[span, :] += nt(dgate[span, :], w[0]) + nt(dup[span, :], w[1])

    @pl.when(pl.program_id(0) == pl.num_programs(0) - 1)
    def _():
        branch_own[...] = branch[:own, :].astype(BF)
        branch_other[...] = branch[own:, :].astype(BF)
        if final:
            outs[10][...] = back[own:, :].astype(BF)


def ffn(tokens, pieces, sums, final):
    own, width = tokens[0].shape
    rows = 2 * own
    planes, deep, cols = pieces[0].shape
    tile = 128
    block = pl.BlockSpec((planes, deep, tile), lambda j: (0, 0, j))
    vmem = pl.BlockSpec(memory_space=pltpu.VMEM)
    grad = pltpu.HBM(pieces[0].shape, BF)
    part = jax.ShapeDtypeStruct((rows, width), F32)
    other = [pltpu.HBM((own, width), BF)] * (3 if final else 2)
    count = 8 + len(other)
    out = pl.pallas_call(
        functools.partial(ffn_kernel, not sums, final),
        grid=(cols // tile,),
        out_shape=(*[grad] * 8, *other, part),
        in_specs=[vmem] * 8 + [block] * 8 + [vmem] * len(sums),
        out_specs=(*[block] * 8, *[whole((own, width))] * len(other), vmem),
        input_output_aliases={16: count} if sums else {},
        scratch_shapes=[pltpu.VMEM((rows, width), F32), pltpu.VMEM((planes, width, 2 * tile), BF)]
        + [pltpu.VMEM((rows, 2 * tile), BF)] * 3,
        compiler_params=params(),
        cost_estimate=pl.CostEstimate(
            flops=36 * rows * width * cols,
            bytes_accessed=24 * width * cols,
            transcendentals=2 * rows * cols,
        ),
        name="ffn",
    )(*tokens, *pieces, *sums)
    return out[:8], out[8:10], out[10:-1], out[-1:]


def middle_kernel(order, middle, scale, gain, cot, *rest):
    block_out, grad, grad_low, gain_grad = rest[-4:]
    branches, backs = rest[: len(rest) - 6], rest[-6:-4]
    x2, r2, up = middle[...], scale[...], backs[0][...].astype(F32)
    for ref in backs[1:]:
        up = up + ref[...].astype(F32)
    total = x2
    for ref in branches:
        total = total + ref[...].astype(F32)
    store_natural(order, block_out, total.astype(BF))
    norm_back(x2, r2, gain, up, cot[...].astype(F32), grad, gain_grad)
    grad_low[...] = grad[...].astype(BF)


def store_natural(order, out, total):
    count = order.shape[0]
    if narrow(order, total.shape[1]):
        out[...] = total
        return
    width = total.shape[1] // count
    for j in range(count):
        spot = pl.ds(pl.multiple_of(order[j] * width, width), width)
        out[:, spot] = total[:, j * width : (j + 1) * width]


def norm_back(values, scale, gain, upstream, carried, out, gain_grad, order=None):
    scaled = upstream * gain[...]
    mean = jnp.mean(scaled * values, axis=-1, keepdims=True)
    total = carried + scale * scaled - values * (scale * scale * scale * mean)
    if order is None:
        out[...] = total
    else:
        store_natural(order, out, total)
    sums = jnp.sum(upstream * values * scale, axis=0, keepdims=True)

    @pl.when(pl.program_id(0) == 0)
    def _():
        gain_grad[...] = sums

    @pl.when(pl.program_id(0) > 0)
    def _():
        gain_grad[...] += sums


def row_specs(tile, width):
    return (
        pl.BlockSpec(memory_space=pltpu.SMEM),
        pl.BlockSpec((tile, width), lambda i: (i, 0)),
        pl.BlockSpec((tile, 1), lambda i: (i, 0)),
        pl.BlockSpec((1, width), lambda i: (0, 0)),
    )


def middle_back(order, middle, scale, gain, cot, branches, backs, deps):
    rows, width = middle.shape
    tile = 128
    smem, row, column, single = row_specs(tile, width)
    count = 5 + len(branches) + len(backs)

    def kernel(*refs):
        middle_kernel(*refs[:count], *refs[count + len(deps) :])

    return pl.pallas_call(
        kernel,
        grid=(rows // tile,),
        out_shape=(
            jax.ShapeDtypeStruct((rows, width), BF),
            jax.ShapeDtypeStruct((rows, width), F32),
            jax.ShapeDtypeStruct((rows, width), BF),
            jax.ShapeDtypeStruct((1, width), F32),
        ),
        in_specs=[smem, row, column, single, row] + [row] * (count - 5) + [ANY] * len(deps),
        out_specs=(row, row, row, single),
        compiler_params=params(),
        cost_estimate=pl.CostEstimate(
            flops=30 * rows * width, bytes_accessed=(4 + 2 * count) * rows * width, transcendentals=0
        ),
        name="middle_back",
    )(order, middle, scale, gain, cot, *branches, *backs, *deps)


def input_kernel(order, values, scale, gain, carried, upstream, out, gain_grad):
    norm_back(
        values[...].astype(F32), scale[...], gain, upstream[...], carried[...], out, gain_grad, order
    )


def input_back(order, values, scale, gain, carried, upstream):
    rows, width = values.shape
    tile = 128
    smem, row, column, single = row_specs(tile, width)
    return pl.pallas_call(
        input_kernel,
        grid=(rows // tile,),
        out_shape=(
            jax.ShapeDtypeStruct((rows, width), F32),
            jax.ShapeDtypeStruct((1, width), F32),
        ),
        in_specs=[smem, row, column, single, row, row],
        out_specs=(row, single),
        compiler_params=params(),
        cost_estimate=pl.CostEstimate(
            flops=20 * rows * width, bytes_accessed=14 * rows * width, transcendentals=0
        ),
        name="input_back",
    )(order, values, scale, gain, carried, upstream)


def mixer_grad_kernel(ht, dt, pa, pb, ya, yb, *rest):
    ga, gb = rest[-2:]
    step = pl.program_id(0)

    @pl.when(step < 3)
    def _():
        ga[0] = nn(ht[...], pa[0]).astype(BF)
        gb[0] = nn(ht[...], pb[0]).astype(BF)

    @pl.when(step == 3)
    def _():
        ga[0] = nn(dt[...], ya[...]).astype(BF)
        gb[0] = nn(dt[...], yb[...]).astype(BF)


def mixer_grad(ht, dt, proj_grad, gated, first, second, deps):
    width, rows = ht.shape
    cols = gated.shape[1] // 4

    def column(block):
        return pl.BlockSpec((1, rows, cols), lambda k: (jnp.minimum(k, 2), 0, block))

    def gated_column(block):
        return pl.BlockSpec((rows, cols), lambda k: (0, block))

    out = pl.BlockSpec((1, width, cols), lambda k: (k, 0, 0))
    grad = jax.ShapeDtypeStruct((4, width, cols), BF)
    return pl.pallas_call(
        mixer_grad_kernel,
        grid=(4,),
        out_shape=(grad, grad),
        in_specs=[
            whole((width, rows)),
            whole((width, rows)),
            column(first),
            column(second),
            gated_column(first),
            gated_column(second),
        ]
        + [ANY] * len(deps),
        out_specs=(out, out),
        compiler_params=params(),
        cost_estimate=pl.CostEstimate(
            flops=16 * rows * width * cols,
            bytes_accessed=4 * rows * width + 16 * width * cols + 16 * rows * cols,
            transcendentals=0,
        ),
        name="mixer_grad",
    )(ht, dt, proj_grad, proj_grad, gated, gated, *deps)


def update_kernel(*refs):
    count = (len(refs) - 12)
    totals, rest = refs[:count], refs[count:]
    wide, tall, wide_new, tall_new = rest[:3], rest[3:6], rest[6:9], rest[9:]
    for i, total in enumerate(totals):

        @pl.when(pl.program_id(0) == i)
        def _():
            last = total.shape[0] - 1
            new = adamw(wide[0][...], total[:last], wide[1][...], wide[2][...], RATE_MATRIX, DECAY)
            for ref, value in zip(wide_new, new):
                ref[...] = value
            grad = jnp.transpose(total[last])
            new = adamw(tall[0][...], grad, tall[1][...], tall[2][...], RATE_MATRIX, DECAY)
            for ref, value in zip(tall_new, new):
                ref[...] = value


def update(totals, wide, tall):
    if (wide[0].shape[2] // len(totals)) % 128:
        totals = [jnp.concatenate(totals, 2)]
    count = len(totals)
    planes, deep, cols = wide[0].shape
    part = cols // count
    wide_spec = pl.BlockSpec((planes, deep, part), lambda i: (0, 0, i))
    tall_spec = pl.BlockSpec((part, deep), lambda i: (i, 0))
    return pl.pallas_call(
        update_kernel,
        grid=(count,),
        out_shape=tuple(jax.ShapeDtypeStruct(a.shape, F32) for a in wide + tall),
        in_specs=[whole(total.shape) for total in totals] + [wide_spec] * 3 + [tall_spec] * 3,
        out_specs=(wide_spec,) * 3 + (tall_spec,) * 3,
        compiler_params=params(),
        cost_estimate=pl.CostEstimate(
            flops=20 * (planes + 1) * deep * cols,
            bytes_accessed=28 * (planes + 1) * deep * cols,
            transcendentals=(planes + 1) * deep * cols,
        ),
        name="update",
    )(*totals, *wide, *tall)


def local(
    tokens,
    segments,
    cotangent,
    mixer_in,
    mixer_out,
    gate_up,
    down_proj,
    norm_gains,
    conv_kernel,
    first_mixer_in,
    second_mixer_in,
    first_mixer_out,
    second_mixer_out,
    first_gate_up,
    second_gate_up,
    first_down_proj,
    second_down_proj,
    first_norm_gains,
    second_norm_gains,
    first_conv_kernel,
    second_conv_kernel,
):
    dp_size, t_size = lax.axis_size("dp"), lax.axis_size("tensor")
    dp_index, t_index = lax.axis_index("dp"), lax.axis_index("tensor")
    rows, length = tokens.shape[0], segments.shape[1]
    order = dp_index ^ jnp.array([rotate_left(j, dp_size) for j in range(dp_size)], jnp.int32)

    z_bits, t_bits = low_bits()
    wide, cut = 1, 2
    ffn_cols = gate_up.shape[2] // PARTS
    own = [join([mixer_in.astype(BF), mixer_out.T.astype(BF)[None]], 0)]
    for i in range(PARTS):
        cols = slice(i * ffn_cols, (i + 1) * ffn_cols)
        own.append(join([gate_up[:, :, cols].astype(BF), down_proj[cols].T.astype(BF)[None]], 0))

    def deepen(places, others, axis, bit, along):
        got = phase(others, [(own[i], axis, bit) for i in places])
        for i, part in zip(places, got):
            own[i] = join([own[i], part], along)
        return got

    def first_rows(places, others):
        for bit in z_bits[:-1]:
            others = deepen(places, others, "dp", bit, wide)
        for bit in t_bits:
            others = deepen(places, others, "tensor", bit, cut)
        return others

    def by_x(value):
        return (value, "dp", 1)

    def by_y(value):
        return (value, "tensor", 2)

    def by_z(value):
        return (value, "dp", z_bits[-1])

    def other_core(value):
        return swap(value, "tensor", 1)

    xa, xb, ya, yb, zb, da, db = ({} for _ in range(7))

    def pieces_of(i):
        return [own[i], zb[i], xa[i], xb[i], ya[i], yb[i], da[i], db[i]]

    small = jnp.concatenate([norm_gains, conv_kernel], 0)[:, None, None, None, None, :]
    small_z = phase([], [(small, "dp", code) for code in range(2, dp_size, 2)])
    before = lax.ppermute(
        tokens[rows - HALO :], "tensor", [(i, i + 1) for i in range(t_size - 1)]
    )
    last = first_rows([0, 1], small_z)
    small = join([small, *small_z], 1)
    small = join([small, swap(small, "dp", 1)], 2)
    small = join([small, *[swap(small, "tensor", code) for code in range(2, t_size, 2)]], 3)
    small = join([small, swap(small, "tensor", 1)], 4)
    last = [*last, small, before]
    xa[0], ya[0], zb[0] = got = phase(last, [by_x(own[0]), by_y(own[0]), by_z(own[0])])
    later = first_rows(range(2, PARTS + 1), last)
    xb[0], yb[0], da[0], ya[1], zb[1] = got = phase(
        [*got, *later], [by_x(zb[0]), by_y(zb[0]), by_x(ya[0]), by_y(own[1]), by_z(own[1])]
    )
    x_ext, cot = arrange(order, *ordered([tokens, before, cotangent], last))
    db[0], xa[1], zb[2], cot_other = phase(
        got[:3], [by_y(xb[0]), by_x(own[1]), by_z(own[2]), (cot, "tensor", 1)]
    )
    small = small.reshape(small.shape[0], dp_size, t_size, small.shape[-1])
    for axis, index, size_axis in ((1, dp_index, dp_size), (2, t_index, t_size)):
        for i in range(size_axis.bit_length() - 1):
            shape = small.shape
            split = small.reshape(shape[:axis] + (size_axis >> (i + 1), 2, 1 << i) + shape[axis + 1 :])
            flipped = jnp.flip(split, axis + 1)
            small = jnp.where((index >> i) & 1 == 1, flipped, split).reshape(shape)
    small = small.reshape(small.shape[0], -1)
    block = small.shape[1] // dp_size
    gains = jnp.concatenate(
        [lax.dynamic_slice_in_dim(small[:2], order[j] * block, block, 1) for j in range(dp_size)], 1
    )
    channels = small.shape[1] // t_size
    codes = block_codes(t_size)
    kernel = jnp.concatenate(
        [
            lax.dynamic_slice_in_dim(small[2:], (t_index ^ code) * channels, channels, 1)
            for code in codes
        ],
        1,
    )

    masks = []
    for mask in lag_masks(segments.reshape(-1), length):
        padded = jnp.concatenate([mask, jnp.zeros((HALO, 1), F32)], 0)
        masks.append(lax.dynamic_slice_in_dim(padded, t_index * rows, rows + HALO, 0))

    extended = x_ext.astype(F32)
    scale_ext = rms_scale(extended)
    normed_ext = (extended * scale_ext * gains[0]).astype(BF)
    ct, ct_other = cot.T, cot_other.T
    (normed_ext,) = ordered([normed_ext], [ct, ct_other])
    values, scale_one, normed_one = extended[HALO:], scale_ext[HALO:], normed_ext[HALO:]
    near, far = join(pieces_of(0)[:4], wide), join(pieces_of(0)[4:], wide)
    wm = [near, other_core(near), far, other_core(far)]
    got = phase(
        [db[0], xa[1], zb[1], ya[1], zb[2]],
        [by_x(zb[1]), by_y(zb[1]), by_x(ya[1]), by_y(own[2]), by_z(own[3])],
    )
    wm_all = jnp.concatenate(wm, 2)
    win_all, wout_all = wm_all[:3], wm_all[3]
    projected = mm("td,kdc->ktc", normed_ext, win_all)
    part_b, part_c, part_x = projected[0], projected[1][HALO:], projected[2]
    product_ext = part_b * part_x
    part_b, part_x = part_b[HALO:], part_x[HALO:]
    product = product_ext[HALO:]
    convolved = kernel[0] * product
    for shift in range(1, KW):
        convolved = convolved + kernel[shift] * masks[shift - 1][:rows] * shift_rows(
            product_ext, HALO - shift, rows
        )
    gated = (part_c * convolved).astype(BF)
    (gated,) = ordered([gated], got)
    middle = values + mm("tc,dc->td", gated, wout_all)
    scale_two = rms_scale(middle)
    normed_two = (middle * scale_two * gains[1]).astype(BF)

    normed_other = other_core(normed_two)
    tokens_both = (normed_two, normed_other, normed_two.T, normed_other.T)
    tokens_both += (cot, cot_other, ct, ct_other)
    sums, grads, back_other, branch_own, branch_other = [], {}, [], [], []
    xb[1], yb[1], da[1], ya[2], zb[3] = got = ordered(got, [normed_two])
    db[1], xa[2] = got = phase(got, [by_y(xb[1]), by_x(own[2])])

    def run(i):
        nonlocal sums, back_other
        grads[i], branches, back_other, sums = ffn(tokens_both, pieces_of(i), list(sums), i == PARTS)
        branch_own.append(branches[0])
        branch_other.append(branches[1])
        return grads[i]

    got = phase(got, [by_x(zb[2]), by_y(zb[2]), by_x(ya[2]), by_y(own[3])])
    xb[2], yb[2], da[2], ya[3] = got = ordered(got, run(1)[:1])
    db[2], xa[3] = got = phase(got, [by_y(xb[2]), by_x(own[3])])

    axa, axb, aya, ayb, ada, adb = ({} for _ in range(6))

    def sum_xb(i):
        return by_x(plus(grads[i][3], adb[i]))

    def sum_ya(i):
        return by_y(plus(grads[i][4], ada[i]))

    got = phase(got, [by_x(zb[3]), by_y(zb[3]), by_x(ya[3]), by_y(grads[1][5])])
    xb[3], yb[3], da[3], ayb[1] = got = ordered(got, run(2)[:1])
    db[3], ada[1] = got = phase(got, [by_y(xb[3]), by_x(grads[1][6])])
    one_t = normed_one.T
    (db[3],) = ordered([db[3]], [ada[1], one_t])
    got = phase(
        got, [by_x(grads[1][2]), by_y(grads[1][7]), by_x(grads[2][6]), by_y(grads[2][7])]
    )
    axa[1], adb[1], ada[2], adb[2] = got = ordered(got, run(3)[:1])
    back_other, back = ordered([*back_other, *sums], got)
    back_in = other_core(back_other)
    branch_in = other_core(
        functools.reduce(jnp.add, [value.astype(F32) for value in branch_other]).astype(BF)
    )
    deps = got
    got = phase(got, [sum_xb(1), sum_ya(1), by_x(grads[2][2]), by_y(grads[2][5])])
    block_out, middle_grad, mixed_grad, gain_two_grad = middle_back(
        order, middle, scale_two, gains[1:2], cot, [*branch_own, branch_in], [back, back_in], deps
    )

    gated_grad = mm("td,dc->tc", mixed_grad, wout_all)
    axb[1], aya[1], axa[2], ayb[2] = got = ordered(got, [gated_grad])
    (gated_grad,) = ordered([gated_grad], got)

    def sum_b(i):
        return by_z(functools.reduce(jnp.add, [v.astype(F32) for v in (grads[i][1], axb[i], ayb[i])]).astype(BF))

    got = phase(
        got, [sum_xb(2), sum_ya(2), by_x(grads[3][6]), by_y(grads[3][7]), sum_b(1)]
    )
    conv_grad = gated_grad * part_c
    after_rel = lax.ppermute(
        conv_grad[:8], "tensor", [(i + 1, i) for i in range(t_size - 1)]
    )
    after = jnp.concatenate(
        [
            lax.dynamic_slice_in_dim(
                after_rel,
                block_place(code ^ t_index ^ (t_index + 1), t_size) % t_size * channels,
                channels,
                1,
            )
            for code in codes
        ],
        1,
    )
    c_grad = gated_grad * convolved
    conv_ext = jnp.concatenate([conv_grad, after], 0)
    kernel_rows = [jnp.sum(conv_grad * product, axis=0)]
    product_grad = kernel[0] * conv_grad
    for shift in range(1, KW):
        masked = masks[shift - 1][: rows + 8] * conv_ext
        kernel_rows.append(
            jnp.sum(masked[:rows] * shift_rows(product_ext, HALO - shift, rows), axis=0)
        )
        product_grad = product_grad + kernel[shift] * shift_rows(masked, shift, rows)
    proj_grad = jnp.stack([product_grad * part_x, c_grad, product_grad * part_b], 0).astype(BF)
    zs = {}
    axb[2], aya[2], ada[3], adb[3], zs[1] = got = ordered(got, [proj_grad])
    mixed_t = mixed_grad.T
    m_near_core, m_far_core = mixer_grad(one_t, mixed_t, proj_grad, gated, 1, 3, [axb[2], aya[2], ada[3], adb[3]])
    m_in = [other_core(m_far_core), other_core(m_near_core)]
    got = phase(
        [*got, *m_in],
        [by_x(grads[3][2]), sum_xb(3), by_y(grads[3][5]), sum_ya(3), sum_b(2)],
    )
    m_near, m_far = mixer_grad(one_t, mixed_t, proj_grad, gated, 0, 2, m_in)
    axa[3], axb[3], ayb[3], aya[3], zs[2] = got = ordered(got, [m_far])
    deep = m_near.shape[wide] // 4
    grads[0] = [
        plus(
            lax.slice_in_dim(value, i * deep, (i + 1) * deep, axis=wide),
            lax.slice_in_dim(other, i * deep, (i + 1) * deep, axis=wide),
        )
        for value, other in ((m_near, m_in[1]), (m_far, m_in[0]))
        for i in range(4)
    ]

    terms, steps = {}, [("tensor", bit, cut) for bit in reversed(t_bits)]
    steps += [("dp", bit, wide) for bit in reversed(z_bits[:-1])]

    def sum_a(i):
        terms[i] = [grads[i][0], axa[i], aya[i], zs[i]]

    def fold_send(i, step):
        axis, bit, along = steps[step]
        return (fold(terms[i], along), axis, bit)

    def folded(i, step, got):
        along = steps[step][2]
        terms[i] = [halves(term, along)[0] for term in terms[i]] + [got]

    sum_a(1)
    got = phase(
        got, [by_x(grads[0][6]), by_x(grads[0][2]), by_y(grads[0][7]), by_y(grads[0][5]), sum_b(3)]
    )
    ada[0], axa[0], adb[0], ayb[0], zs[3] = last = got

    (late,) = ordered([proj_grad], grads[0][:1])
    normed_one_grad = mm("ktc,kdc->td", late, win_all)
    grad_input, gain_one_grad = input_back(
        order, x_ext[HALO:], scale_one, gains[:1], middle_grad, normed_one_grad
    )

    gain_rel = jnp.concatenate([gain_one_grad, gain_two_grad], 0)
    kernel_rel = jnp.stack(kernel_rows, 0)
    gain_sums = jnp.concatenate(
        [
            lax.dynamic_slice_in_dim(gain_rel, rotate_right(dp_index ^ q, dp_size) * block, block, 1)
            for q in range(dp_size)
        ],
        1,
    )
    kernel_sums = jnp.concatenate(
        [
            lax.dynamic_slice_in_dim(
                kernel_rel, block_place(t_index ^ q, t_size) * channels, channels, 1
            )
            for q in range(t_size)
        ],
        1,
    )
    total_small = jnp.concatenate([gain_sums, kernel_sums], 0)

    def small_step(value, others, axis, codes):
        return functools.reduce(jnp.add, [value, *phase(others, [(value, axis, code) for code in codes])])

    sum_a(2)
    sum_a(3)
    total_small = small_step(total_small, last, "tensor", range(1, t_size))
    got = phase([*last, gain_one_grad], [sum_xb(0), sum_ya(0), *[fold_send(i, 0) for i in range(1, PARTS + 1)]])
    axb[0], aya[0] = got[:2]
    for i in range(1, PARTS + 1):
        folded(i, 0, got[i + 1])
    total_small = small_step(total_small, got[:2], "dp", [1])
    (zs[0],) = phase(got[:2], [sum_b(0)])
    for step in range(1, len(steps)):
        got = phase(got, [fold_send(i, step) for i in range(1, PARTS + 1)])
        for i in range(1, PARTS + 1):
            folded(i, step, got[i - 1])
    sum_a(0)
    total_small = small_step(total_small, [zs[0]], "dp", range(2, dp_size, 2))
    for step in range(len(steps)):
        (got,) = phase([], [fold_send(0, step)])
        folded(0, step, got)
    own_width = norm_gains.shape[1]
    own_small = lax.dynamic_slice_in_dim(
        total_small, (dp_index * t_size + t_index) * own_width, own_width, 1
    )

    def total(i):
        return functools.reduce(jnp.add, [term.astype(F32) for term in terms[i]])

    ffn_new = update(
        [total(i) for i in range(1, PARTS + 1)],
        (gate_up, first_gate_up, second_gate_up),
        (down_proj, first_down_proj, second_down_proj),
    )
    mix_new = update(
        [total(0)], (mixer_in, first_mixer_in, second_mixer_in), (mixer_out, first_mixer_out, second_mixer_out)
    )
    gains_new = adamw(norm_gains, own_small[:2], first_norm_gains, second_norm_gains, RATE_SMALL, 0.0)
    kernel_new = adamw(conv_kernel, own_small[2:], first_conv_kernel, second_conv_kernel, RATE_SMALL, DECAY)
    block_out, grad_input = to_natural(block_out, order), to_natural(grad_input, order)
    return (block_out, grad_input, *mix_new, *ffn_new, *gains_new, *kernel_new)


def solution(mesh):
    rows = P(("dp", "tensor"), None)
    in_w, out_w, small = P(None, "dp", "tensor"), P("tensor", "dp"), P(None, ("dp", "tensor"))
    return jax.shard_map(
        local,
        mesh=mesh,
        in_specs=(
            (rows, P("dp", None), rows, in_w, out_w, in_w, out_w, small, small)
            + (in_w,) * 2
            + (out_w,) * 2
            + (in_w,) * 2
            + (out_w,) * 2
            + (small,) * 4
        ),
        out_specs=(rows, rows)
        + (in_w,) * 3
        + (out_w,) * 3
        + (in_w,) * 3
        + (out_w,) * 3
        + (small,) * 6,
        check_vma=False,
    )
```

```python
import functools

import jax
import jax.numpy as jnp
from jax import lax
from jax.experimental import pallas as pl
from jax.experimental.pallas import tpu as pltpu
from jax.sharding import PartitionSpec as P

KW = 3
STEP = 10
HALO = 16
PARTS = 3

EPS_NORM = 1e-05
EPS_ADAM = 1e-08
BETA_FIRST = 0.9
BETA_SECOND = 0.95
RATE_MATRIX = 0.05
RATE_SMALL = 0.5
DECAY = 0.1

BF = jnp.bfloat16
F32 = jnp.float32


def swap(values, axis, bit):
    size = lax.axis_size(axis)
    return lax.ppermute(values, axis, [(i, i ^ bit) for i in range(size)])


def halves(values, axis):
    size = values.shape[axis] // 2
    return (
        lax.slice_in_dim(values, 0, size, axis=axis),
        lax.slice_in_dim(values, size, 2 * size, axis=axis),
    )


def low_bits():
    return (
        [2 << i for i in range((lax.axis_size("dp") // 2).bit_length() - 1)],
        [4 << i for i in range((lax.axis_size("tensor") // 4).bit_length() - 1)],
    )


def ordered(values, others):
    values = list(values)
    return list(lax.optimization_barrier((*values, *others)))[: len(values)]


def phase(others, sends):
    values = ordered([send[0] for send in sends], others)
    return [swap(value, axis, bit) for value, (_, axis, bit) in zip(values, sends)]


def join(parts, axis):
    return jnp.concatenate(parts, axis)


def fold(parts, wide):
    return functools.reduce(jnp.add, [halves(part, wide)[1].astype(F32) for part in parts]).astype(BF)


def plus(left, right):
    return (left.astype(F32) + right.astype(F32)).astype(BF)


def rotate_left(values, count):
    bits = count.bit_length() - 1
    return ((values << 1) | (values >> (bits - 1))) & (count - 1)


def rotate_right(values, count):
    bits = count.bit_length() - 1
    return ((values & 1) << (bits - 1)) | (values >> 1)


def block_codes(count):
    return [base ^ (e << 2) for base in (0, 1, 2, 3) for e in range(count // 4)]


def block_place(code, count):
    return (code & 3) * (count // 4) + (code >> 2)


def shift_rows(values, start, rows):
    return lax.slice_in_dim(values, start, start + rows, axis=0)


def lag_masks(seg_flat, length):
    positions = jnp.arange(seg_flat.shape[0], dtype=jnp.int32) % length
    masks = []
    for shift in range(1, KW):
        before = jnp.concatenate([jnp.zeros((shift,), seg_flat.dtype), seg_flat[:-shift]], 0)
        same = (positions >= shift) & (seg_flat == before)
        masks.append(jnp.where(same, 1.0, 0.0).astype(F32)[:, None])
    return masks


def rms_scale(values):
    return lax.rsqrt(jnp.mean(values * values, axis=-1, keepdims=True) + EPS_NORM)


def adamw(param, grad, first, second, rate, decay):
    first_new = BETA_FIRST * first + (1.0 - BETA_FIRST) * grad
    second_new = BETA_SECOND * second + (1.0 - BETA_SECOND) * grad * grad
    first_hat = first_new / (1.0 - BETA_FIRST**STEP)
    second_hat = second_new / (1.0 - BETA_SECOND**STEP)
    return (
        param - rate * (first_hat / (jnp.sqrt(second_hat) + EPS_ADAM) + decay * param),
        first_new,
        second_new,
    )


def mm(spec, left, right, out=F32):
    return jnp.einsum(spec, left, right, preferred_element_type=F32).astype(out)


ANY = pl.BlockSpec(memory_space=pl.ANY)
LIMIT = 26 * 1024 * 1024


def params(count=1):
    return pltpu.CompilerParams(
        vmem_limit_bytes=LIMIT, dimension_semantics=("arbitrary",) * count
    )


def whole(shape):
    return pl.BlockSpec(shape, lambda *_: (0,) * len(shape), pipeline_mode=pl.Buffered(1))


def arrange_kernel(order, tokens, before, cot, x_out, cot_out):
    count = order.shape[0]
    width = tokens.shape[1] // count
    for j in range(count):
        spot = pl.ds(pl.multiple_of(order[j] * width, width), width)
        own = pl.ds(j * width, width)
        x_out[:HALO, own] = before[:, spot]
        x_out[HALO:, own] = tokens[:, spot]
        cot_out[:, own] = cot[:, spot]


def pick_blocks(values, places):
    count = places.shape[0]
    width = values.shape[1] // count
    return jnp.concatenate(
        [lax.dynamic_slice_in_dim(values, places[j] * width, width, 1) for j in range(count)], 1
    )


def narrow(order, width):
    return (width // order.shape[0]) % 128 != 0


def to_natural(values, order):
    if not narrow(order, values.shape[1]):
        return values
    return pick_blocks(values, jnp.argsort(order))


def arrange(order, tokens, before, cot):
    rows, width = tokens.shape
    if narrow(order, width):
        extended = jnp.concatenate([before, tokens], 0)
        return pick_blocks(extended, order), pick_blocks(cot, order)
    vmem = pl.BlockSpec(memory_space=pltpu.VMEM)
    return pl.pallas_call(
        arrange_kernel,
        out_shape=(
            jax.ShapeDtypeStruct((rows + HALO, width), BF),
            jax.ShapeDtypeStruct((rows, width), BF),
        ),
        in_specs=[pl.BlockSpec(memory_space=pltpu.SMEM), vmem, vmem, vmem],
        out_specs=(vmem, vmem),
        compiler_params=pltpu.CompilerParams(vmem_limit_bytes=LIMIT),
        name="arrange",
    )(order, tokens, before, cot)


def nt(left, right):
    return lax.dot_general(left, right, (((1,), (1,)), ((), ())), preferred_element_type=F32)


def nn(left, right):
    return jnp.dot(left, right, preferred_element_type=F32)


def ffn_kernel(first, final, *refs):
    tokens, pieces, rest = refs[:8], refs[8:16], refs[16:]
    h, ht, c, ct = tokens[:2], tokens[2:4], tokens[4:6], tokens[6:]
    branch, w, act, dgate, dup = rest[-5:]
    back, outs = rest[-6], rest[: -6] if first else rest[1:-6]
    grads, branch_own, branch_other = outs[:8], outs[8], outs[9]
    deep, half = pieces[0].shape[1:]
    spots = [
        (pl.ds(i % 4 * deep, deep), pl.ds(i // 4 * half, half)) for i in range(8)
    ]
    own = h[0].shape[0]
    tall = 384

    @pl.when(pl.program_id(0) == 0)
    def _():
        branch[...] = jnp.zeros_like(branch)
        back[...] = jnp.zeros_like(back) if first else rest[0][...]

    for piece, (deep_span, span) in zip(pieces, spots):
        w[:, deep_span, span] = piece[...]
    for start in range(0, 2 * own, tall):
        span, part = pl.ds(start, tall), pl.ds(start % own, tall)
        gate = nn(h[start // own][part, :], w[0])
        up = nn(h[start // own][part, :], w[1])
        da = nn(c[start // own][part, :], w[2])
        sigma = 1.0 / (1.0 + jnp.exp(-gate))
        silu = gate * sigma
        act[span, :] = (silu * up).astype(BF)
        dup[span, :] = (da * silu).astype(BF)
        dgate[span, :] = (da * up * (sigma + silu * (1.0 - sigma))).astype(BF)
    for k, (left, right) in enumerate(((ht, dgate), (ht, dup), (ct, act))):
        grad = (nn(left[0][...], right[:own, :]) + nn(left[1][...], right[own:, :])).astype(BF)
        for i, out in enumerate(grads):
            out[k] = grad[i % 4 * deep : (i % 4 + 1) * deep, i // 4 * half : (i // 4 + 1) * half]
    for start in range(0, 2 * own, tall):
        span = pl.ds(start, tall)
        branch[span, :] += nt(act[span, :], w[2])
        back[span, :] += nt(dgate[span, :], w[0]) + nt(dup[span, :], w[1])

    @pl.when(pl.program_id(0) == pl.num_programs(0) - 1)
    def _():
        branch_own[...] = branch[:own, :].astype(BF)
        branch_other[...] = branch[own:, :].astype(BF)
        if final:
            outs[10][...] = back[own:, :].astype(BF)


def ffn(tokens, pieces, sums, final):
    own, width = tokens[0].shape
    rows = 2 * own
    planes, deep, cols = pieces[0].shape
    tile = 128
    block = pl.BlockSpec((planes, deep, tile), lambda j: (0, 0, j))
    vmem = pl.BlockSpec(memory_space=pltpu.VMEM)
    grad = pltpu.HBM(pieces[0].shape, BF)
    part = jax.ShapeDtypeStruct((rows, width), F32)
    other = [pltpu.HBM((own, width), BF)] * (3 if final else 2)
    count = 8 + len(other)
    out = pl.pallas_call(
        functools.partial(ffn_kernel, not sums, final),
        grid=(cols // tile,),
        out_shape=(*[grad] * 8, *other, part),
        in_specs=[vmem] * 8 + [block] * 8 + [vmem] * len(sums),
        out_specs=(*[block] * 8, *[whole((own, width))] * len(other), vmem),
        input_output_aliases={16: count} if sums else {},
        scratch_shapes=[pltpu.VMEM((rows, width), F32), pltpu.VMEM((planes, width, 2 * tile), BF)]
        + [pltpu.VMEM((rows, 2 * tile), BF)] * 3,
        compiler_params=params(),
        cost_estimate=pl.CostEstimate(
            flops=36 * rows * width * cols,
            bytes_accessed=24 * width * cols,
            transcendentals=2 * rows * cols,
        ),
        name="ffn",
    )(*tokens, *pieces, *sums)
    return out[:8], out[8:10], out[10:-1], out[-1:]


def middle_kernel(order, middle, scale, gain, cot, *rest):
    block_out, grad, grad_low, gain_grad = rest[-4:]
    branches, backs = rest[: len(rest) - 6], rest[-6:-4]
    x2, r2, up = middle[...], scale[...], backs[0][...].astype(F32)
    for ref in backs[1:]:
        up = up + ref[...].astype(F32)
    total = x2
    for ref in branches:
        total = total + ref[...].astype(F32)
    store_natural(order, block_out, total.astype(BF))
    norm_back(x2, r2, gain, up, cot[...].astype(F32), grad, gain_grad)
    grad_low[...] = grad[...].astype(BF)


def store_natural(order, out, total):
    count = order.shape[0]
    if narrow(order, total.shape[1]):
        out[...] = total
        return
    width = total.shape[1] // count
    for j in range(count):
        spot = pl.ds(pl.multiple_of(order[j] * width, width), width)
        out[:, spot] = total[:, j * width : (j + 1) * width]


def norm_back(values, scale, gain, upstream, carried, out, gain_grad, order=None):
    scaled = upstream * gain[...]
    mean = jnp.mean(scaled * values, axis=-1, keepdims=True)
    total = carried + scale * scaled - values * (scale * scale * scale * mean)
    if order is None:
        out[...] = total
    else:
        store_natural(order, out, total)
    sums = jnp.sum(upstream * values * scale, axis=0, keepdims=True)

    @pl.when(pl.program_id(0) == 0)
    def _():
        gain_grad[...] = sums

    @pl.when(pl.program_id(0) > 0)
    def _():
        gain_grad[...] += sums


def row_specs(tile, width):
    return (
        pl.BlockSpec(memory_space=pltpu.SMEM),
        pl.BlockSpec((tile, width), lambda i: (i, 0)),
        pl.BlockSpec((tile, 1), lambda i: (i, 0)),
        pl.BlockSpec((1, width), lambda i: (0, 0)),
    )


def middle_back(order, middle, scale, gain, cot, branches, backs, deps):
    rows, width = middle.shape
    tile = 128
    smem, row, column, single = row_specs(tile, width)
    count = 5 + len(branches) + len(backs)

    def kernel(*refs):
        middle_kernel(*refs[:count], *refs[count + len(deps) :])

    return pl.pallas_call(
        kernel,
        grid=(rows // tile,),
        out_shape=(
            jax.ShapeDtypeStruct((rows, width), BF),
            jax.ShapeDtypeStruct((rows, width), F32),
            jax.ShapeDtypeStruct((rows, width), BF),
            jax.ShapeDtypeStruct((1, width), F32),
        ),
        in_specs=[smem, row, column, single, row] + [row] * (count - 5) + [ANY] * len(deps),
        out_specs=(row, row, row, single),
        compiler_params=params(),
        cost_estimate=pl.CostEstimate(
            flops=30 * rows * width, bytes_accessed=(4 + 2 * count) * rows * width, transcendentals=0
        ),
        name="middle_back",
    )(order, middle, scale, gain, cot, *branches, *backs, *deps)


def input_kernel(order, values, scale, gain, carried, upstream, out, gain_grad):
    norm_back(
        values[...].astype(F32), scale[...], gain, upstream[...], carried[...], out, gain_grad, order
    )


def input_back(order, values, scale, gain, carried, upstream):
    rows, width = values.shape
    tile = 128
    smem, row, column, single = row_specs(tile, width)
    return pl.pallas_call(
        input_kernel,
        grid=(rows // tile,),
        out_shape=(
            jax.ShapeDtypeStruct((rows, width), F32),
            jax.ShapeDtypeStruct((1, width), F32),
        ),
        in_specs=[smem, row, column, single, row, row],
        out_specs=(row, single),
        compiler_params=params(),
        cost_estimate=pl.CostEstimate(
            flops=20 * rows * width, bytes_accessed=14 * rows * width, transcendentals=0
        ),
        name="input_back",
    )(order, values, scale, gain, carried, upstream)


def mixer_grad_kernel(ht, dt, pa, pb, ya, yb, *rest):
    ga, gb = rest[-2:]
    step = pl.program_id(0)

    @pl.when(step < 3)
    def _():
        ga[0] = nn(ht[...], pa[0]).astype(BF)
        gb[0] = nn(ht[...], pb[0]).astype(BF)

    @pl.when(step == 3)
    def _():
        ga[0] = nn(dt[...], ya[...]).astype(BF)
        gb[0] = nn(dt[...], yb[...]).astype(BF)


def mixer_grad(ht, dt, proj_grad, gated, first, second, deps):
    width, rows = ht.shape
    cols = gated.shape[1] // 4

    def column(block):
        return pl.BlockSpec((1, rows, cols), lambda k: (jnp.minimum(k, 2), 0, block))

    def gated_column(block):
        return pl.BlockSpec((rows, cols), lambda k: (0, block))

    out = pl.BlockSpec((1, width, cols), lambda k: (k, 0, 0))
    grad = jax.ShapeDtypeStruct((4, width, cols), BF)
    return pl.pallas_call(
        mixer_grad_kernel,
        grid=(4,),
        out_shape=(grad, grad),
        in_specs=[
            whole((width, rows)),
            whole((width, rows)),
            column(first),
            column(second),
            gated_column(first),
            gated_column(second),
        ]
        + [ANY] * len(deps),
        out_specs=(out, out),
        compiler_params=params(),
        cost_estimate=pl.CostEstimate(
            flops=16 * rows * width * cols,
            bytes_accessed=4 * rows * width + 16 * width * cols + 16 * rows * cols,
            transcendentals=0,
        ),
        name="mixer_grad",
    )(ht, dt, proj_grad, proj_grad, gated, gated, *deps)


def update_kernel(*refs):
    count = (len(refs) - 12)
    totals, rest = refs[:count], refs[count:]
    wide, tall, wide_new, tall_new = rest[:3], rest[3:6], rest[6:9], rest[9:]
    for i, total in enumerate(totals):

        @pl.when(pl.program_id(0) == i)
        def _():
            last = total.shape[0] - 1
            new = adamw(wide[0][...], total[:last], wide[1][...], wide[2][...], RATE_MATRIX, DECAY)
            for ref, value in zip(wide_new, new):
                ref[...] = value
            grad = jnp.transpose(total[last])
            new = adamw(tall[0][...], grad, tall[1][...], tall[2][...], RATE_MATRIX, DECAY)
            for ref, value in zip(tall_new, new):
                ref[...] = value


def update(totals, wide, tall):
    if (wide[0].shape[2] // len(totals)) % 128:
        totals = [jnp.concatenate(totals, 2)]
    count = len(totals)
    planes, deep, cols = wide[0].shape
    part = cols // count
    wide_spec = pl.BlockSpec((planes, deep, part), lambda i: (0, 0, i))
    tall_spec = pl.BlockSpec((part, deep), lambda i: (i, 0))
    return pl.pallas_call(
        update_kernel,
        grid=(count,),
        out_shape=tuple(jax.ShapeDtypeStruct(a.shape, F32) for a in wide + tall),
        in_specs=[whole(total.shape) for total in totals] + [wide_spec] * 3 + [tall_spec] * 3,
        out_specs=(wide_spec,) * 3 + (tall_spec,) * 3,
        compiler_params=params(),
        cost_estimate=pl.CostEstimate(
            flops=20 * (planes + 1) * deep * cols,
            bytes_accessed=28 * (planes + 1) * deep * cols,
            transcendentals=(planes + 1) * deep * cols,
        ),
        name="update",
    )(*totals, *wide, *tall)


def local(
    tokens,
    segments,
    cotangent,
    mixer_in,
    mixer_out,
    gate_up,
    down_proj,
    norm_gains,
    conv_kernel,
    first_mixer_in,
    second_mixer_in,
    first_mixer_out,
    second_mixer_out,
    first_gate_up,
    second_gate_up,
    first_down_proj,
    second_down_proj,
    first_norm_gains,
    second_norm_gains,
    first_conv_kernel,
    second_conv_kernel,
):
    dp_size, t_size = lax.axis_size("dp"), lax.axis_size("tensor")
    dp_index, t_index = lax.axis_index("dp"), lax.axis_index("tensor")
    rows, length = tokens.shape[0], segments.shape[1]
    order = dp_index ^ jnp.array([rotate_left(j, dp_size) for j in range(dp_size)], jnp.int32)

    z_bits, t_bits = low_bits()
    wide, cut = 1, 2
    ffn_cols = gate_up.shape[2] // PARTS
    own = [join([mixer_in.astype(BF), mixer_out.T.astype(BF)[None]], 0)]
    for i in range(PARTS):
        cols = slice(i * ffn_cols, (i + 1) * ffn_cols)
        own.append(join([gate_up[:, :, cols].astype(BF), down_proj[cols].T.astype(BF)[None]], 0))

    def deepen(places, others, axis, bit, along):
        got = phase(others, [(own[i], axis, bit) for i in places])
        for i, part in zip(places, got):
            own[i] = join([own[i], part], along)
        return got

    def first_rows(places, others):
        for bit in z_bits[:-1]:
            others = deepen(places, others, "dp", bit, wide)
        for bit in t_bits:
            others = deepen(places, others, "tensor", bit, cut)
        return others

    def by_x(value):
        return (value, "dp", 1)

    def by_y(value):
        return (value, "tensor", 2)

    def by_z(value):
        return (value, "dp", z_bits[-1])

    def other_core(value):
        return swap(value, "tensor", 1)

    xa, xb, ya, yb, zb, da, db = ({} for _ in range(7))

    def pieces_of(i):
        return [own[i], zb[i], xa[i], xb[i], ya[i], yb[i], da[i], db[i]]

    small = jnp.concatenate([norm_gains, conv_kernel], 0)[:, None, None, None, None, :]
    small_z = phase([], [(small, "dp", code) for code in range(2, dp_size, 2)])
    before = lax.ppermute(
        tokens[rows - HALO :], "tensor", [(i, i + 1) for i in range(t_size - 1)]
    )
    last = first_rows([0, 1], small_z)
    small = join([small, *small_z], 1)
    small = join([small, swap(small, "dp", 1)], 2)
    small = join([small, *[swap(small, "tensor", code) for code in range(2, t_size, 2)]], 3)
    small = join([small, swap(small, "tensor", 1)], 4)
    last = [*last, small, before]
    xa[0], ya[0], zb[0] = got = phase(last, [by_x(own[0]), by_y(own[0]), by_z(own[0])])
    later = first_rows(range(2, PARTS + 1), last)
    xb[0], yb[0], da[0], ya[1], zb[1] = got = phase(
        [*got, *later], [by_x(zb[0]), by_y(zb[0]), by_x(ya[0]), by_y(own[1]), by_z(own[1])]
    )
    x_ext, cot = arrange(order, *ordered([tokens, before, cotangent], last))
    db[0], xa[1], cot_other = phase(got, [by_y(xb[0]), by_x(own[1]), (cot, "tensor", 1)])
    (db[0],) = ordered([db[0]], [xa[1], cot_other])
    small = small.reshape(small.shape[0], dp_size, t_size, small.shape[-1])
    for axis, index, size_axis in ((1, dp_index, dp_size), (2, t_index, t_size)):
        for i in range(size_axis.bit_length() - 1):
            shape = small.shape
            split = small.reshape(shape[:axis] + (size_axis >> (i + 1), 2, 1 << i) + shape[axis + 1 :])
            flipped = jnp.flip(split, axis + 1)
            small = jnp.where((index >> i) & 1 == 1, flipped, split).reshape(shape)
    small = small.reshape(small.shape[0], -1)
    block = small.shape[1] // dp_size
    gains = jnp.concatenate(
        [lax.dynamic_slice_in_dim(small[:2], order[j] * block, block, 1) for j in range(dp_size)], 1
    )
    channels = small.shape[1] // t_size
    codes = block_codes(t_size)
    kernel = jnp.concatenate(
        [
            lax.dynamic_slice_in_dim(small[2:], (t_index ^ code) * channels, channels, 1)
            for code in codes
        ],
        1,
    )

    masks = []
    for mask in lag_masks(segments.reshape(-1), length):
        padded = jnp.concatenate([mask, jnp.zeros((HALO, 1), F32)], 0)
        masks.append(lax.dynamic_slice_in_dim(padded, t_index * rows, rows + HALO, 0))

    extended = x_ext.astype(F32)
    scale_ext = rms_scale(extended)
    normed_ext = (extended * scale_ext * gains[0]).astype(BF)
    ct, ct_other = cot.T, cot_other.T
    (normed_ext,) = ordered([normed_ext], [ct, ct_other])
    values, scale_one, normed_one = extended[HALO:], scale_ext[HALO:], normed_ext[HALO:]
    near, far = join(pieces_of(0)[:4], wide), join(pieces_of(0)[4:], wide)
    wm = [near, other_core(near), far, other_core(far)]
    got = phase(
        [db[0], xa[1]],
        [by_x(zb[1]), by_y(zb[1]), by_x(ya[1]), by_y(own[2]), by_z(own[2])],
    )
    wm_all = jnp.concatenate(wm, 2)
    win_all, wout_all = wm_all[:3], wm_all[3]
    projected = mm("td,kdc->ktc", normed_ext, win_all)
    part_b, part_c, part_x = projected[0], projected[1][HALO:], projected[2]
    product_ext = part_b * part_x
    part_b, part_x = part_b[HALO:], part_x[HALO:]
    product = product_ext[HALO:]
    convolved = kernel[0] * product
    for shift in range(1, KW):
        convolved = convolved + kernel[shift] * masks[shift - 1][:rows] * shift_rows(
            product_ext, HALO - shift, rows
        )
    gated = (part_c * convolved).astype(BF)
    (gated,) = ordered([gated], got)
    middle = values + mm("tc,dc->td", gated, wout_all)
    scale_two = rms_scale(middle)
    normed_two = (middle * scale_two * gains[1]).astype(BF)

    normed_other = other_core(normed_two)
    tokens_both = (normed_two, normed_other, normed_two.T, normed_other.T)
    tokens_both += (cot, cot_other, ct, ct_other)
    sums, grads, back_other, branch_own, branch_other = [], {}, [], [], []
    xb[1], yb[1], da[1], ya[2], zb[2] = got = ordered(got, [normed_two])
    db[1], xa[2] = got = phase(got, [by_y(xb[1]), by_x(own[2])])

    def run(i):
        nonlocal sums, back_other
        grads[i], branches, back_other, sums = ffn(tokens_both, pieces_of(i), list(sums), i == PARTS)
        branch_own.append(branches[0])
        branch_other.append(branches[1])
        return grads[i]

    got = phase(got, [by_x(zb[2]), by_y(zb[2]), by_x(ya[2]), by_y(own[3]), by_z(own[3])])
    xb[2], yb[2], da[2], ya[3], zb[3] = got = ordered(got, run(1)[:1])
    db[2], xa[3] = got = phase(got, [by_y(xb[2]), by_x(own[3])])

    axa, axb, aya, ayb, ada, adb = ({} for _ in range(6))

    def sum_xb(i):
        return by_x(plus(grads[i][3], adb[i]))

    def sum_ya(i):
        return by_y(plus(grads[i][4], ada[i]))

    got = phase(got, [by_x(zb[3]), by_y(zb[3]), by_x(ya[3]), by_y(grads[1][5])])
    xb[3], yb[3], da[3], ayb[1] = got = ordered(got, run(2)[:1])
    db[3], ada[1] = got = phase(got, [by_y(xb[3]), by_x(grads[1][6])])
    one_t = normed_one.T
    (db[3],) = ordered([db[3]], [ada[1], one_t])
    early = plus(branch_other[0], branch_other[1])
    got = phase(
        got,
        [
            by_x(grads[1][2]),
            by_y(grads[1][7]),
            by_x(grads[2][6]),
            by_y(grads[2][7]),
            (early, "tensor", 1),
        ],
    )
    axa[1], adb[1], ada[2], adb[2], early = got = ordered(got, run(3)[:1])
    back_other, back = ordered([*back_other, *sums], got)
    back_in = other_core(back_other)
    branch_in = other_core(branch_other[2])
    deps = got
    got = phase(got, [sum_xb(1), sum_ya(1), by_x(grads[2][2]), by_y(grads[2][5])])
    block_out, middle_grad, mixed_grad, gain_two_grad = middle_back(
        order, middle, scale_two, gains[1:2], cot, [*branch_own, early, branch_in], [back, back_in], deps
    )

    gated_grad = mm("td,dc->tc", mixed_grad, wout_all)
    axb[1], aya[1], axa[2], ayb[2] = got = ordered(got, [gated_grad])
    (gated_grad,) = ordered([gated_grad], got)

    def sum_b(i):
        return by_z(functools.reduce(jnp.add, [v.astype(F32) for v in (grads[i][1], axb[i], ayb[i])]).astype(BF))

    got = phase(
        got, [sum_xb(2), sum_ya(2), by_x(grads[3][6]), by_y(grads[3][7]), sum_b(1)]
    )
    conv_grad = gated_grad * part_c
    after_rel = lax.ppermute(
        conv_grad[:8], "tensor", [(i + 1, i) for i in range(t_size - 1)]
    )
    after = jnp.concatenate(
        [
            lax.dynamic_slice_in_dim(
                after_rel,
                block_place(code ^ t_index ^ (t_index + 1), t_size) % t_size * channels,
                channels,
                1,
            )
            for code in codes
        ],
        1,
    )
    c_grad = gated_grad * convolved
    conv_ext = jnp.concatenate([conv_grad, after], 0)
    kernel_rows = [jnp.sum(conv_grad * product, axis=0)]
    product_grad = kernel[0] * conv_grad
    for shift in range(1, KW):
        masked = masks[shift - 1][: rows + 8] * conv_ext
        kernel_rows.append(
            jnp.sum(masked[:rows] * shift_rows(product_ext, HALO - shift, rows), axis=0)
        )
        product_grad = product_grad + kernel[shift] * shift_rows(masked, shift, rows)
    proj_grad = jnp.stack([product_grad * part_x, c_grad, product_grad * part_b], 0).astype(BF)
    zs = {}
    axb[2], aya[2], ada[3], adb[3], zs[1] = got = ordered(got, [proj_grad])
    mixed_t = mixed_grad.T
    m_near_core, m_far_core = mixer_grad(one_t, mixed_t, proj_grad, gated, 1, 3, [axb[2], aya[2], ada[3], adb[3]])
    m_in = [other_core(m_far_core), other_core(m_near_core)]
    got = phase(
        [*got, *m_in],
        [by_x(grads[3][2]), sum_xb(3), by_y(grads[3][5]), sum_ya(3), sum_b(2)],
    )
    m_near, m_far = mixer_grad(one_t, mixed_t, proj_grad, gated, 0, 2, m_in)
    axa[3], axb[3], ayb[3], aya[3], zs[2] = got = ordered(got, [m_far])
    deep = m_near.shape[wide] // 4
    grads[0] = [
        plus(
            lax.slice_in_dim(value, i * deep, (i + 1) * deep, axis=wide),
            lax.slice_in_dim(other, i * deep, (i + 1) * deep, axis=wide),
        )
        for value, other in ((m_near, m_in[1]), (m_far, m_in[0]))
        for i in range(4)
    ]

    terms, steps = {}, [("tensor", bit, cut) for bit in reversed(t_bits)]
    steps += [("dp", bit, wide) for bit in reversed(z_bits[:-1])]

    def sum_a(i):
        terms[i] = [grads[i][0], axa[i], aya[i], zs[i]]

    def fold_send(i, step):
        axis, bit, along = steps[step]
        return (fold(terms[i], along), axis, bit)

    def folded(i, step, got):
        along = steps[step][2]
        terms[i] = [halves(term, along)[0] for term in terms[i]] + [got]

    sum_a(1)
    got = phase(
        got, [by_x(grads[0][6]), by_x(grads[0][2]), by_y(grads[0][7]), by_y(grads[0][5]), sum_b(3)]
    )
    ada[0], axa[0], adb[0], ayb[0], zs[3] = last = got

    (late,) = ordered([proj_grad], grads[0][:1])
    normed_one_grad = mm("ktc,kdc->td", late, win_all)
    grad_input, gain_one_grad = input_back(
        order, x_ext[HALO:], scale_one, gains[:1], middle_grad, normed_one_grad
    )

    gain_rel = jnp.concatenate([gain_one_grad, gain_two_grad], 0)
    kernel_rel = jnp.stack(kernel_rows, 0)
    gain_sums = jnp.concatenate(
        [
            lax.dynamic_slice_in_dim(gain_rel, rotate_right(dp_index ^ q, dp_size) * block, block, 1)
            for q in range(dp_size)
        ],
        1,
    )
    kernel_sums = jnp.concatenate(
        [
            lax.dynamic_slice_in_dim(
                kernel_rel, block_place(t_index ^ q, t_size) * channels, channels, 1
            )
            for q in range(t_size)
        ],
        1,
    )
    total_small = jnp.concatenate([gain_sums, kernel_sums], 0)

    def small_step(value, others, axis, codes):
        return functools.reduce(jnp.add, [value, *phase(others, [(value, axis, code) for code in codes])])

    sum_a(2)
    sum_a(3)
    total_small = small_step(total_small, last, "tensor", range(1, t_size))
    got = phase([*last, gain_one_grad], [sum_xb(0), sum_ya(0), *[fold_send(i, 0) for i in range(1, PARTS + 1)]])
    axb[0], aya[0] = got[:2]
    for i in range(1, PARTS + 1):
        folded(i, 0, got[i + 1])
    total_small = small_step(total_small, got[:2], "dp", [1])
    (zs[0],) = phase(got[:2], [sum_b(0)])
    for step in range(1, len(steps)):
        got = phase(got, [fold_send(i, step) for i in range(1, PARTS + 1)])
        for i in range(1, PARTS + 1):
            folded(i, step, got[i - 1])
    sum_a(0)
    total_small = small_step(total_small, [zs[0]], "dp", range(2, dp_size, 2))
    for step in range(len(steps)):
        (got,) = phase([], [fold_send(0, step)])
        folded(0, step, got)
    own_width = norm_gains.shape[1]
    own_small = lax.dynamic_slice_in_dim(
        total_small, (dp_index * t_size + t_index) * own_width, own_width, 1
    )

    def total(i):
        return functools.reduce(jnp.add, [term.astype(F32) for term in terms[i]])

    ffn_new = update(
        [total(i) for i in range(1, PARTS + 1)],
        (gate_up, first_gate_up, second_gate_up),
        (down_proj, first_down_proj, second_down_proj),
    )
    mix_new = update(
        [total(0)], (mixer_in, first_mixer_in, second_mixer_in), (mixer_out, first_mixer_out, second_mixer_out)
    )
    gains_new = adamw(norm_gains, own_small[:2], first_norm_gains, second_norm_gains, RATE_SMALL, 0.0)
    kernel_new = adamw(conv_kernel, own_small[2:], first_conv_kernel, second_conv_kernel, RATE_SMALL, DECAY)
    block_out, grad_input = to_natural(block_out, order), to_natural(grad_input, order)
    return (block_out, grad_input, *mix_new, *ffn_new, *gains_new, *kernel_new)


def solution(mesh):
    rows = P(("dp", "tensor"), None)
    in_w, out_w, small = P(None, "dp", "tensor"), P("tensor", "dp"), P(None, ("dp", "tensor"))
    return jax.shard_map(
        local,
        mesh=mesh,
        in_specs=(
            (rows, P("dp", None), rows, in_w, out_w, in_w, out_w, small, small)
            + (in_w,) * 2
            + (out_w,) * 2
            + (in_w,) * 2
            + (out_w,) * 2
            + (small,) * 4
        ),
        out_specs=(rows, rows)
        + (in_w,) * 3
        + (out_w,) * 3
        + (in_w,) * 3
        + (out_w,) * 3
        + (small,) * 6,
        check_vma=False,
    )
```
